512 devices in a mesh: req: 64 (over z, y_hi, core), tp: 8 (over y_lo, x).
Axes of the slice: x: 4, y: 8 (y_hi: 4, y_lo: 2; y = y_hi * 2 + y_lo), z: 8, core: 2. Of those that a mesh axis runs over, the one named last changes fastest.
Arguments:
- stale_cache: bfloat16 [64, 128, 2048], P('req', None, 'tp'), may hold values from -6 to 6
- fresh_input: bfloat16 [64, 16, 8192], P('tp', None, 'req'), may hold values from -6 to 6
- kv_weight: bfloat16 [8192, 2048], P('req'), may hold values from -0.0625 to 0.0625
- sel_index: int32 [64, 16], replicated, may hold values from 0 to 127, as said below
- owner: int32 [64], replicated, may hold values from 0 to 63, each once
- retrieval: int32 [512, 4], P('req'), may hold values from 0 to 63
- queries: bfloat16 [512, 32, 8192], P('req', None, 'tp'), may hold values from -90 to 90
- question_kv: bfloat16 [512, 32, 2048], P('req', None, 'tp'), may hold values from -6 to 6
Outputs:
- attended: bfloat16 [512, 32, 8192], P('req', None, 'tp')
The draws below stay inside these ranges and needn't reach their ends.
Inputs may be any that keep to these rules, and one draw needn't show every extreme that they name: `sel_index`: the positions of one passage are distinct.
All inputs are finite; a program needn't handle non-finite values.
Results may differ from the reference program's by a relative error of at most 0.0056.
Values may be sent and summed in bfloat16 or wider, within the bound.
A program may use at most 64 MiB of HBM per device.

```python
import math
import jax
import jax.numpy as jnp
import numpy as np
from jax import lax

D = 8192
QH = 64
KVH = 8
HD = 128
PLEN = 128
QLEN = 32
K_RET = 4
SEL = 16
PASSAGES = 64
REQS = 512


def shared_keys(key):
    return jnp.clip(jax.random.normal(key, (REQS, QLEN, KVH * 2 * HD), jnp.float32), -6.0, 6.0)


def draw_question_kv(key, part):
    base = shared_keys(key)
    return base.astype(jnp.bfloat16)


def draw_queries(key, part):
    key = jax.random.fold_in(key, 5)
    values = jnp.clip(jax.random.normal(key, (REQS, QLEN, QH * HD), jnp.float32), -6.0, 6.0)
    return values.astype(jnp.bfloat16)


def draw_sel_index(key, part):
    key = jax.random.fold_in(key, 3)
    keys = jax.random.split(key, PASSAGES)
    rows = jax.vmap(lambda k: jax.random.permutation(k, PLEN)[:SEL])(keys)
    return rows.astype(jnp.int32)


def touch_ends(values, key, smallest, high):
    spot = [jax.random.randint(jax.random.fold_in(key, axis), (), 0, length) for axis, length in enumerate(values.shape)]
    main_axis = values.shape.index(max(values.shape))
    next_to = spot[:main_axis] + [(spot[main_axis] + 1) % values.shape[main_axis]] + spot[main_axis + 1:]
    return values.at[tuple(spot)].set(smallest).at[tuple(next_to)].set(high)


def block_scale(rng, extent, cuts, least, largest):
    factor_of, own = 1.0, jax.random.fold_in(rng, 6)
    for position, blocks in cuts:
        steps = jnp.exp(jax.random.uniform(jax.random.fold_in(own, position), (blocks,), jnp.float32, least / len(cuts), largest / len(cuts)))
        factor_of = factor_of * jnp.repeat(steps, extent[position] // blocks).reshape([-1 if axis == position else 1 for axis in range(len(extent))])
    return factor_of


def rank_bounds(number_of, skew):
    weights = [(1 << 20) // math.isqrt(rank ** skew) + 1 for rank in range(1, number_of + 1)]
    spread = 1 + sum(weights) // (1 << 30)
    return np.cumsum(np.array([max(1, weight // spread) for weight in weights]))


def ranked(stream_key, extent, number_of, skew):
    grid = rank_bounds(number_of, skew)
    lot = jax.random.randint(jax.random.fold_in(stream_key, 1), extent, 0, int(grid[number_of - 1]))
    standing = jnp.searchsorted(jnp.asarray(grid, jnp.int32), lot, side="right")
    return jax.random.permutation(jax.random.fold_in(stream_key, 2), number_of)[standing].astype(jnp.int32)


def scatter_about(key, dims, deviation, reach, cuts=(), kind=jnp.bfloat16):
    result = jax.random.normal(key, dims, jnp.float32) * deviation
    if len(cuts) > 0:
        result = block_scale(key, dims, cuts, -0.22, 0.18) * result
    return jnp.clip(result, min=-reach, max=reach).astype(kind)


def setup_inputs(seed: int = 0) -> dict:
    key_list = jax.random.split(jax.random.key(seed), 9)
    return {
        "stale_cache": scatter_about(key_list[0], (PASSAGES, PLEN, KVH * 2 * HD), 1.0, 6.0, ((0, 64), (2, 8))),
        "fresh_input": scatter_about(key_list[1], (PASSAGES, SEL, D), 1.0, 6.0, ((0, 8), (2, 64))),
        "kv_weight": scatter_about(key_list[2], (D, KVH * 2 * HD), D ** -0.5, 0.0625, ((0, 64),)),
        "sel_index": draw_sel_index(jax.random.fold_in(key_list[8], 71), 0),
        "owner": jax.random.permutation(key_list[4], PASSAGES).astype(jnp.int32),
        "retrieval": touch_ends(ranked(key_list[5], (REQS, K_RET), PASSAGES, 2), jax.random.fold_in(key_list[5], 3), 0, PASSAGES - 1).astype(jnp.int32),
        "queries": draw_queries(jax.random.fold_in(key_list[8], 71), 0),
        "question_kv": draw_question_kv(jax.random.fold_in(key_list[8], 71), 0),
    }


theta_base = 500000.0

def rope(x, pos):
    half = x.shape[-1] // 2
    freqs = theta_base ** (-(jnp.arange(half, dtype=jnp.float32) * 2.0 / x.shape[-1]))
    angle = pos[..., None] * freqs
    cosine = jnp.cos(angle)
    sine = jnp.sin(angle)
    first = x[..., :half]
    second = x[..., half:]
    return jnp.concatenate([first * cosine - second * sine, second * cosine + first * sine], -1)

def blend_all(stale, fresh, sel_rows):
    count, picked, width = fresh.shape
    heads = width // (2 * HD)
    parts = fresh.astype(jnp.float32).reshape(count, picked, heads, 2, HD)
    turned = rope(parts[:, :, :, 0], sel_rows.astype(jnp.float32)[:, :, None])
    fresh_rot = jnp.stack([turned, parts[:, :, :, 1]], 3).reshape(count, picked, width).astype(jnp.bfloat16)
    onehot = sel_rows[:, :, None] == jnp.arange(stale.shape[1], dtype=jnp.int32)[None, None, :]
    placed = jnp.einsum('psl,psc->plc', onehot.astype(jnp.float32), fresh_rot.astype(jnp.float32))
    hit = jnp.any(onehot, axis=1)[:, :, None]
    return jnp.where(hit, placed.astype(jnp.bfloat16), stale)

def attend_one(query, own_kv, rows_kv):
    slots, plen, width = rows_kv.shape
    heads = width // (2 * HD)
    qlen = query.shape[0]
    qheads = query.shape[1] // HD
    parts = rows_kv.reshape(slots * plen, heads, 2, HD)
    pos = (jnp.arange(slots * plen, dtype=jnp.int32) // plen * plen).astype(jnp.float32)
    keys = rope(parts[:, :, 0].astype(jnp.float32), pos[:, None]).astype(jnp.bfloat16)
    own = own_kv.reshape(qlen, heads, 2, HD)
    keys = jnp.concatenate([keys, own[:, :, 0]], 0)
    values = jnp.concatenate([parts[:, :, 1], own[:, :, 1]], 0)
    grouped = query.reshape(qlen, heads, qheads // heads, HD)
    scores = jnp.einsum('qhgd,khd->hgqk', grouped.astype(jnp.float32), keys.astype(jnp.float32)) / jnp.sqrt(jnp.float32(HD))
    total = slots * plen + qlen
    kpos = jnp.arange(total, dtype=jnp.int32)
    qpos = jnp.arange(qlen, dtype=jnp.int32)
    allowed = (kpos[None, :] < slots * plen) | (kpos[None, :] - slots * plen <= qpos[:, None])
    scores = jnp.where(allowed, scores, jnp.float32(-1e+30))
    top = lax.optimization_barrier(jnp.max(scores, -1, keepdims=True))
    expo = jnp.exp(scores - top)
    weights = (expo / lax.optimization_barrier(jnp.sum(expo, -1, keepdims=True))).astype(jnp.bfloat16)
    out = jnp.einsum('hgqk,khd->qhgd', weights.astype(jnp.float32), values.astype(jnp.float32))
    return out.astype(jnp.bfloat16).reshape(qlen, qheads * HD)

def reference(stale_cache, fresh_input, kv_weight, sel_index, owner, retrieval, queries, question_kv):
    count, picked, width = fresh_input.shape
    fresh = jnp.dot(fresh_input.reshape(count * picked, width), kv_weight, preferred_element_type=jnp.float32)
    fresh = fresh.astype(jnp.bfloat16).reshape(count, picked, kv_weight.shape[1])
    blended = blend_all(stale_cache, fresh, sel_index)

    def one_request(items):
        query, own_kv, chosen = items
        rows = jnp.take(blended, jnp.take(owner, chosen), axis=0)
        return attend_one(query, own_kv, rows)
    return lax.map(one_request, (queries, question_kv, retrieval))
```

```python
import functools
import math

import jax
import jax.numpy as jnp
import numpy as np
from jax import lax
from jax.experimental import pallas as pl
from jax.experimental.pallas import tpu as pltpu
from jax.sharding import PartitionSpec as P

MESH = pl.DeviceIdType.MESH
HD = 128
NZ, NY, NX = 8, 4, 4
PLEN, QLEN, SEL, SLOTS = 128, 32, 16, 4
GROUP = 8
KV = 2 * HD
LAST = SLOTS * PLEN
KEYS = LAST + 128
CHUNK = 64
SCALE = math.log2(math.e) / math.sqrt(HD)
NEG = -1e30
THETA = 500000.0


def trig_tables():
    positions = np.concatenate([np.arange(PLEN), np.arange(8) * PLEN]).astype(np.float32)
    freqs = (THETA ** (-(np.arange(HD // 2, dtype=np.float64) * 2.0 / HD))).astype(np.float32)
    angle = (positions[:, None] * freqs).astype(np.float32).astype(np.float64)
    cosine, sine = np.cos(angle), np.sin(angle)
    return (
        np.concatenate([cosine, cosine], -1).astype(np.float32),
        np.concatenate([-sine, sine], -1).astype(np.float32),
    )


def kernel(
    stale_hbm, x_hbm, w_hbm, sel_hbm, owner_hbm, chosen_hbm, cos_hbm, sin_hbm, q_hbm, own_hbm,
    out_hbm,
    stale_buf, fresh_buf, xbuf, wbuf, zsum, zrecv, bias, trig_c, trig_s,
    kbuf0, vbuf0, kbuf1, vbuf1, sbuf0, pbuf0, sbuf1, pbuf1, tail,
    x_ref, selv_ref, cos_ref, sin_ref, q_ref, own_ref, out_ref, sel_ref, owner_ref, chosen_ref,
    local_sem, out_sem, xy_send, xy_recv, xx_send, xx_recv, w_send, w_recv, wsib,
    sy_send, sy_recv, sz_send, sz_recv, ss_send, ss_recv,
    rz_send, rz_recv, fz_send, fz_recv, fy_send, fy_recv, fs_send, fs_recv,
):
    r, t = lax.axis_index("req"), lax.axis_index("tp")
    z, y, c = r // 8, lax.rem(r, 8) // 2, lax.rem(r, 2)
    ylo, x = t // 4, lax.rem(t, 4)

    def dev(zz, yy, cc, tt):
        return (zz * 8 + yy * 2 + cc, tt)

    def at_z(k):
        return lax.rem(z + k + 2 * NZ, NZ)

    def at_y(k):
        return lax.rem(y + k + 2 * NY, NY)

    sibling = dev(z, y, 1 - c, t)

    def remote(src, dst, send_sem, recv_sem, device):
        return pltpu.make_async_remote_copy(
            src_ref=src, dst_ref=dst, send_sem=send_sem, recv_sem=recv_sem,
            device_id=device, device_id_type=MESH,
        )

    pending = []

    def send(*args):
        copy = remote(*args)
        copy.start()
        pending.append(copy)

    def arrived(dst, recv_sem, send_sem):
        remote(dst, dst, send_sem, recv_sem, sibling).wait_recv()

    plane = [(dy, dl, dc) for dy in range(NY) for dl in range(2) for dc in range(2)][1:]

    def plane_dev(k):
        dy, dl, dc = plane[k]
        yy, ll, cc = at_y(dy), lax.rem(ylo + dl, 2), lax.rem(c + dc, 2)
        return yy, ll, cc

    barrier = pltpu.get_barrier_semaphore()
    peers = []
    for k in range(len(plane)):
        yy, ll, cc = plane_dev(k)
        peers.append(dev(z, yy, cc, ll * 4 + x))
    for k in range(1, NX):
        peers.append((r, ylo * 4 + lax.rem(x + k, NX)))
    for k in range(1, NZ):
        peers.append(dev(at_z(k), y, c, t))
    for peer in peers:
        pl.semaphore_signal(barrier, inc=1, device_id=peer, device_id_type=MESH)

    columns = pl.ds(pl.multiple_of(t * KV, KV), KV)

    def slot(zz, yy):
        return stale_buf.at[zz * 8 + c * 4 + yy]

    def row(zz, cc):
        return stale_buf.at[pl.ds(zz * 8 + cc * 4, 4)]

    def xpiece(ts, ys, cs):
        return xbuf.at[ts, :, pl.ds(pl.multiple_of((cs * 4 + ys) * HD, HD), HD)]

    loads = []
    for source, target in (
        (x_hbm, x_ref), (w_hbm.at[:, columns], wbuf.at[c * 4 + y]), (stale_hbm.at[0], slot(z, y)),
        (sel_hbm, sel_ref), (sel_hbm, selv_ref), (cos_hbm, cos_ref), (sin_hbm, sin_ref),
        (owner_hbm, owner_ref), (chosen_hbm, chosen_ref), (q_hbm, q_ref), (own_hbm, own_ref),
    ):
        loads.append(pltpu.make_async_copy(source, target, local_sem.at[len(loads)]))
        loads[-1].start()
    load_x, load_w, load_stale = loads[:3]
    load_x.wait()
    own_x = pltpu.make_async_copy(x_ref.at[y, c], xpiece(t, y, c), local_sem.at[len(loads)])
    own_x.start()

    pl.semaphore_wait(barrier, len(peers))

    for k in range(len(plane)):
        yy, ll, cc = plane_dev(k)
        send(x_ref.at[yy, cc], xpiece(t, y, c), xy_send.at[k], xy_recv.at[k], dev(z, yy, cc, ll * 4 + x))
    load_w.wait()
    for e in range(1, NY):
        send(wbuf.at[c * 4 + y], wbuf.at[c * 4 + y], w_send.at[e], w_recv.at[e], dev(z, at_y(e), c, t))

    def ring(src, zz, yy, s, d, way):
        step = 1 if way == 0 else -1
        send(src, slot(zz, yy), sz_send.at[way, s, d], sz_recv.at[way, s, d], dev(at_z(step), y, c, t))

    load_stale.wait()
    ring(slot(z, y), z, y, 1, 0, 0)
    ring(slot(z, y), z, y, 1, 0, 1)
    for e in (1, 3, 2):
        send(slot(z, y), slot(z, y), sy_send.at[e], sy_recv.at[e], dev(z, at_y(e), c, t))

    def hop(s, d):
        for way in range(2):
            if s == 4 and (d < 2) != (way == 0):
                continue
            zz, yy = at_z(-s if way == 0 else s), at_y(d)
            arrived(slot(zz, yy), sz_recv.at[way, s, d], sz_send.at[way, s, d])
            if s < 3 or (s == 3 and (d < 2) == (way == 0)):
                ring(slot(zz, yy), zz, yy, s + 1, d, way)

    def share(zz, k):
        send(row(zz, c), row(zz, c), ss_send.at[k], ss_recv.at[k], sibling)

    for load in loads[3:]:
        load.wait()
    place = lax.broadcasted_iota(jnp.int32, (PLEN, 64), 0)
    hit = place == selv_ref[0:1, :]
    for k in range(1, SEL):
        hit = hit | (place == selv_ref[k : k + 1, :])
    bias[...] = jnp.transpose(jnp.where(hit, jnp.float32(NEG), jnp.float32(0.0)))
    for k in range(SEL):
        position = sel_ref[k, r]
        trig_c[pl.ds(k, 1), :] = cos_ref[pl.ds(position, 1), :]
        trig_s[pl.ds(k, 1), :] = sin_ref[pl.ds(position, 1), :]
    col = lax.broadcasted_iota(jnp.int32, (CHUNK, 128), 1)
    token = lax.rem(lax.broadcasted_iota(jnp.int32, (CHUNK, 128), 0), QLEN)
    seen = (col < 64) | ((col < 96) & (col - 64 <= token))
    tail[...] = jnp.where(seen, jnp.float32(0.0), jnp.float32(NEG))
    for buf in (kbuf0, vbuf0, kbuf1, vbuf1):
        buf[LAST + 96 :, :] = jnp.zeros((32, HD), jnp.bfloat16)

    own_x.wait()
    for k in range(len(plane)):
        dy, dl, dc = plane[k]
        ys, ls, cs = at_y(-dy), lax.rem(ylo + dl, 2), lax.rem(c + dc, 2)
        arrived(xpiece(ls * 4 + x, ys, cs), xy_recv.at[k], xy_send.at[k])
    xall = xbuf.reshape(2, 4, SEL, 8 * HD)
    for k in range(1, NX):
        send(xall.at[:, x], xall.at[:, x], xx_send.at[k], xx_recv.at[k], (r, ylo * 4 + lax.rem(x + k, NX)))
    hop(1, 0)
    for e in range(1, NY):
        arrived(wbuf.at[c * 4 + at_y(-e)], w_recv.at[e], w_send.at[e])
    mine_w = wbuf.at[pl.ds(c * 4, 4)]
    send(mine_w, mine_w, wsib.at[0], wsib.at[1], sibling)
    for e in (3, 1, 2):
        d = (NY - e) % NY
        arrived(slot(z, at_y(d)), sy_recv.at[e], sy_send.at[e])
        ring(slot(z, at_y(d)), z, at_y(d), 1, d, 0)
        ring(slot(z, at_y(d)), z, at_y(d), 1, d, 1)
    share(z, 0)
    hop(2, 0)
    for k in range(1, NX):
        xs = lax.rem(x + NX - k, NX)
        arrived(xall.at[:, xs], xx_recv.at[k], xx_send.at[k])
    arrived(wbuf.at[pl.ds((1 - c) * 4, 4)], wsib.at[1], wsib.at[0])
    part = jnp.dot(
        xbuf[...].reshape(NZ * SEL, 8 * HD),
        wbuf[...].reshape(8 * HD, KV),
        preferred_element_type=jnp.float32,
    )
    zsum[...] = part.reshape(NZ, SEL, KV)
    for k in range(1, NZ):
        send(zsum.at[at_z(k)], zrecv.at[k], rz_send.at[k], rz_recv.at[k], dev(at_z(k), y, c, t))
    for d in (1, 3, 2):
        hop(1, d)
    share(at_z(-1), 1)
    share(at_z(1), 2)

    total = zsum[z]
    for k in range(1, NZ):
        arrived(zrecv.at[k], rz_recv.at[k], rz_send.at[k])
        total = total + zrecv[k]
    fresh = total.astype(jnp.bfloat16).astype(jnp.float32)
    keys = fresh[:, :HD]
    keys = keys * trig_c[...] + pltpu.roll(keys, HD // 2, 1) * trig_s[...]

    def fslot(yy, zz):
        return fresh_buf.at[c * 4 + yy, zz]

    fresh_buf[c * 4 + y, z, :, :HD] = keys.astype(jnp.bfloat16)
    fresh_buf[c * 4 + y, z, :, HD:] = fresh[:, HD:].astype(jnp.bfloat16)
    for k in range(1, NZ):
        send(fslot(y, z), fslot(y, z), fz_send.at[k], fz_recv.at[k], dev(at_z(k), y, c, t))

    hop(3, 0)
    for d in (1, 3, 2):
        hop(2, d)
    share(at_z(-2), 3)
    share(at_z(2), 4)

    for k in range(1, NZ):
        arrived(fslot(y, at_z(-k)), fz_recv.at[k], fz_send.at[k])

    def fcol(yy, cc):
        return fresh_buf.at[cc * 4 + yy]

    for e in (1, 3, 2):
        send(fcol(y, c), fcol(y, c), fy_send.at[e], fy_recv.at[e], dev(z, at_y(e), c, t))
    send(fcol(y, c), fcol(y, c), fs_send.at[0], fs_recv.at[0], sibling)

    for d in (1, 3, 2):
        hop(3, d)
    share(at_z(-3), 5)
    share(at_z(3), 6)
    for e in (3, 1, 2):
        yy = at_y(-e)
        arrived(fcol(yy, c), fy_recv.at[e], fy_send.at[e])
        send(fcol(yy, c), fcol(yy, c), fs_send.at[e], fs_recv.at[e], sibling)
    for d in (0, 1, 3, 2):
        hop(4, d)
    share(at_z(4), 7)

    for e in range(NY):
        arrived(fcol(at_y(-e), 1 - c), fs_recv.at[e], fs_send.at[e])
    for k, far in enumerate((0, -1, 1, -2, 2, -3, 3, 4)):
        arrived(row(at_z(far), 1 - c), ss_recv.at[k], ss_send.at[k])
    for copy in pending:
        copy.wait_send()

    def turn(block, j):
        wide = block.astype(jnp.float32)
        wide = wide * cos_ref[pl.ds(PLEN + j, 1), :] + pltpu.roll(wide, HD // 2, 1) * sin_ref[pl.ds(PLEN + j, 1), :]
        return wide.astype(jnp.bfloat16)

    def assemble(i, kbuf, vbuf):
        biases = []
        for j in range(SLOTS):
            o = owner_ref[chosen_ref[j, i]]
            oz, oy, oc = o // 8, lax.rem(o, 8) // 2, lax.rem(o, 2)
            old = stale_buf[oz * 8 + oc * 4 + oy]
            new = fresh_buf[oc * 4 + oy, oz]
            biases.append(bias[pl.ds(o, 1), :])
            old_key, new_key = old[:, :HD], new[:, :HD]
            if j:
                old_key, new_key = turn(old_key, j), turn(new_key, j)
            kbuf[j * PLEN : (j + 1) * PLEN, :] = old_key
            vbuf[j * PLEN : (j + 1) * PLEN, :] = old[:, HD:]
            kbuf[LAST + j * SEL : LAST + (j + 1) * SEL, :] = new_key
            vbuf[LAST + j * SEL : LAST + (j + 1) * SEL, :] = new[:, HD:]
        own = own_ref[i]
        kbuf[LAST + 64 : LAST + 96, :] = own[:, :HD]
        vbuf[LAST + 64 : LAST + 96, :] = own[:, HD:]
        return jnp.concatenate(biases, 1)

    def score(i, kbuf, sbuf):
        query = q_ref[i]
        query = jnp.concatenate([query[:, h * HD : (h + 1) * HD] for h in range(GROUP)], 0)
        sbuf[...] = lax.dot_general(
            query, kbuf[...], (((1,), (1,)), ((), ())), preferred_element_type=jnp.float32
        )

    def soften(masked, sbuf, pbuf):
        for first in range(0, GROUP * QLEN, CHUNK):
            part_rows = slice(first, first + CHUNK)
            raw = jnp.concatenate([sbuf[part_rows, :LAST] + masked, sbuf[part_rows, LAST:] + tail[...]], 1)
            expo = jnp.exp2((raw - jnp.max(raw, 1, keepdims=True)) * SCALE)
            pbuf[part_rows, :] = (expo * (1.0 / jnp.sum(expo, 1, keepdims=True))).astype(jnp.bfloat16)

    def weigh(i, vbuf, pbuf):
        result = jnp.dot(pbuf[...], vbuf[...], preferred_element_type=jnp.float32).astype(jnp.bfloat16)
        for h in range(GROUP):
            out_ref[i, :, h * HD : (h + 1) * HD] = result[h * QLEN : (h + 1) * QLEN]

    def store(i):
        return pltpu.make_async_copy(out_ref.at[i], out_hbm.at[i], out_sem.at[i])

    def pair(p, carry):
        i0, i1 = 2 * p, 2 * p + 1
        masked0 = assemble(i0, kbuf0, vbuf0)
        masked1 = assemble(i1, kbuf1, vbuf1)
        score(i0, kbuf0, sbuf0)
        score(i1, kbuf1, sbuf1)
        soften(masked0, sbuf0, pbuf0)
        weigh(i0, vbuf0, pbuf0)
        soften(masked1, sbuf1, pbuf1)
        weigh(i1, vbuf1, pbuf1)
        store(i0).start()
        store(i1).start()
        return carry

    lax.fori_loop(0, 4, pair, 0)
    for i in range(8):
        store(i).wait()


def local(stale, fresh_input, kv_weight, sel_index, owner, retrieval, queries, question_kv):
    cosine, sine = trig_tables()
    any_spec = pl.BlockSpec(memory_space=pl.ANY)
    dma = pltpu.SemaphoreType.DMA
    return pl.pallas_call(
        kernel,
        out_shape=jax.ShapeDtypeStruct(queries.shape, jnp.bfloat16),
        in_specs=[any_spec] * 10,
        out_specs=any_spec,
        scratch_shapes=[
            pltpu.VMEM((64, PLEN, KV), jnp.bfloat16),
            pltpu.VMEM((8, NZ, SEL, KV), jnp.bfloat16),
            pltpu.VMEM((8, SEL, 8 * HD), jnp.bfloat16),
            pltpu.VMEM((8, HD, KV), jnp.bfloat16),
            pltpu.VMEM((NZ, SEL, KV), jnp.float32),
            pltpu.VMEM((NZ, SEL, KV), jnp.float32),
            pltpu.VMEM((64, PLEN), jnp.float32),
            pltpu.VMEM((SEL, HD), jnp.float32),
            pltpu.VMEM((SEL, HD), jnp.float32),
            pltpu.VMEM((KEYS, HD), jnp.bfloat16),
            pltpu.VMEM((KEYS, HD), jnp.bfloat16),
            pltpu.VMEM((KEYS, HD), jnp.bfloat16),
            pltpu.VMEM((KEYS, HD), jnp.bfloat16),
            pltpu.VMEM((GROUP * QLEN, KEYS), jnp.float32),
            pltpu.VMEM((GROUP * QLEN, KEYS), jnp.bfloat16),
            pltpu.VMEM((GROUP * QLEN, KEYS), jnp.float32),
            pltpu.VMEM((GROUP * QLEN, KEYS), jnp.bfloat16),
            pltpu.VMEM((CHUNK, 128), jnp.float32),
            pltpu.VMEM((NY, 2, SEL, HD), jnp.bfloat16),
            pltpu.VMEM((SEL, 64), jnp.int32),
            pltpu.VMEM(cosine.shape, jnp.float32),
            pltpu.VMEM(sine.shape, jnp.float32),
            pltpu.VMEM(queries.shape, jnp.bfloat16),
            pltpu.VMEM(question_kv.shape, jnp.bfloat16),
            pltpu.VMEM(queries.shape, jnp.bfloat16),
            pltpu.SMEM((SEL, 64), jnp.int32),
            pltpu.SMEM((64,), jnp.int32),
            pltpu.SMEM((SLOTS, 8), jnp.int32),
            dma((12,)),
            dma((8,)),
            dma((15,)), dma((15,)),
            dma((NX,)), dma((NX,)),
            dma((NY,)), dma((NY,)),
            dma((2,)),
            dma((NY,)), dma((NY,)),
            dma((2, 5, NY)), dma((2, 5, NY)),
            dma((8,)), dma((8,)),
            dma((NZ,)), dma((NZ,)),
            dma((NZ,)), dma((NZ,)),
            dma((NY,)), dma((NY,)),
            dma((NY,)), dma((NY,)),
        ],
        compiler_params=pltpu.CompilerParams(
            collective_id=0, has_side_effects=True, vmem_limit_bytes=62 * 1024 * 1024
        ),
    )(
        stale,
        fresh_input.reshape(NY, 2, SEL, HD),
        kv_weight,
        sel_index.T,
        owner,
        retrieval.T,
        jnp.asarray(cosine),
        jnp.asarray(sine),
        queries,
        question_kv,
    )


def solution(mesh):
    return jax.shard_map(
        local,
        mesh=mesh,
        in_specs=(
            P("req", None, "tp"),
            P("tp", None, "req"),
            P("req", None),
            P(),
            P(),
            P("req", None),
            P("req", None, "tp"),
            P("req", None, "tp"),
        ),
        out_specs=P("req", None, "tp"),
        check_vma=False,
    )
```

```python
import functools
import math

import jax
import jax.numpy as jnp
import numpy as np
from jax import lax
from jax.experimental import pallas as pl
from jax.experimental.pallas import tpu as pltpu
from jax.sharding import PartitionSpec as P

MESH = pl.DeviceIdType.MESH
HD = 128
NZ, NY, NX = 8, 4, 4
PLEN, QLEN, SEL, SLOTS = 128, 32, 16, 4
GROUP = 8
KV = 2 * HD
LAST = SLOTS * PLEN
KEYS = LAST + 128
KEPT = PLEN - SEL
CHUNK = 64
SCALE = math.log2(math.e) / math.sqrt(HD)
NEG = -1e30
THETA = 500000.0


def trig_tables():
    positions = np.concatenate([np.arange(PLEN), np.arange(8) * PLEN]).astype(np.float32)
    freqs = (THETA ** (-(np.arange(HD // 2, dtype=np.float64) * 2.0 / HD))).astype(np.float32)
    angle = (positions[:, None] * freqs).astype(np.float32).astype(np.float64)
    cosine, sine = np.cos(angle), np.sin(angle)
    return (
        np.concatenate([cosine, cosine], -1).astype(np.float32),
        np.concatenate([-sine, sine], -1).astype(np.float32),
    )


def gather_kernel(
    stale_hbm, x_hbm, w_hbm, sel_hbm, cos_hbm, sin_hbm,
    pas,
    stale_ref, own_rows, own_fresh, xbuf, wbuf, zsum, zrecv, trig_c, trig_s, x_ref, w_ref, cos_ref, sin_ref, sel_ref,
    local_sem, xy_send, xy_recv, xx_send, xx_recv, w_send, w_recv, wr_send, wr_recv,
    seed_send, seed_recv, yr_send, yr_recv, sz_send, sz_recv, ss_send, ss_recv,
    rz_send, rz_recv, fz_send, fz_recv, fy_send, fy_recv, fr_send, fr_recv, fs_send, fs_recv,
):
    r, t = lax.axis_index("req"), lax.axis_index("tp")
    z, y, c = r // 8, lax.rem(r, 8) // 2, lax.rem(r, 2)
    ylo, x = t // 4, lax.rem(t, 4)

    def dev(zz, yy, cc, tt):
        return (zz * 8 + yy * 2 + cc, tt)

    def at_z(k):
        return lax.rem(z + k + 2 * NZ, NZ)

    def at_y(k):
        return lax.rem(y + k + 2 * NY, NY)

    def at_x(k):
        return lax.rem(x + k + 2 * NX, NX)

    def other(dl):
        return lax.rem(ylo + dl, 2)

    def remote(src, dst, send_sem, recv_sem, device):
        return pltpu.make_async_remote_copy(
            src_ref=src, dst_ref=dst, send_sem=send_sem, recv_sem=recv_sem,
            device_id=device, device_id_type=MESH,
        )

    def arrived(dst, recv_sem, send_sem):
        remote(dst, dst, send_sem, recv_sem, dev(z, y, 1 - c, t)).wait_recv()

    def send(pending, *args):
        copy = remote(*args)
        copy.start()
        pending.append(copy)

    line = [(dy, dl) for dy in range(NY) for dl in range(2)]
    sides = [(0, 1), (0, -1), (1, 0), (-1, 0)]

    barrier = pltpu.get_barrier_semaphore()

    def greet(device):
        pl.semaphore_signal(barrier, inc=1, device_id=device, device_id_type=MESH)

    @pl.when(c == 0)
    def _():
        for dz, dy in sides:
            for cc in range(2):
                greet(dev(at_z(dz), at_y(dy), cc, t))
        greet(dev(z, y, 1, t))

    @pl.when(c == 1)
    def _():
        for dy, dl in line[1:]:
            for cc in range(2):
                greet(dev(z, at_y(dy), cc, other(dl) * 4 + x))
        greet(dev(z, y, 0, t))
        for k in range(1, NX):
            greet((r, ylo * 4 + at_x(k)))
        for k in range(1, NZ):
            greet(dev(at_z(k), y, 1, t))

    columns = pl.ds(pl.multiple_of(t * KV, KV), KV)

    def chunk(zz, yy):
        return pas.at[zz, yy, :, pl.ds(0, KEPT)]

    def kept(zz, yy, cc):
        return pas.at[zz, yy, cc, pl.ds(0, KEPT)]

    def column(yy):
        return pas.at[:, yy, :, pl.ds(KEPT, SEL)]

    def half_column(yy, cc):
        return pas.at[:, yy, cc, pl.ds(KEPT, SEL)]

    def fresh_slot(zz):
        return pas.at[zz, y, :, pl.ds(KEPT, SEL)]

    def xpiece(ts, ys, cs):
        return xbuf.at[ts, :, :, pl.ds(pl.multiple_of((ys * 2 + cs) * HD, HD), HD)]

    def wpiece(ys, cs):
        return wbuf.at[ys, cs]

    loads = []

    def load(source, target):
        copy = pltpu.make_async_copy(source, target, local_sem.at[len(loads)])
        copy.start()
        loads.append(copy)
        return copy

    load_sel = load(sel_hbm, sel_ref)
    load_stale = load(stale_hbm.at[0], stale_ref)
    load_x = load(x_hbm, x_ref)
    load_w = load(w_hbm.at[:, columns], w_ref)
    load_cos = load(cos_hbm, cos_ref)
    load_sin = load(sin_hbm, sin_ref)

    load_sel.wait()
    lane = lax.broadcasted_iota(jnp.int32, (8, PLEN), 1)
    hit = lane == sel_ref[0, r]
    for k in range(1, SEL):
        hit = hit | (lane == sel_ref[k, r])
    keep = jnp.where(hit, jnp.float32(0.0), jnp.float32(1.0))
    before = lax.broadcasted_iota(jnp.int32, (PLEN, PLEN), 0) < lax.broadcasted_iota(jnp.int32, (PLEN, PLEN), 1)
    rank = jnp.dot(
        keep.astype(jnp.bfloat16),
        jnp.where(before, jnp.float32(1.0), jnp.float32(0.0)).astype(jnp.bfloat16),
        preferred_element_type=jnp.float32,
    )
    order = lax.broadcasted_iota(jnp.int32, (KEPT, PLEN), 0).astype(jnp.float32)
    picked = jnp.where(order == rank[0:1], keep[0:1], jnp.float32(0.0)).astype(jnp.bfloat16)
    load_stale.wait()
    own_rows[...] = jnp.dot(picked, stale_ref[...], preferred_element_type=jnp.float32).astype(jnp.bfloat16)
    load_x.wait()
    load_w.wait()
    load_cos.wait()
    load_sin.wait()

    @pl.when(c == 0)
    def _():
        pl.semaphore_wait(barrier, 12)

    @pl.when(c == 1)
    def _():
        pl.semaphore_wait(barrier, 22)

    started = []
    for k, (dy, dl) in enumerate(line[1:]):
        send(
            started, x_ref.at[at_y(dy)], xpiece(t, y, c), xy_send.at[k + 1], xy_recv.at[k + 1, c],
            dev(z, at_y(dy), 1, other(dl) * 4 + x),
        )
    for k in (2, 3, 0, 1):
        dz, dy = sides[k]
        send(
            started, own_rows, kept(z, y, c), seed_send.at[k], seed_recv.at[k, c], dev(at_z(dz), at_y(dy), 0, t)
        )
    for k in range(2):
        send(
            started, w_ref, wpiece(y, c), w_send.at[k], w_recv.at[k, c], dev(z, at_y(sides[k][1]), 1, t)
        )

    @pl.when(c == 0)
    def _():
        pending = []
        mate = dev(z, y, 1, t)
        send(pending, x_ref.at[y], xpiece(t, y, 0), xy_send.at[0], xy_recv.at[0, 0], mate)
        send(pending, w_ref, wpiece(y, 0), w_send.at[2], w_recv.at[2, 0], mate)
        own_copy = pltpu.make_async_copy(own_rows, kept(z, y, 0), local_sem.at[len(loads)])
        own_copy.start()

        def ring(zz, yy, s, d, way):
            step = 1 if way == 0 else -1
            send(
                pending, chunk(zz, yy), chunk(zz, yy), sz_send.at[way, s, d], sz_recv.at[way, s, d],
                dev(at_z(step), y, 0, t),
            )

        def share(zz, yy, rel, d):
            send(pending, chunk(zz, yy), chunk(zz, yy), ss_send.at[rel, d], ss_recv.at[rel, d], mate)

        def inject(d):
            for way in range(2):
                ring(z, at_y(d), 1, d, way)
            share(z, at_y(d), 0, d)

        def hop(s, d):
            for way in range(2):
                if s == 4 and (d < 2) != (way == 0):
                    continue
                rel = (-s if way == 0 else s) % NZ
                zz, yy = at_z(rel), at_y(d)
                if s == 1 and d == 0:
                    for cc in range(2):
                        arrived(kept(zz, yy, cc), seed_recv.at[2 + way, cc], seed_send.at[2 + way])
                else:
                    arrived(chunk(zz, yy), sz_recv.at[way, s, d], sz_send.at[way, s, d])
                if s < 3 or (s == 3 and (d < 2) == (way == 0)):
                    ring(zz, yy, s + 1, d, way)
                share(zz, yy, rel, d)

        hop(1, 0)
        for k in range(2):
            yy = at_y(-sides[k][1])
            for cc in range(2):
                arrived(kept(z, yy, cc), seed_recv.at[k, cc], seed_send.at[k])
            send(
                pending, kept(z, yy, k), kept(z, yy, k), yr_send.at[k], yr_recv.at[k],
                dev(z, at_y(sides[k][1]), 0, t),
            )
            inject(3 if k == 0 else 1)
        hop(2, 0)
        hop(1, 3)
        hop(1, 1)
        for k in range(2):
            arrived(kept(z, at_y(2), k), yr_recv.at[k], yr_send.at[k])
        inject(2)
        own_copy.wait()
        arrived(kept(z, y, 1), ss_recv.at[0, 0], ss_send.at[0, 0])
        send(pending, kept(z, y, 0), kept(z, y, 0), ss_send.at[0, 0], ss_recv.at[0, 0], mate)
        for s, d in (
            (3, 0), (2, 3), (2, 1), (1, 2), (4, 0), (3, 3), (3, 1), (2, 2), (4, 3), (4, 1), (3, 2), (4, 2),
        ):
            hop(s, d)
        for d in range(NY):
            arrived(column(at_y(d)), fs_recv.at[d], fs_send.at[d])
        for copy in pending:
            copy.wait_send()

    @pl.when(c == 1)
    def _():
        pending = []
        mate = dev(z, y, 0, t)
        own_x = pltpu.make_async_copy(x_ref.at[y], xpiece(t, y, 1), local_sem.at[len(loads)])
        own_w = pltpu.make_async_copy(w_ref, wpiece(y, 1), local_sem.at[len(loads) + 1])
        own_copy = pltpu.make_async_copy(own_rows, kept(z, y, 1), local_sem.at[len(loads) + 2])
        own_x.start()
        own_w.start()
        own_copy.start()
        send(pending, own_rows, kept(z, y, 1), ss_send.at[0, 0], ss_recv.at[0, 0], mate)
        own_x.wait()
        arrived(xpiece(t, y, 0), xy_recv.at[0, 0], xy_send.at[0])
        for k, (dy, dl) in enumerate(line[1:]):
            for cc in range(2):
                arrived(xpiece(other(dl) * 4 + x, at_y(-dy), cc), xy_recv.at[k + 1, cc], xy_send.at[k + 1])
        xall = xbuf.reshape(2, 4, 2, SEL, 8 * HD)
        for k in range(1, NX):
            send(
                pending, xall.at[:, x], xall.at[:, x], xx_send.at[k], xx_recv.at[k], (r, ylo * 4 + at_x(k))
            )
        for k in range(2):
            yy = at_y(-sides[k][1])
            for cc in range(2):
                arrived(wpiece(yy, cc), w_recv.at[k, cc], w_send.at[k])
            send(
                pending, wpiece(yy, k), wpiece(yy, k), wr_send.at[k], wr_recv.at[k],
                dev(z, at_y(sides[k][1]), 1, t),
            )
        for cc in range(2):
            for k in range(SEL):
                position = sel_ref[k, r - 1 + cc]
                trig_c[cc, pl.ds(k, 1), :] = cos_ref[pl.ds(position, 1), :]
                trig_s[cc, pl.ds(k, 1), :] = sin_ref[pl.ds(position, 1), :]
        own_w.wait()
        arrived(wpiece(y, 0), w_recv.at[2, 0], w_send.at[2])
        for k in range(1, NX):
            arrived(xall.at[:, at_x(-k)], xx_recv.at[k], xx_send.at[k])
        for k in range(2):
            arrived(wpiece(at_y(2), k), wr_recv.at[k], wr_send.at[k])
        part = jnp.dot(
            xbuf[...].reshape(NZ * 2 * SEL, 8 * HD),
            wbuf[...].reshape(8 * HD, KV),
            preferred_element_type=jnp.float32,
        )
        zsum[...] = part.reshape(NZ, 2, SEL, KV)
        for k in range(1, NZ):
            send(
                pending, zsum.at[at_z(k)], zrecv.at[k], rz_send.at[k], rz_recv.at[k], dev(at_z(k), y, 1, t)
            )
        total = zsum[z]
        for k in range(1, NZ):
            arrived(zrecv.at[k], rz_recv.at[k], rz_send.at[k])
            total = total + zrecv[k]
        fresh = total.astype(jnp.bfloat16).astype(jnp.float32)
        for cc in range(2):
            keys = fresh[cc, :, :HD]
            keys = keys * trig_c[cc] + pltpu.roll(keys, HD // 2, 1) * trig_s[cc]
            own_fresh[cc, :, :HD] = keys.astype(jnp.bfloat16)
            own_fresh[cc, :, HD:] = fresh[cc, :, HD:].astype(jnp.bfloat16)
        for k in range(1, NZ):
            send(pending, own_fresh, fresh_slot(z), fz_send.at[k], fz_recv.at[k], dev(at_z(k), y, 1, t))
        keep_fresh = pltpu.make_async_copy(own_fresh, fresh_slot(z), local_sem.at[len(loads) + 3])
        keep_fresh.start()
        keep_fresh.wait()
        for k in range(1, NZ):
            arrived(fresh_slot(at_z(-k)), fz_recv.at[k], fz_send.at[k])

        def share(d):
            send(pending, column(at_y(d)), column(at_y(d)), fs_send.at[d], fs_recv.at[d], mate)

        for k in range(2):
            send(
                pending, column(y), column(y), fy_send.at[k], fy_recv.at[k], dev(z, at_y(sides[k][1]), 1, t)
            )
        share(0)
        for k in range(2):
            yy = at_y(-sides[k][1])
            arrived(column(yy), fy_recv.at[k], fy_send.at[k])
            send(
                pending, half_column(yy, k), half_column(yy, k), fr_send.at[k], fr_recv.at[k],
                dev(z, at_y(sides[k][1]), 1, t),
            )
            share(3 if k == 0 else 1)
        for k in range(2):
            arrived(half_column(at_y(2), k), fr_recv.at[k], fr_send.at[k])
        share(2)
        own_copy.wait()
        arrived(kept(z, y, 0), ss_recv.at[0, 0], ss_send.at[0, 0])
        for rel in range(NZ):
            for d in range(NY):
                if rel or d:
                    arrived(chunk(at_z(rel), at_y(d)), ss_recv.at[rel, d], ss_send.at[rel, d])
        for copy in pending:
            copy.wait_send()

    for copy in started:
        copy.wait_send()


PAIR = 2


def attend_kernel(owner_ref, chosen_ref, *refs):
    blocks, (cos_ref, sin_ref, q_ref, own_ref, out_ref), scratch = refs[:8], refs[8:13], refs[13:]
    kbufs, vbufs, sbufs, pbufs = scratch[0:2], scratch[2:4], scratch[4:6], scratch[6:8]
    col = lax.broadcasted_iota(jnp.int32, (CHUNK, 128), 1)
    token = lax.rem(lax.broadcasted_iota(jnp.int32, (CHUNK, 128), 0), QLEN)
    tail = jnp.where(col <= token, jnp.float32(0.0), jnp.float32(NEG))

    def turn(block, j):
        wide = block.astype(jnp.float32)
        wide = wide * cos_ref[j : j + 1, :] + pltpu.roll(wide, HD // 2, 1) * sin_ref[j : j + 1, :]
        return wide.astype(jnp.bfloat16)

    for i in range(PAIR):
        kbuf, vbuf = kbufs[i], vbufs[i]
        for j in range(SLOTS):
            block = blocks[i * SLOTS + j]
            keys = block[0, :, :HD]
            kbuf[j * PLEN : (j + 1) * PLEN, :] = turn(keys, j) if j else keys
            vbuf[j * PLEN : (j + 1) * PLEN, :] = block[0, :, HD:]
        kbuf[LAST : LAST + QLEN, :] = own_ref[i, :, :HD]
        vbuf[LAST : LAST + QLEN, :] = own_ref[i, :, HD:]
        kbuf[LAST + QLEN :, :] = jnp.zeros((128 - QLEN, HD), jnp.bfloat16)
        vbuf[LAST + QLEN :, :] = jnp.zeros((128 - QLEN, HD), jnp.bfloat16)
    for i in range(PAIR):
        query = q_ref[i]
        query = jnp.concatenate([query[:, h * HD : (h + 1) * HD] for h in range(GROUP)], 0)
        sbufs[i][...] = lax.dot_general(
            query, kbufs[i][...], (((1,), (1,)), ((), ())), preferred_element_type=jnp.float32
        )
    for i in range(PAIR):
        sbuf, pbuf = sbufs[i], pbufs[i]
        for first in range(0, GROUP * QLEN, CHUNK):
            rows = slice(first, first + CHUNK)
            raw = jnp.concatenate([sbuf[rows, :LAST], sbuf[rows, LAST:] + tail], 1)
            expo = jnp.exp2((raw - jnp.max(raw, 1, keepdims=True)) * SCALE)
            pbuf[rows, :] = (expo * (1.0 / jnp.sum(expo, 1, keepdims=True))).astype(jnp.bfloat16)
        result = jnp.dot(pbuf[...], vbufs[i][...], preferred_element_type=jnp.float32).astype(jnp.bfloat16)
        for h in range(GROUP):
            out_ref[i, :, h * HD : (h + 1) * HD] = result[h * QLEN : (h + 1) * QLEN]


def gather(stale, fresh_input, kv_weight, sel_index, cosine, sine):
    any_spec = pl.BlockSpec(memory_space=pl.ANY)
    dma = pltpu.SemaphoreType.DMA
    return pl.pallas_call(
        gather_kernel,
        out_shape=jax.ShapeDtypeStruct((NZ, NY, 2, PLEN, KV), jnp.bfloat16),
        in_specs=[any_spec] * 6,
        out_specs=any_spec,
        scratch_shapes=[
            pltpu.VMEM((PLEN, KV), jnp.bfloat16),
            pltpu.VMEM((KEPT, KV), jnp.bfloat16),
            pltpu.VMEM((2, SEL, KV), jnp.bfloat16),
            pltpu.VMEM((8, 2, SEL, 8 * HD), jnp.bfloat16),
            pltpu.VMEM((NY, 2, HD, KV), jnp.bfloat16),
            pltpu.VMEM((NZ, 2, SEL, KV), jnp.float32),
            pltpu.VMEM((NZ, 2, SEL, KV), jnp.float32),
            pltpu.VMEM((2, SEL, HD), jnp.float32),
            pltpu.VMEM((2, SEL, HD), jnp.float32),
            pltpu.VMEM((NY, 2, SEL, HD), jnp.bfloat16),
            pltpu.VMEM((HD, KV), jnp.bfloat16),
            pltpu.VMEM(cosine.shape, jnp.float32),
            pltpu.VMEM(sine.shape, jnp.float32),
            pltpu.SMEM((SEL, 64), jnp.int32),
            dma((12,)),
            dma((8,)), dma((8, 2)),
            dma((NX,)), dma((NX,)),
            dma((3,)), dma((3, 2)),
            dma((2,)), dma((2,)),
            dma((4,)), dma((4, 2)),
            dma((2,)), dma((2,)),
            dma((2, 5, NY)), dma((2, 5, NY)),
            dma((NZ, NY)), dma((NZ, NY)),
            dma((NZ,)), dma((NZ,)),
            dma((NZ,)), dma((NZ,)),
            dma((2,)), dma((2,)),
            dma((2,)), dma((2,)),
            dma((NY,)), dma((NY,)),
        ],
        compiler_params=pltpu.CompilerParams(
            collective_id=0, has_side_effects=True, vmem_limit_bytes=62 * 1024 * 1024
        ),
    )(
        stale,
        fresh_input.reshape(NY, 2, SEL, HD),
        kv_weight,
        sel_index.T,
        cosine,
        sine,
    )


def attend(owner, retrieval, passages, cosine, sine, queries, question_kv):
    def block_spec(k):
        i, j = k // SLOTS, k % SLOTS

        def place(step, owner_ref, chosen_ref):
            o = owner_ref[chosen_ref[j, PAIR * step + i]]
            return o, 0, 0

        return pl.BlockSpec((1, PLEN, KV), place)

    def by_pair(shape):
        return pl.BlockSpec((PAIR,) + shape[1:], lambda step, a, b: (step, 0, 0))

    def whole(shape):
        return pl.BlockSpec(shape, lambda step, a, b: (0, 0))

    rows = GROUP * QLEN
    return pl.pallas_call(
        attend_kernel,
        grid_spec=pltpu.PrefetchScalarGridSpec(
            num_scalar_prefetch=2,
            grid=(queries.shape[0] // PAIR,),
            in_specs=[block_spec(k) for k in range(PAIR * SLOTS)]
            + [whole(cosine.shape), whole(sine.shape), by_pair(queries.shape), by_pair(question_kv.shape)],
            out_specs=by_pair(queries.shape),
            scratch_shapes=[pltpu.VMEM((KEYS, HD), jnp.bfloat16)] * 4
            + [pltpu.VMEM((rows, KEYS), jnp.float32)] * 2
            + [pltpu.VMEM((rows, KEYS), jnp.bfloat16)] * 2,
        ),
        out_shape=jax.ShapeDtypeStruct(queries.shape, jnp.bfloat16),
        compiler_params=pltpu.CompilerParams(vmem_limit_bytes=62 * 1024 * 1024),
    )(owner, retrieval.T, *([passages] * (PAIR * SLOTS)), cosine, sine, queries, question_kv)


def local(stale, fresh_input, kv_weight, sel_index, owner, retrieval, queries, question_kv):
    cosine, sine = trig_tables()
    passages = gather(
        stale, fresh_input, kv_weight, sel_index, jnp.asarray(cosine[:PLEN]), jnp.asarray(sine[:PLEN])
    )
    return attend(
        owner, retrieval, passages.reshape(64, PLEN, KV), jnp.asarray(cosine[PLEN:]), jnp.asarray(sine[PLEN:]),
        queries, question_kv,
    )


def solution(mesh):
    return jax.shard_map(
        local,
        mesh=mesh,
        in_specs=(
            P("req", None, "tp"),
            P("tp", None, "req"),
            P("req", None),
            P(),
            P(),
            P("req", None),
            P("req", None, "tp"),
            P("req", None, "tp"),
        ),
        out_specs=P("req", None, "tp"),
        check_vma=False,
    )
```

```python
import functools
import math

import jax
import jax.numpy as jnp
import numpy as np
from jax import lax
from jax.experimental import pallas as pl
from jax.experimental.pallas import tpu as pltpu
from jax.sharding import PartitionSpec as P

MESH = pl.DeviceIdType.MESH
HD = 128
NZ, NY, NX = 8, 4, 4
PLEN, QLEN, SEL, SLOTS = 128, 32, 16, 4
GROUP = 8
KV = 2 * HD
LAST = SLOTS * PLEN
KEYS = LAST + 128
KEPT = PLEN - SEL
CHUNK = 64
SCALE = math.log2(math.e) / math.sqrt(HD)
NEG = -1e30
THETA = 500000.0
PAIR = 2


def trig_tables():
    positions = np.concatenate([np.arange(PLEN), np.arange(8) * PLEN]).astype(np.float32)
    freqs = (THETA ** (-(np.arange(HD // 2, dtype=np.float64) * 2.0 / HD))).astype(np.float32)
    angle = (positions[:, None] * freqs).astype(np.float32).astype(np.float64)
    cosine, sine = np.cos(angle), np.sin(angle)
    return (
        np.concatenate([cosine, cosine], -1).astype(np.float32),
        np.concatenate([-sine, sine], -1).astype(np.float32),
    )


def kernel(
    stale_hbm, x_hbm, w_hbm, sel_hbm, cos_hbm, sin_hbm, owner_hbm, chosen_hbm, q_hbm, own_hbm,
    out_hbm,
    pas, kbuf0, vbuf0, kbuf1, vbuf1, sbuf0, pbuf0, sbuf1, pbuf1, q_ref, own_ref, out_ref, owner_ref, chosen_ref,
    stale_ref, own_rows, own_fresh, xbuf, wbuf, zsum, zrecv, trig_c, trig_s, x_ref, w_ref, cos_ref, sin_ref, sel_ref,
    local_sem, xy_send, xy_recv, xx_send, xx_recv, w_send, w_recv, wr_send, wr_recv,
    seed_send, seed_recv, yr_send, yr_recv, sz_send, sz_recv, ss_send, ss_recv,
    rz_send, rz_recv, fz_send, fz_recv, fy_send, fy_recv, fr_send, fr_recv, fs_send, fs_recv, q_sem, out_sem,
):
    r, t = lax.axis_index("req"), lax.axis_index("tp")
    z, y, c = r // 8, lax.rem(r, 8) // 2, lax.rem(r, 2)
    ylo, x = t // 4, lax.rem(t, 4)

    def dev(zz, yy, cc, tt):
        return (zz * 8 + yy * 2 + cc, tt)

    def at_z(k):
        return lax.rem(z + k + 2 * NZ, NZ)

    def at_y(k):
        return lax.rem(y + k + 2 * NY, NY)

    def at_x(k):
        return lax.rem(x + k + 2 * NX, NX)

    def other(dl):
        return lax.rem(ylo + dl, 2)

    def remote(src, dst, send_sem, recv_sem, device):
        return pltpu.make_async_remote_copy(
            src_ref=src, dst_ref=dst, send_sem=send_sem, recv_sem=recv_sem,
            device_id=device, device_id_type=MESH,
        )

    def arrived(dst, recv_sem, send_sem):
        remote(dst, dst, send_sem, recv_sem, dev(z, y, 1 - c, t)).wait_recv()

    def send(pending, *args):
        copy = remote(*args)
        copy.start()
        pending.append(copy)

    line = [(dy, dl) for dy in range(NY) for dl in range(2)]
    sides = [(0, 1), (0, -1), (1, 0), (-1, 0)]

    barrier = pltpu.get_barrier_semaphore()

    def greet(device):
        pl.semaphore_signal(barrier, inc=1, device_id=device, device_id_type=MESH)

    @pl.when(c == 0)
    def _():
        for dz, dy in sides:
            for cc in range(2):
                greet(dev(at_z(dz), at_y(dy), cc, t))
        greet(dev(z, y, 1, t))

    @pl.when(c == 1)
    def _():
        for dy, dl in line[1:]:
            for cc in range(2):
                greet(dev(z, at_y(dy), cc, other(dl) * 4 + x))
        greet(dev(z, y, 0, t))
        for k in range(1, NX):
            greet((r, ylo * 4 + at_x(k)))
        for k in range(1, NZ):
            greet(dev(at_z(k), y, 1, t))

    columns = pl.ds(pl.multiple_of(t * KV, KV), KV)

    def chunk(zz, yy):
        return pas.at[zz, yy, :, pl.ds(0, KEPT)]

    def kept(zz, yy, cc):
        return pas.at[zz, yy, cc, pl.ds(0, KEPT)]

    def column(yy):
        return pas.at[:, yy, :, pl.ds(KEPT, SEL)]

    def half_column(yy, cc):
        return pas.at[:, yy, cc, pl.ds(KEPT, SEL)]

    def fresh_slot(zz):
        return pas.at[zz, y, :, pl.ds(KEPT, SEL)]

    def xpiece(ts, ys, cs):
        return xbuf.at[ts, :, :, pl.ds(pl.multiple_of((ys * 2 + cs) * HD, HD), HD)]

    def wpiece(ys, cs):
        return wbuf.at[ys, cs]

    loads = []

    def load(source, target):
        copy = pltpu.make_async_copy(source, target, local_sem.at[len(loads)])
        copy.start()
        loads.append(copy)
        return copy

    load_sel = load(sel_hbm, sel_ref)
    load_stale = load(stale_hbm.at[0], stale_ref)
    load_x = load(x_hbm, x_ref)
    load_w = load(w_hbm.at[:, columns], w_ref)
    load_cos = load(cos_hbm, cos_ref)
    load_sin = load(sin_hbm, sin_ref)
    load_owner = load(owner_hbm, owner_ref)
    load_chosen = load(chosen_hbm, chosen_ref)
    later = []
    for k, (source, target) in enumerate(((q_hbm, q_ref), (own_hbm, own_ref))):
        later.append(pltpu.make_async_copy(source, target, q_sem.at[k]))
        later[-1].start()

    load_sel.wait()
    lane = lax.broadcasted_iota(jnp.int32, (8, PLEN), 1)
    hit = lane == sel_ref[0, r]
    for k in range(1, SEL):
        hit = hit | (lane == sel_ref[k, r])
    keep = jnp.where(hit, jnp.float32(0.0), jnp.float32(1.0))
    before = lax.broadcasted_iota(jnp.int32, (PLEN, PLEN), 0) < lax.broadcasted_iota(jnp.int32, (PLEN, PLEN), 1)
    rank = jnp.dot(
        keep.astype(jnp.bfloat16),
        jnp.where(before, jnp.float32(1.0), jnp.float32(0.0)).astype(jnp.bfloat16),
        preferred_element_type=jnp.float32,
    )
    order = lax.broadcasted_iota(jnp.int32, (KEPT, PLEN), 0).astype(jnp.float32)
    picked = jnp.where(order == rank[0:1], keep[0:1], jnp.float32(0.0)).astype(jnp.bfloat16)
    load_stale.wait()
    own_rows[...] = jnp.dot(picked, stale_ref[...], preferred_element_type=jnp.float32).astype(jnp.bfloat16)
    load_x.wait()
    load_w.wait()
    load_cos.wait()
    load_sin.wait()
    load_owner.wait()
    load_chosen.wait()

    @pl.when(c == 0)
    def _():
        pl.semaphore_wait(barrier, 12)

    @pl.when(c == 1)
    def _():
        pl.semaphore_wait(barrier, 22)

    started = []
    for k, (dy, dl) in enumerate(line[1:]):
        send(
            started, x_ref.at[at_y(dy)], xpiece(t, y, c), xy_send.at[k + 1], xy_recv.at[k + 1, c],
            dev(z, at_y(dy), 1, other(dl) * 4 + x),
        )
    for k in (2, 3, 0, 1):
        dz, dy = sides[k]
        send(
            started, own_rows, kept(z, y, c), seed_send.at[k], seed_recv.at[k, c], dev(at_z(dz), at_y(dy), 0, t)
        )
    for k in range(2):
        send(
            started, w_ref, wpiece(y, c), w_send.at[k], w_recv.at[k, c], dev(z, at_y(sides[k][1]), 1, t)
        )

    @pl.when(c == 0)
    def _():
        pending = []
        mate = dev(z, y, 1, t)
        send(pending, x_ref.at[y], xpiece(t, y, 0), xy_send.at[0], xy_recv.at[0, 0], mate)
        send(pending, w_ref, wpiece(y, 0), w_send.at[2], w_recv.at[2, 0], mate)
        own_copy = pltpu.make_async_copy(own_rows, kept(z, y, 0), local_sem.at[len(loads)])
        own_copy.start()

        def ring(zz, yy, s, d, way):
            step = 1 if way == 0 else -1
            send(
                pending, chunk(zz, yy), chunk(zz, yy), sz_send.at[way, s, d], sz_recv.at[way, s, d],
                dev(at_z(step), y, 0, t),
            )

        def share(zz, yy, rel, d):
            send(pending, chunk(zz, yy), chunk(zz, yy), ss_send.at[rel, d], ss_recv.at[rel, d], mate)

        def inject(d):
            for way in range(2):
                ring(z, at_y(d), 1, d, way)
            share(z, at_y(d), 0, d)

        def hop(s, d):
            for way in range(2):
                if s == 4 and (d < 2) != (way == 0):
                    continue
                rel = (-s if way == 0 else s) % NZ
                zz, yy = at_z(rel), at_y(d)
                if s == 1 and d == 0:
                    for cc in range(2):
                        arrived(kept(zz, yy, cc), seed_recv.at[2 + way, cc], seed_send.at[2 + way])
                else:
                    arrived(chunk(zz, yy), sz_recv.at[way, s, d], sz_send.at[way, s, d])
                if s < 3 or (s == 3 and (d < 2) == (way == 0)):
                    ring(zz, yy, s + 1, d, way)
                share(zz, yy, rel, d)

        hop(1, 0)
        for k in range(2):
            yy = at_y(-sides[k][1])
            for cc in range(2):
                arrived(kept(z, yy, cc), seed_recv.at[k, cc], seed_send.at[k])
            send(
                pending, kept(z, yy, k), kept(z, yy, k), yr_send.at[k], yr_recv.at[k],
                dev(z, at_y(sides[k][1]), 0, t),
            )
            inject(3 if k == 0 else 1)
        hop(2, 0)
        hop(1, 3)
        hop(1, 1)
        for k in range(2):
            arrived(kept(z, at_y(2), k), yr_recv.at[k], yr_send.at[k])
        inject(2)
        own_copy.wait()
        arrived(kept(z, y, 1), ss_recv.at[0, 0], ss_send.at[0, 0])
        send(pending, kept(z, y, 0), kept(z, y, 0), ss_send.at[0, 0], ss_recv.at[0, 0], mate)
        for s, d in (
            (3, 0), (2, 3), (2, 1), (1, 2), (4, 0), (3, 3), (3, 1), (2, 2), (4, 3), (4, 1), (3, 2), (4, 2),
        ):
            hop(s, d)
        for d in range(NY):
            arrived(column(at_y(d)), fs_recv.at[d], fs_send.at[d])
        for copy in pending:
            copy.wait_send()

    @pl.when(c == 1)
    def _():
        pending = []
        mate = dev(z, y, 0, t)
        own_x = pltpu.make_async_copy(x_ref.at[y], xpiece(t, y, 1), local_sem.at[len(loads)])
        own_w = pltpu.make_async_copy(w_ref, wpiece(y, 1), local_sem.at[len(loads) + 1])
        own_copy = pltpu.make_async_copy(own_rows, kept(z, y, 1), local_sem.at[len(loads) + 2])
        own_x.start()
        own_w.start()
        own_copy.start()
        send(pending, own_rows, kept(z, y, 1), ss_send.at[0, 0], ss_recv.at[0, 0], mate)
        own_x.wait()
        arrived(xpiece(t, y, 0), xy_recv.at[0, 0], xy_send.at[0])
        for k, (dy, dl) in enumerate(line[1:]):
            for cc in range(2):
                arrived(xpiece(other(dl) * 4 + x, at_y(-dy), cc), xy_recv.at[k + 1, cc], xy_send.at[k + 1])
        xall = xbuf.reshape(2, 4, 2, SEL, 8 * HD)
        for k in range(1, NX):
            send(
                pending, xall.at[:, x], xall.at[:, x], xx_send.at[k], xx_recv.at[k], (r, ylo * 4 + at_x(k))
            )
        for k in range(2):
            yy = at_y(-sides[k][1])
            for cc in range(2):
                arrived(wpiece(yy, cc), w_recv.at[k, cc], w_send.at[k])
            send(
                pending, wpiece(yy, k), wpiece(yy, k), wr_send.at[k], wr_recv.at[k],
                dev(z, at_y(sides[k][1]), 1, t),
            )
        for cc in range(2):
            for k in range(SEL):
                position = sel_ref[k, r - 1 + cc]
                trig_c[cc, pl.ds(k, 1), :] = cos_ref[pl.ds(position, 1), :]
                trig_s[cc, pl.ds(k, 1), :] = sin_ref[pl.ds(position, 1), :]
        own_w.wait()
        arrived(wpiece(y, 0), w_recv.at[2, 0], w_send.at[2])
        for k in range(1, NX):
            arrived(xall.at[:, at_x(-k)], xx_recv.at[k], xx_send.at[k])
        for k in range(2):
            arrived(wpiece(at_y(2), k), wr_recv.at[k], wr_send.at[k])
        part = jnp.dot(
            xbuf[...].reshape(NZ * 2 * SEL, 8 * HD),
            wbuf[...].reshape(8 * HD, KV),
            preferred_element_type=jnp.float32,
        )
        zsum[...] = part.reshape(NZ, 2, SEL, KV)
        for k in range(1, NZ):
            send(
                pending, zsum.at[at_z(k)], zrecv.at[k], rz_send.at[k], rz_recv.at[k], dev(at_z(k), y, 1, t)
            )
        total = zsum[z]
        for k in range(1, NZ):
            arrived(zrecv.at[k], rz_recv.at[k], rz_send.at[k])
            total = total + zrecv[k]
        fresh = total.astype(jnp.bfloat16).astype(jnp.float32)
        for cc in range(2):
            keys = fresh[cc, :, :HD]
            keys = keys * trig_c[cc] + pltpu.roll(keys, HD // 2, 1) * trig_s[cc]
            own_fresh[cc, :, :HD] = keys.astype(jnp.bfloat16)
            own_fresh[cc, :, HD:] = fresh[cc, :, HD:].astype(jnp.bfloat16)
        for k in range(1, NZ):
            send(pending, own_fresh, fresh_slot(z), fz_send.at[k], fz_recv.at[k], dev(at_z(k), y, 1, t))
        keep_fresh = pltpu.make_async_copy(own_fresh, fresh_slot(z), local_sem.at[len(loads) + 3])
        keep_fresh.start()
        keep_fresh.wait()
        for k in range(1, NZ):
            arrived(fresh_slot(at_z(-k)), fz_recv.at[k], fz_send.at[k])

        def share(d):
            send(pending, column(at_y(d)), column(at_y(d)), fs_send.at[d], fs_recv.at[d], mate)

        for k in range(2):
            send(
                pending, column(y), column(y), fy_send.at[k], fy_recv.at[k], dev(z, at_y(sides[k][1]), 1, t)
            )
        share(0)
        for k in range(2):
            yy = at_y(-sides[k][1])
            arrived(column(yy), fy_recv.at[k], fy_send.at[k])
            send(
                pending, half_column(yy, k), half_column(yy, k), fr_send.at[k], fr_recv.at[k],
                dev(z, at_y(sides[k][1]), 1, t),
            )
            share(3 if k == 0 else 1)
        for k in range(2):
            arrived(half_column(at_y(2), k), fr_recv.at[k], fr_send.at[k])
        share(2)
        own_copy.wait()
        arrived(kept(z, y, 0), ss_recv.at[0, 0], ss_send.at[0, 0])
        for rel in range(NZ):
            for d in range(NY):
                if rel or d:
                    arrived(chunk(at_z(rel), at_y(d)), ss_recv.at[rel, d], ss_send.at[rel, d])
        for copy in pending:
            copy.wait_send()

    for copy in started:
        copy.wait_send()

    kbufs, vbufs, sbufs, pbufs = (kbuf0, kbuf1), (vbuf0, vbuf1), (sbuf0, sbuf1), (pbuf0, pbuf1)
    steps = q_ref.shape[0] // PAIR

    def result_copy(step):
        rows = pl.ds(step * PAIR, PAIR)
        return pltpu.make_async_copy(out_ref.at[rows], out_hbm.at[rows], out_sem.at[step])

    col = lax.broadcasted_iota(jnp.int32, (CHUNK, 128), 1)
    token = lax.rem(lax.broadcasted_iota(jnp.int32, (CHUNK, 128), 0), QLEN)
    tail = jnp.where(col <= token, jnp.float32(0.0), jnp.float32(NEG))
    for i in range(PAIR):
        kbufs[i][LAST + QLEN :, :] = jnp.zeros((128 - QLEN, HD), jnp.bfloat16)
        vbufs[i][LAST + QLEN :, :] = jnp.zeros((128 - QLEN, HD), jnp.bfloat16)
    for copy in later:
        copy.wait()

    def turn(block, j):
        wide = block.astype(jnp.float32)
        wide = wide * cos_ref[PLEN + j : PLEN + j + 1, :] + pltpu.roll(wide, HD // 2, 1) * sin_ref[PLEN + j : PLEN + j + 1, :]
        return wide.astype(jnp.bfloat16)

    def pair(step, carry):
        for i in range(PAIR):
            kbuf, vbuf = kbufs[i], vbufs[i]
            request = step * PAIR + i
            for j in range(SLOTS):
                o = owner_ref[chosen_ref[j, request]]
                block = pas[o // 8, lax.rem(o, 8) // 2, lax.rem(o, 2)]
                keys = block[:, :HD]
                kbuf[j * PLEN : (j + 1) * PLEN, :] = turn(keys, j) if j else keys
                vbuf[j * PLEN : (j + 1) * PLEN, :] = block[:, HD:]
            own = own_ref[request]
            kbuf[LAST : LAST + QLEN, :] = own[:, :HD]
            vbuf[LAST : LAST + QLEN, :] = own[:, HD:]
        for i in range(PAIR):
            query = q_ref[step * PAIR + i]
            query = jnp.concatenate([query[:, h * HD : (h + 1) * HD] for h in range(GROUP)], 0)
            sbufs[i][...] = lax.dot_general(
                query, kbufs[i][...], (((1,), (1,)), ((), ())), preferred_element_type=jnp.float32
            )
        for i in range(PAIR):
            sbuf, pbuf = sbufs[i], pbufs[i]
            for first in range(0, GROUP * QLEN, CHUNK):
                rows = slice(first, first + CHUNK)
                raw = jnp.concatenate([sbuf[rows, :LAST], sbuf[rows, LAST:] + tail], 1)
                expo = jnp.exp2((raw - jnp.max(raw, 1, keepdims=True)) * SCALE)
                pbuf[rows, :] = (expo * (1.0 / jnp.sum(expo, 1, keepdims=True))).astype(jnp.bfloat16)
            result = jnp.dot(pbuf[...], vbufs[i][...], preferred_element_type=jnp.float32).astype(jnp.bfloat16)
            for h in range(GROUP):
                out_ref[step * PAIR + i, :, h * HD : (h + 1) * HD] = result[h * QLEN : (h + 1) * QLEN]
        result_copy(step).start()
        return carry

    lax.fori_loop(0, steps, pair, 0)
    for step in range(steps):
        result_copy(step).wait()


def local(stale, fresh_input, kv_weight, sel_index, owner, retrieval, queries, question_kv):
    cosine, sine = trig_tables()
    any_spec = pl.BlockSpec(memory_space=pl.ANY)
    dma = pltpu.SemaphoreType.DMA
    rows = GROUP * QLEN
    return pl.pallas_call(
        kernel,
        out_shape=jax.ShapeDtypeStruct(queries.shape, jnp.bfloat16),
        in_specs=[any_spec] * 10,
        out_specs=any_spec,
        scratch_shapes=[
            pltpu.VMEM((NZ, NY, 2, PLEN, KV), jnp.bfloat16),
            pltpu.VMEM((KEYS, HD), jnp.bfloat16),
            pltpu.VMEM((KEYS, HD), jnp.bfloat16),
            pltpu.VMEM((KEYS, HD), jnp.bfloat16),
            pltpu.VMEM((KEYS, HD), jnp.bfloat16),
            pltpu.VMEM((rows, KEYS), jnp.float32),
            pltpu.VMEM((rows, KEYS), jnp.bfloat16),
            pltpu.VMEM((rows, KEYS), jnp.float32),
            pltpu.VMEM((rows, KEYS), jnp.bfloat16),
            pltpu.VMEM(queries.shape, jnp.bfloat16),
            pltpu.VMEM(question_kv.shape, jnp.bfloat16),
            pltpu.VMEM(queries.shape, jnp.bfloat16),
            pltpu.SMEM((64,), jnp.int32),
            pltpu.SMEM((SLOTS, 8), jnp.int32),
            pltpu.VMEM((PLEN, KV), jnp.bfloat16),
            pltpu.VMEM((KEPT, KV), jnp.bfloat16),
            pltpu.VMEM((2, SEL, KV), jnp.bfloat16),
            pltpu.VMEM((8, 2, SEL, 8 * HD), jnp.bfloat16),
            pltpu.VMEM((NY, 2, HD, KV), jnp.bfloat16),
            pltpu.VMEM((NZ, 2, SEL, KV), jnp.float32),
            pltpu.VMEM((NZ, 2, SEL, KV), jnp.float32),
            pltpu.VMEM((2, SEL, HD), jnp.float32),
            pltpu.VMEM((2, SEL, HD), jnp.float32),
            pltpu.VMEM((NY, 2, SEL, HD), jnp.bfloat16),
            pltpu.VMEM((HD, KV), jnp.bfloat16),
            pltpu.VMEM(cosine.shape, jnp.float32),
            pltpu.VMEM(sine.shape, jnp.float32),
            pltpu.SMEM((SEL, 64), jnp.int32),
            dma((12,)),
            dma((8,)), dma((8, 2)),
            dma((NX,)), dma((NX,)),
            dma((3,)), dma((3, 2)),
            dma((2,)), dma((2,)),
            dma((4,)), dma((4, 2)),
            dma((2,)), dma((2,)),
            dma((2, 5, NY)), dma((2, 5, NY)),
            dma((NZ, NY)), dma((NZ, NY)),
            dma((NZ,)), dma((NZ,)),
            dma((NZ,)), dma((NZ,)),
            dma((2,)), dma((2,)),
            dma((2,)), dma((2,)),
            dma((NY,)), dma((NY,)),
            dma((2,)), dma((4,)),
        ],
        compiler_params=pltpu.CompilerParams(
            collective_id=0, has_side_effects=True, vmem_limit_bytes=62 * 1024 * 1024
        ),
    )(
        stale,
        fresh_input.reshape(NY, 2, SEL, HD),
        kv_weight,
        sel_index.T,
        jnp.asarray(cosine),
        jnp.asarray(sine),
        owner,
        retrieval.T,
        queries,
        question_kv,
    )


def solution(mesh):
    return jax.shard_map(
        local,
        mesh=mesh,
        in_specs=(
            P("req", None, "tp"),
            P("tp", None, "req"),
            P("req", None),
            P(),
            P(),
            P("req", None),
            P("req", None, "tp"),
            P("req", None, "tp"),
        ),
        out_specs=P("req", None, "tp"),
        check_vma=False,
    )
```

```python
import functools
import math

import jax
import jax.numpy as jnp
import numpy as np
from jax import lax
from jax.experimental import pallas as pl
from jax.experimental.pallas import tpu as pltpu
from jax.sharding import PartitionSpec as P

MESH = pl.DeviceIdType.MESH
HD = 128
NZ, NY, NX = 8, 4, 4
PLEN, QLEN, SEL, SLOTS = 128, 32, 16, 4
GROUP = 8
KV = 2 * HD
LAST = SLOTS * PLEN
KEYS = LAST + 128
KEPT = PLEN - SEL
CHUNK = 64
SCALE = math.log2(math.e) / math.sqrt(HD)
NEG = -1e30
THETA = 500000.0
PAIR = 2


def trig_tables():
    positions = np.concatenate([np.arange(PLEN), np.arange(8) * PLEN]).astype(np.float32)
    freqs = (THETA ** (-(np.arange(HD // 2, dtype=np.float64) * 2.0 / HD))).astype(np.float32)
    angle = (positions[:, None] * freqs).astype(np.float32).astype(np.float64)
    cosine, sine = np.cos(angle), np.sin(angle)
    return (
        np.concatenate([cosine, cosine], -1).astype(np.float32),
        np.concatenate([-sine, sine], -1).astype(np.float32),
    )


def kernel(
    stale_hbm, x_hbm, w_hbm, sel_hbm, cos_hbm, sin_hbm, owner_hbm, chosen_hbm, q_hbm, own_hbm,
    out_hbm,
    pas, kbuf0, vbuf0, kbuf1, vbuf1, sbuf0, pbuf0, sbuf1, pbuf1, q_ref, own_ref, out_ref, owner_ref, chosen_ref,
    stale_ref, own_rows, own_fresh, xbuf, wbuf, zsum, zrecv, trig_c, trig_s, x_ref, w_ref, cos_ref, sin_ref, sel_ref,
    local_sem, xy_send, xy_recv, xx_send, xx_recv, w_send, w_recv, wr_send, wr_recv,
    seed_send, seed_recv, yr_send, yr_recv, yf_send, yf_recv, sz_send, sz_recv, ss_send, ss_recv,
    rz_send, rz_recv, fz_send, fz_recv, fy_send, fy_recv, fr_send, fr_recv, fs_send, fs_recv, q_sem, out_sem,
):
    r, t = lax.axis_index("req"), lax.axis_index("tp")
    z, y, c = r // 8, lax.rem(r, 8) // 2, lax.rem(r, 2)
    ylo, x = t // 4, lax.rem(t, 4)

    def dev(zz, yy, cc, tt):
        return (zz * 8 + yy * 2 + cc, tt)

    def at_z(k):
        return lax.rem(z + k + 2 * NZ, NZ)

    def at_y(k):
        return lax.rem(y + k + 2 * NY, NY)

    def at_x(k):
        return lax.rem(x + k + 2 * NX, NX)

    def other(dl):
        return lax.rem(ylo + dl, 2)

    def remote(src, dst, send_sem, recv_sem, device):
        return pltpu.make_async_remote_copy(
            src_ref=src, dst_ref=dst, send_sem=send_sem, recv_sem=recv_sem,
            device_id=device, device_id_type=MESH,
        )

    def arrived(dst, recv_sem, send_sem):
        remote(dst, dst, send_sem, recv_sem, dev(z, y, 1 - c, t)).wait_recv()

    def send(pending, *args):
        copy = remote(*args)
        copy.start()
        pending.append(copy)

    line = [(dy, dl) for dy in range(NY) for dl in range(2)]
    sides = [(0, 1), (0, -1), (1, 0), (-1, 0)]

    barrier = pltpu.get_barrier_semaphore()

    def greet(device):
        pl.semaphore_signal(barrier, inc=1, device_id=device, device_id_type=MESH)

    @pl.when(c == 0)
    def _():
        for dz, dy in sides:
            for cc in range(2):
                greet(dev(at_z(dz), at_y(dy), cc, t))
        greet(dev(z, y, 1, t))

    @pl.when(c == 1)
    def _():
        for dy, dl in line[1:]:
            for cc in range(2):
                greet(dev(z, at_y(dy), cc, other(dl) * 4 + x))
        greet(dev(z, y, 0, t))
        for k in range(1, NX):
            greet((r, ylo * 4 + at_x(k)))
        for k in range(1, NZ):
            greet(dev(at_z(k), y, 1, t))

    columns = pl.ds(pl.multiple_of(t * KV, KV), KV)

    def chunk(zz, yy):
        return pas.at[zz, yy, :, pl.ds(0, KEPT)]

    def kept(zz, yy, cc):
        return pas.at[zz, yy, cc, pl.ds(0, KEPT)]

    def column(yy):
        return pas.at[:, yy, :, pl.ds(KEPT, SEL)]

    def piece(zz, yy):
        return pas.at[zz, yy, :, pl.ds(KEPT, SEL)]

    def half_piece(zz, yy, cc):
        return pas.at[zz, yy, cc, pl.ds(KEPT, SEL)]

    def xpiece(ts, ys, cs):
        return xbuf.at[ts, :, :, pl.ds(pl.multiple_of((ys * 2 + cs) * HD, HD), HD)]

    def wpiece(ys, cs):
        return wbuf.at[ys, cs]

    loads = []

    def load(source, target):
        copy = pltpu.make_async_copy(source, target, local_sem.at[len(loads)])
        copy.start()
        loads.append(copy)
        return copy

    load_sel = load(sel_hbm, sel_ref)
    load_stale = load(stale_hbm.at[0], stale_ref)
    load_x = load(x_hbm, x_ref)
    load_w = load(w_hbm.at[:, columns], w_ref)
    load_cos = load(cos_hbm, cos_ref)
    load_sin = load(sin_hbm, sin_ref)
    load_owner = load(owner_hbm, owner_ref)
    load_chosen = load(chosen_hbm, chosen_ref)
    later = []
    for k, (source, target) in enumerate(((q_hbm, q_ref), (own_hbm, own_ref))):
        later.append(pltpu.make_async_copy(source, target, q_sem.at[k]))
        later[-1].start()

    load_sel.wait()
    lane = lax.broadcasted_iota(jnp.int32, (8, PLEN), 1)
    hit = lane == sel_ref[0, r]
    for k in range(1, SEL):
        hit = hit | (lane == sel_ref[k, r])
    keep = jnp.where(hit, jnp.float32(0.0), jnp.float32(1.0))
    before = lax.broadcasted_iota(jnp.int32, (PLEN, PLEN), 0) < lax.broadcasted_iota(jnp.int32, (PLEN, PLEN), 1)
    rank = jnp.dot(
        keep.astype(jnp.bfloat16),
        jnp.where(before, jnp.float32(1.0), jnp.float32(0.0)).astype(jnp.bfloat16),
        preferred_element_type=jnp.float32,
    )
    order = lax.broadcasted_iota(jnp.int32, (KEPT, PLEN), 0).astype(jnp.float32)
    picked = jnp.where(order == rank[0:1], keep[0:1], jnp.float32(0.0)).astype(jnp.bfloat16)
    load_stale.wait()
    own_rows[...] = jnp.dot(picked, stale_ref[...], preferred_element_type=jnp.float32).astype(jnp.bfloat16)
    load_x.wait()
    load_w.wait()
    load_cos.wait()
    load_sin.wait()
    load_owner.wait()
    load_chosen.wait()

    @pl.when(c == 0)
    def _():
        pl.semaphore_wait(barrier, 12)

    @pl.when(c == 1)
    def _():
        pl.semaphore_wait(barrier, 22)

    started = []
    for k, (dy, dl) in enumerate(line[1:]):
        send(
            started, x_ref.at[at_y(dy)], xpiece(t, y, c), xy_send.at[k + 1], xy_recv.at[k + 1, c],
            dev(z, at_y(dy), 1, other(dl) * 4 + x),
        )
    for k in (2, 3, 0, 1):
        dz, dy = sides[k]
        send(
            started, own_rows, kept(z, y, c), seed_send.at[k], seed_recv.at[k, c], dev(at_z(dz), at_y(dy), 0, t)
        )
    for k in range(2):
        send(
            started, w_ref, wpiece(y, c), w_send.at[k], w_recv.at[k, c], dev(z, at_y(sides[k][1]), 1, t)
        )

    @pl.when(c == 0)
    def _():
        pending = []
        mate = dev(z, y, 1, t)
        send(pending, x_ref.at[y], xpiece(t, y, 0), xy_send.at[0], xy_recv.at[0, 0], mate)
        send(pending, w_ref, wpiece(y, 0), w_send.at[2], w_recv.at[2, 0], mate)
        own_copy = pltpu.make_async_copy(own_rows, kept(z, y, 0), local_sem.at[len(loads)])
        own_copy.start()

        def ring(zz, yy, s, d, way):
            step = 1 if way == 0 else -1
            send(
                pending, chunk(zz, yy), chunk(zz, yy), sz_send.at[way, s, d], sz_recv.at[way, s, d],
                dev(at_z(step), y, 0, t),
            )

        def share(zz, yy, rel, d):
            send(pending, chunk(zz, yy), chunk(zz, yy), ss_send.at[rel, d], ss_recv.at[rel, d], mate)

        def inject(d):
            for way in range(2):
                ring(z, at_y(d), 1, d, way)
            share(z, at_y(d), 0, d)

        def last_way(d):
            return 0 if d == 1 else 1

        def hop(s, d):
            for way in range(2):
                if s == 4 and way != last_way(d):
                    continue
                rel = (-s if way == 0 else s) % NZ
                zz, yy = at_z(rel), at_y(d)
                if s == 1 and d == 0:
                    for cc in range(2):
                        arrived(kept(zz, yy, cc), seed_recv.at[2 + way, cc], seed_send.at[2 + way])
                else:
                    arrived(chunk(zz, yy), sz_recv.at[way, s, d], sz_send.at[way, s, d])
                if s < (2 if d == 2 else 3) or (s == 3 and way == last_way(d)):
                    ring(zz, yy, s + 1, d, way)
                if s >= 3 and d:
                    k = 0 if d == 3 else 1
                    send(
                        pending, kept(zz, yy, k), kept(zz, yy, k), yf_send.at[rel, k], yf_recv.at[rel, k],
                        dev(z, at_y(sides[k][1]), 0, t),
                    )
                share(zz, yy, rel, d)

        hop(1, 0)
        for k in range(2):
            yy = at_y(-sides[k][1])
            for cc in range(2):
                arrived(kept(z, yy, cc), seed_recv.at[k, cc], seed_send.at[k])
            send(
                pending, kept(z, yy, k), kept(z, yy, k), yr_send.at[k], yr_recv.at[k],
                dev(z, at_y(sides[k][1]), 0, t),
            )
            inject(3 if k == 0 else 1)
        hop(2, 0)
        hop(1, 3)
        hop(1, 1)
        for k in range(2):
            arrived(kept(z, at_y(2), k), yr_recv.at[k], yr_send.at[k])
        inject(2)
        own_copy.wait()
        arrived(kept(z, y, 1), ss_recv.at[0, 0], ss_send.at[0, 0])
        send(pending, kept(z, y, 0), kept(z, y, 0), ss_send.at[0, 0], ss_recv.at[0, 0], mate)
        for s, d in (
            (3, 0), (2, 3), (2, 1), (1, 2), (4, 0), (3, 3), (3, 1), (2, 2), (4, 3), (4, 1),
        ):
            hop(s, d)
        for rel in (5, 3, 4):
            for k in range(2):
                arrived(kept(at_z(rel), at_y(2), k), yf_recv.at[rel, k], yf_send.at[rel, k])
            share(at_z(rel), at_y(2), rel, 2)
        for d in range(NY):
            arrived(column(at_y(d)), fs_recv.at[d], fs_send.at[d])
        for copy in pending:
            copy.wait_send()

    @pl.when(c == 1)
    def _():
        pending = []
        mate = dev(z, y, 0, t)
        own_x = pltpu.make_async_copy(x_ref.at[y], xpiece(t, y, 1), local_sem.at[len(loads)])
        own_w = pltpu.make_async_copy(w_ref, wpiece(y, 1), local_sem.at[len(loads) + 1])
        own_copy = pltpu.make_async_copy(own_rows, kept(z, y, 1), local_sem.at[len(loads) + 2])
        own_x.start()
        own_w.start()
        own_copy.start()
        send(pending, own_rows, kept(z, y, 1), ss_send.at[0, 0], ss_recv.at[0, 0], mate)
        own_x.wait()
        arrived(xpiece(t, y, 0), xy_recv.at[0, 0], xy_send.at[0])
        for k, (dy, dl) in enumerate(line[1:]):
            for cc in range(2):
                arrived(xpiece(other(dl) * 4 + x, at_y(-dy), cc), xy_recv.at[k + 1, cc], xy_send.at[k + 1])
        xall = xbuf.reshape(2, 4, 2, SEL, 8 * HD)
        for k in range(1, NX):
            send(
                pending, xall.at[:, x], xall.at[:, x], xx_send.at[k], xx_recv.at[k], (r, ylo * 4 + at_x(k))
            )
        for k in range(2):
            yy = at_y(-sides[k][1])
            for cc in range(2):
                arrived(wpiece(yy, cc), w_recv.at[k, cc], w_send.at[k])
            send(
                pending, wpiece(yy, k), wpiece(yy, k), wr_send.at[k], wr_recv.at[k],
                dev(z, at_y(sides[k][1]), 1, t),
            )
        for cc in range(2):
            for k in range(SEL):
                position = sel_ref[k, r - 1 + cc]
                trig_c[cc, pl.ds(k, 1), :] = cos_ref[pl.ds(position, 1), :]
                trig_s[cc, pl.ds(k, 1), :] = sin_ref[pl.ds(position, 1), :]
        own_w.wait()
        arrived(wpiece(y, 0), w_recv.at[2, 0], w_send.at[2])
        for k in range(1, NX):
            arrived(xall.at[:, at_x(-k)], xx_recv.at[k], xx_send.at[k])
        for k in range(2):
            arrived(wpiece(at_y(2), k), wr_recv.at[k], wr_send.at[k])
        part = jnp.dot(
            xbuf[...].reshape(NZ * 2 * SEL, 8 * HD),
            wbuf[...].reshape(8 * HD, KV),
            preferred_element_type=jnp.float32,
        )
        zsum[...] = part.reshape(NZ, 2, SEL, KV)
        for k in range(1, NZ):
            send(
                pending, zsum.at[at_z(k)], zrecv.at[k], rz_send.at[k], rz_recv.at[k], dev(at_z(k), y, 1, t)
            )
        total = zsum[z]
        for k in range(1, NZ):
            arrived(zrecv.at[k], rz_recv.at[k], rz_send.at[k])
            total = total + zrecv[k]
        fresh = total.astype(jnp.bfloat16).astype(jnp.float32)
        for cc in range(2):
            keys = fresh[cc, :, :HD]
            keys = keys * trig_c[cc] + pltpu.roll(keys, HD // 2, 1) * trig_s[cc]
            own_fresh[cc, :, :HD] = keys.astype(jnp.bfloat16)
            own_fresh[cc, :, HD:] = fresh[cc, :, HD:].astype(jnp.bfloat16)
        for k in range(1, NZ):
            send(pending, own_fresh, piece(z, y), fz_send.at[k], fz_recv.at[k], dev(at_z(k), y, 1, t))
        keep_fresh = pltpu.make_async_copy(own_fresh, piece(z, y), local_sem.at[len(loads) + 3])
        keep_fresh.start()
        keep_fresh.wait()
        def share(d):
            send(pending, column(at_y(d)), column(at_y(d)), fs_send.at[d], fs_recv.at[d], mate)

        near_first = (0, 1, 7, 2, 6, 3, 5, 4)
        for rel in near_first:
            here = piece(at_z(-rel), y)
            if rel:
                arrived(here, fz_recv.at[rel], fz_send.at[rel])
            for k in range(2):
                send(
                    pending, here, here, fy_send.at[rel, k], fy_recv.at[rel, k],
                    dev(z, at_y(sides[k][1]), 1, t),
                )
        share(0)
        for rel in near_first:
            zz = at_z(-rel)
            for k in range(2):
                yy = at_y(-sides[k][1])
                arrived(piece(zz, yy), fy_recv.at[rel, k], fy_send.at[rel, k])
                send(
                    pending, half_piece(zz, yy, k), half_piece(zz, yy, k), fr_send.at[rel, k], fr_recv.at[rel, k],
                    dev(z, at_y(sides[k][1]), 1, t),
                )
        share(3)
        share(1)
        for rel in near_first:
            for k in range(2):
                arrived(half_piece(at_z(-rel), at_y(2), k), fr_recv.at[rel, k], fr_send.at[rel, k])
        share(2)
        own_copy.wait()
        arrived(kept(z, y, 0), ss_recv.at[0, 0], ss_send.at[0, 0])
        for rel in range(NZ):
            for d in range(NY):
                if rel or d:
                    arrived(chunk(at_z(rel), at_y(d)), ss_recv.at[rel, d], ss_send.at[rel, d])
        for copy in pending:
            copy.wait_send()

    for copy in started:
        copy.wait_send()

    kbufs, vbufs, sbufs, pbufs = (kbuf0, kbuf1), (vbuf0, vbuf1), (sbuf0, sbuf1), (pbuf0, pbuf1)
    steps = q_ref.shape[0] // PAIR

    def result_copy(step):
        rows = pl.ds(step * PAIR, PAIR)
        return pltpu.make_async_copy(out_ref.at[rows], out_hbm.at[rows], out_sem.at[step])

    col = lax.broadcasted_iota(jnp.int32, (CHUNK, 128), 1)
    token = lax.rem(lax.broadcasted_iota(jnp.int32, (CHUNK, 128), 0), QLEN)
    tail = jnp.where(col <= token, jnp.float32(0.0), jnp.float32(NEG))
    for i in range(PAIR):
        kbufs[i][LAST + QLEN :, :] = jnp.zeros((128 - QLEN, HD), jnp.bfloat16)
        vbufs[i][LAST + QLEN :, :] = jnp.zeros((128 - QLEN, HD), jnp.bfloat16)
    for copy in later:
        copy.wait()

    def turn(block, j):
        wide = block.astype(jnp.float32)
        wide = wide * cos_ref[PLEN + j : PLEN + j + 1, :] + pltpu.roll(wide, HD // 2, 1) * sin_ref[PLEN + j : PLEN + j + 1, :]
        return wide.astype(jnp.bfloat16)

    def pair(step, carry):
        for i in range(PAIR):
            kbuf, vbuf = kbufs[i], vbufs[i]
            request = step * PAIR + i
            for j in range(SLOTS):
                o = owner_ref[chosen_ref[j, request]]
                block = pas[o // 8, lax.rem(o, 8) // 2, lax.rem(o, 2)]
                keys = block[:, :HD]
                kbuf[j * PLEN : (j + 1) * PLEN, :] = turn(keys, j) if j else keys
                vbuf[j * PLEN : (j + 1) * PLEN, :] = block[:, HD:]
            own = own_ref[request]
            kbuf[LAST : LAST + QLEN, :] = own[:, :HD]
            vbuf[LAST : LAST + QLEN, :] = own[:, HD:]
        for i in range(PAIR):
            query = q_ref[step * PAIR + i]
            query = jnp.concatenate([query[:, h * HD : (h + 1) * HD] for h in range(GROUP)], 0)
            sbufs[i][...] = lax.dot_general(
                query, kbufs[i][...], (((1,), (1,)), ((), ())), preferred_element_type=jnp.float32
            )
        for i in range(PAIR):
            sbuf, pbuf = sbufs[i], pbufs[i]
            for first in range(0, GROUP * QLEN, CHUNK):
                rows = slice(first, first + CHUNK)
                raw = jnp.concatenate([sbuf[rows, :LAST], sbuf[rows, LAST:] + tail], 1)
                expo = jnp.exp2((raw - jnp.max(raw, 1, keepdims=True)) * SCALE)
                pbuf[rows, :] = (expo * (1.0 / jnp.sum(expo, 1, keepdims=True))).astype(jnp.bfloat16)
            result = jnp.dot(pbuf[...], vbufs[i][...], preferred_element_type=jnp.float32).astype(jnp.bfloat16)
            for h in range(GROUP):
                out_ref[step * PAIR + i, :, h * HD : (h + 1) * HD] = result[h * QLEN : (h + 1) * QLEN]
        result_copy(step).start()
        return carry

    lax.fori_loop(0, steps, pair, 0)
    for step in range(steps):
        result_copy(step).wait()


def local(stale, fresh_input, kv_weight, sel_index, owner, retrieval, queries, question_kv):
    cosine, sine = trig_tables()
    any_spec = pl.BlockSpec(memory_space=pl.ANY)
    dma = pltpu.SemaphoreType.DMA
    rows = GROUP * QLEN
    return pl.pallas_call(
        kernel,
        out_shape=jax.ShapeDtypeStruct(queries.shape, jnp.bfloat16),
        in_specs=[any_spec] * 10,
        out_specs=any_spec,
        scratch_shapes=[
            pltpu.VMEM((NZ, NY, 2, PLEN, KV), jnp.bfloat16),
            pltpu.VMEM((KEYS, HD), jnp.bfloat16),
            pltpu.VMEM((KEYS, HD), jnp.bfloat16),
            pltpu.VMEM((KEYS, HD), jnp.bfloat16),
            pltpu.VMEM((KEYS, HD), jnp.bfloat16),
            pltpu.VMEM((rows, KEYS), jnp.float32),
            pltpu.VMEM((rows, KEYS), jnp.bfloat16),
            pltpu.VMEM((rows, KEYS), jnp.float32),
            pltpu.VMEM((rows, KEYS), jnp.bfloat16),
            pltpu.VMEM(queries.shape, jnp.bfloat16),
            pltpu.VMEM(question_kv.shape, jnp.bfloat16),
            pltpu.VMEM(queries.shape, jnp.bfloat16),
            pltpu.SMEM((64,), jnp.int32),
            pltpu.SMEM((SLOTS, 8), jnp.int32),
            pltpu.VMEM((PLEN, KV), jnp.bfloat16),
            pltpu.VMEM((KEPT, KV), jnp.bfloat16),
            pltpu.VMEM((2, SEL, KV), jnp.bfloat16),
            pltpu.VMEM((8, 2, SEL, 8 * HD), jnp.bfloat16),
            pltpu.VMEM((NY, 2, HD, KV), jnp.bfloat16),
            pltpu.VMEM((NZ, 2, SEL, KV), jnp.float32),
            pltpu.VMEM((NZ, 2, SEL, KV), jnp.float32),
            pltpu.VMEM((2, SEL, HD), jnp.float32),
            pltpu.VMEM((2, SEL, HD), jnp.float32),
            pltpu.VMEM((NY, 2, SEL, HD), jnp.bfloat16),
            pltpu.VMEM((HD, KV), jnp.bfloat16),
            pltpu.VMEM(cosine.shape, jnp.float32),
            pltpu.VMEM(sine.shape, jnp.float32),
            pltpu.SMEM((SEL, 64), jnp.int32),
            dma((12,)),
            dma((8,)), dma((8, 2)),
            dma((NX,)), dma((NX,)),
            dma((3,)), dma((3, 2)),
            dma((2,)), dma((2,)),
            dma((4,)), dma((4, 2)),
            dma((2,)), dma((2,)),
            dma((NZ, 2)), dma((NZ, 2)),
            dma((2, 5, NY)), dma((2, 5, NY)),
            dma((NZ, NY)), dma((NZ, NY)),
            dma((NZ,)), dma((NZ,)),
            dma((NZ,)), dma((NZ,)),
            dma((NZ, 2)), dma((NZ, 2)),
            dma((NZ, 2)), dma((NZ, 2)),
            dma((NY,)), dma((NY,)),
            dma((2,)), dma((4,)),
        ],
        compiler_params=pltpu.CompilerParams(
            collective_id=0, has_side_effects=True, vmem_limit_bytes=62 * 1024 * 1024
        ),
    )(
        stale,
        fresh_input.reshape(NY, 2, SEL, HD),
        kv_weight,
        sel_index.T,
        jnp.asarray(cosine),
        jnp.asarray(sine),
        owner,
        retrieval.T,
        queries,
        question_kv,
    )


def solution(mesh):
    return jax.shard_map(
        local,
        mesh=mesh,
        in_specs=(
            P("req", None, "tp"),
            P("tp", None, "req"),
            P("req", None),
            P(),
            P(),
            P("req", None),
            P("req", None, "tp"),
            P("req", None, "tp"),
        ),
        out_specs=P("req", None, "tp"),
        check_vma=False,
    )
```

```python
import functools
import math

import jax
import jax.numpy as jnp
import numpy as np
from jax import lax
from jax.experimental import pallas as pl
from jax.experimental.pallas import tpu as pltpu
from jax.sharding import PartitionSpec as P

MESH = pl.DeviceIdType.MESH
HD = 128
NZ, NY, NX = 8, 4, 4
PLEN, QLEN, SEL, SLOTS = 128, 32, 16, 4
GROUP = 8
KV = 2 * HD
LAST = SLOTS * PLEN
KEYS = LAST + 128
KEPT = PLEN - SEL
CHUNK = 64
SCALE = math.log2(math.e) / math.sqrt(HD)
NEG = -1e30
THETA = 500000.0
PAIR = 2


def trig_tables():
    positions = np.concatenate([np.arange(PLEN), np.arange(8) * PLEN]).astype(np.float32)
    freqs = (THETA ** (-(np.arange(HD // 2, dtype=np.float64) * 2.0 / HD))).astype(np.float32)
    angle = (positions[:, None] * freqs).astype(np.float32).astype(np.float64)
    cosine, sine = np.cos(angle), np.sin(angle)
    return (
        np.concatenate([cosine, cosine], -1).astype(np.float32),
        np.concatenate([-sine, sine], -1).astype(np.float32),
    )


def kernel(
    stale_hbm, x_hbm, w_hbm, sel_hbm, cos_hbm, sin_hbm, owner_hbm, chosen_hbm, q_hbm, own_hbm,
    out_hbm,
    pas, kbuf0, vbuf0, kbuf1, vbuf1, sbuf0, pbuf0, sbuf1, pbuf1, q_ref, own_ref, out_ref, owner_ref, chosen_ref,
    stale_ref, own_rows, own_fresh, xbuf, wbuf, zsum, zrecv, trig_c, trig_s, x_ref, w_ref, cos_ref, sin_ref, sel_ref,
    local_sem, xy_send, xy_recv, xx_send, xx_recv, w_send, w_recv, wr_send, wr_recv,
    seed_send, seed_recv, yr_send, yr_recv, yf_send, yf_recv, sz_send, sz_recv, ss_send, ss_recv,
    rz_send, rz_recv, fz_send, fz_recv, fy_send, fy_recv, fr_send, fr_recv, fs_send, fs_recv, q_sem, out_sem,
):
    r, t = lax.axis_index("req"), lax.axis_index("tp")
    z, y, c = r // 8, lax.rem(r, 8) // 2, lax.rem(r, 2)
    ylo, x = t // 4, lax.rem(t, 4)

    def dev(zz, yy, cc, tt):
        return (zz * 8 + yy * 2 + cc, tt)

    def at_z(k):
        return lax.rem(z + k + 2 * NZ, NZ)

    def at_y(k):
        return lax.rem(y + k + 2 * NY, NY)

    def at_x(k):
        return lax.rem(x + k + 2 * NX, NX)

    def other(dl):
        return lax.rem(ylo + dl, 2)

    def remote(src, dst, send_sem, recv_sem, device):
        return pltpu.make_async_remote_copy(
            src_ref=src, dst_ref=dst, send_sem=send_sem, recv_sem=recv_sem,
            device_id=device, device_id_type=MESH,
        )

    def arrived(dst, recv_sem, send_sem):
        remote(dst, dst, send_sem, recv_sem, dev(z, y, 1 - c, t)).wait_recv()

    def send(pending, *args):
        copy = remote(*args)
        copy.start()
        pending.append(copy)

    line = [(dy, dl) for dy in range(NY) for dl in range(2)]
    sides = [(0, 1), (0, -1), (1, 0), (-1, 0)]

    barrier = pltpu.get_barrier_semaphore()

    def greet(device):
        pl.semaphore_signal(barrier, inc=1, device_id=device, device_id_type=MESH)

    @pl.when(c == 0)
    def _():
        for dz, dy in sides:
            for cc in range(2):
                greet(dev(at_z(dz), at_y(dy), cc, t))
        greet(dev(z, y, 1, t))

    @pl.when(c == 1)
    def _():
        for dy, dl in line[1:]:
            for cc in range(2):
                greet(dev(z, at_y(dy), cc, other(dl) * 4 + x))
        greet(dev(z, y, 0, t))
        for k in range(1, NX):
            greet((r, ylo * 4 + at_x(k)))
        for k in range(1, NZ):
            greet(dev(at_z(k), y, 1, t))

    columns = pl.ds(pl.multiple_of(t * KV, KV), KV)

    def chunk(zz, yy):
        return pas.at[zz, yy, :, pl.ds(0, KEPT)]

    def kept(zz, yy, cc):
        return pas.at[zz, yy, cc, pl.ds(0, KEPT)]

    def column(yy):
        return pas.at[:, yy, :, pl.ds(KEPT, SEL)]

    def piece(zz, yy):
        return pas.at[zz, yy, :, pl.ds(KEPT, SEL)]

    def half_piece(zz, yy, cc):
        return pas.at[zz, yy, cc, pl.ds(KEPT, SEL)]

    def xpiece(ts, ys, cs):
        return xbuf.at[ts, :, :, pl.ds(pl.multiple_of((ys * 2 + cs) * HD, HD), HD)]

    def wpiece(ys, cs):
        return wbuf.at[ys, cs]

    loads = []

    def load(source, target):
        copy = pltpu.make_async_copy(source, target, local_sem.at[len(loads)])
        copy.start()
        loads.append(copy)
        return copy

    load_sel = load(sel_hbm, sel_ref)
    load_stale = load(stale_hbm.at[0], stale_ref)
    load_x = load(x_hbm, x_ref)
    load_w = load(w_hbm.at[:, columns], w_ref)
    load_cos = load(cos_hbm, cos_ref)
    load_sin = load(sin_hbm, sin_ref)
    load_owner = load(owner_hbm, owner_ref)
    load_chosen = load(chosen_hbm, chosen_ref)
    later = []
    for k, (source, target) in enumerate(((q_hbm, q_ref), (own_hbm, own_ref))):
        later.append(pltpu.make_async_copy(source, target, q_sem.at[k]))
        later[-1].start()

    load_x.wait()

    @pl.when(c == 0)
    def _():
        pl.semaphore_wait(barrier, 12)

    @pl.when(c == 1)
    def _():
        pl.semaphore_wait(barrier, 22)

    started = []
    for k, (dy, dl) in enumerate(line[1:]):
        send(
            started, x_ref.at[at_y(dy)], xpiece(t, y, c), xy_send.at[k + 1], xy_recv.at[k + 1, c],
            dev(z, at_y(dy), 1, other(dl) * 4 + x),
        )
    load_sel.wait()
    lane = lax.broadcasted_iota(jnp.int32, (8, PLEN), 1)
    hit = lane == sel_ref[0, r]
    for k in range(1, SEL):
        hit = hit | (lane == sel_ref[k, r])
    keep = jnp.where(hit, jnp.float32(0.0), jnp.float32(1.0))
    before = lax.broadcasted_iota(jnp.int32, (PLEN, PLEN), 0) < lax.broadcasted_iota(jnp.int32, (PLEN, PLEN), 1)
    rank = jnp.dot(
        keep.astype(jnp.bfloat16),
        jnp.where(before, jnp.float32(1.0), jnp.float32(0.0)).astype(jnp.bfloat16),
        preferred_element_type=jnp.float32,
    )
    order = lax.broadcasted_iota(jnp.int32, (KEPT, PLEN), 0).astype(jnp.float32)
    picked = jnp.where(order == rank[0:1], keep[0:1], jnp.float32(0.0)).astype(jnp.bfloat16)
    load_stale.wait()
    own_rows[...] = jnp.dot(picked, stale_ref[...], preferred_element_type=jnp.float32).astype(jnp.bfloat16)
    for k in (2, 3, 0, 1):
        dz, dy = sides[k]
        send(
            started, own_rows, kept(z, y, c), seed_send.at[k], seed_recv.at[k, c], dev(at_z(dz), at_y(dy), 0, t)
        )
    load_w.wait()
    for k in range(2):
        send(
            started, w_ref, wpiece(y, c), w_send.at[k], w_recv.at[k, c], dev(z, at_y(sides[k][1]), 1, t)
        )

    for copy in (load_cos, load_sin, load_owner, load_chosen):
        copy.wait()

    @pl.when(c == 0)
    def _():
        pending = []
        mate = dev(z, y, 1, t)
        send(pending, x_ref.at[y], xpiece(t, y, 0), xy_send.at[0], xy_recv.at[0, 0], mate)
        send(pending, w_ref, wpiece(y, 0), w_send.at[2], w_recv.at[2, 0], mate)
        own_copy = pltpu.make_async_copy(own_rows, kept(z, y, 0), local_sem.at[len(loads)])
        own_copy.start()

        def ring(zz, yy, s, d, way, cc):
            step = 1 if way == 0 else -1
            send(
                pending, kept(zz, yy, cc), kept(zz, yy, cc), sz_send.at[way, s, d, cc], sz_recv.at[way, s, d, cc],
                dev(at_z(step), y, 0, t),
            )

        def share(zz, yy, rel, d):
            send(pending, chunk(zz, yy), chunk(zz, yy), ss_send.at[rel, d], ss_recv.at[rel, d], mate)

        def inject(d, cc):
            for way in range(2):
                ring(z, at_y(d), 1, d, way, cc)

        def last_way(d):
            return 0 if d == 1 else 1

        def hop(s, d):
            ways = [way for way in range(2) if s < 4 or way == last_way(d)]
            where = [((-s if way == 0 else s) % NZ, way) for way in ways]
            for cc in range(2):
                for rel, way in where:
                    block = kept(at_z(rel), at_y(d), cc)
                    if s == 1 and d == 0:
                        arrived(block, seed_recv.at[2 + way, cc], seed_send.at[2 + way])
                    else:
                        arrived(block, sz_recv.at[way, s, d, cc], sz_send.at[way, s, d, cc])
                    if s < (2 if d == 2 else 3) or (s == 3 and way == last_way(d)):
                        ring(at_z(rel), at_y(d), s + 1, d, way, cc)
                    if s >= 3 and d and cc == (0 if d == 3 else 1):
                        send(
                            pending, block, block, yf_send.at[rel, cc], yf_recv.at[rel, cc],
                            dev(z, at_y(sides[cc][1]), 0, t),
                        )
            for rel, way in where:
                share(at_z(rel), at_y(d), rel, d)

        hop(1, 0)
        for k in range(2):
            yy = at_y(-sides[k][1])
            d = 3 if k == 0 else 1
            for cc in range(2):
                arrived(kept(z, yy, cc), seed_recv.at[k, cc], seed_send.at[k])
                if cc == k:
                    send(
                        pending, kept(z, yy, k), kept(z, yy, k), yr_send.at[k], yr_recv.at[k],
                        dev(z, at_y(sides[k][1]), 0, t),
                    )
                inject(d, cc)
            share(z, yy, 0, d)
        hop(2, 0)
        hop(1, 3)
        hop(1, 1)
        for k in range(2):
            arrived(kept(z, at_y(2), k), yr_recv.at[k], yr_send.at[k])
            inject(2, k)
        share(z, at_y(2), 0, 2)
        own_copy.wait()
        arrived(kept(z, y, 1), ss_recv.at[0, 0], ss_send.at[0, 0])
        send(pending, kept(z, y, 0), kept(z, y, 0), ss_send.at[0, 0], ss_recv.at[0, 0], mate)
        for s, d in (
            (3, 0), (2, 3), (2, 1), (1, 2), (4, 0), (3, 3), (3, 1), (2, 2), (4, 3), (4, 1),
        ):
            hop(s, d)
        for rel in (5, 3, 4):
            for k in range(2):
                arrived(kept(at_z(rel), at_y(2), k), yf_recv.at[rel, k], yf_send.at[rel, k])
            share(at_z(rel), at_y(2), rel, 2)
        for d in range(NY):
            arrived(column(at_y(d)), fs_recv.at[d], fs_send.at[d])
        for copy in pending:
            copy.wait_send()

    @pl.when(c == 1)
    def _():
        pending = []
        mate = dev(z, y, 0, t)
        own_x = pltpu.make_async_copy(x_ref.at[y], xpiece(t, y, 1), local_sem.at[len(loads)])
        own_w = pltpu.make_async_copy(w_ref, wpiece(y, 1), local_sem.at[len(loads) + 1])
        own_copy = pltpu.make_async_copy(own_rows, kept(z, y, 1), local_sem.at[len(loads) + 2])
        own_x.start()
        own_w.start()
        own_copy.start()
        send(pending, own_rows, kept(z, y, 1), ss_send.at[0, 0], ss_recv.at[0, 0], mate)
        own_x.wait()
        arrived(xpiece(t, y, 0), xy_recv.at[0, 0], xy_send.at[0])
        for k, (dy, dl) in enumerate(line[1:]):
            for cc in range(2):
                arrived(xpiece(other(dl) * 4 + x, at_y(-dy), cc), xy_recv.at[k + 1, cc], xy_send.at[k + 1])
        xall = xbuf.reshape(2, 4, 2, SEL, 8 * HD)
        for k in range(1, NX):
            send(
                pending, xall.at[:, x], xall.at[:, x], xx_send.at[k], xx_recv.at[k], (r, ylo * 4 + at_x(k))
            )
        for k in range(2):
            yy = at_y(-sides[k][1])
            for cc in range(2):
                arrived(wpiece(yy, cc), w_recv.at[k, cc], w_send.at[k])
            send(
                pending, wpiece(yy, k), wpiece(yy, k), wr_send.at[k], wr_recv.at[k],
                dev(z, at_y(sides[k][1]), 1, t),
            )
        for cc in range(2):
            for k in range(SEL):
                position = sel_ref[k, r - 1 + cc]
                trig_c[cc, pl.ds(k, 1), :] = cos_ref[pl.ds(position, 1), :]
                trig_s[cc, pl.ds(k, 1), :] = sin_ref[pl.ds(position, 1), :]
        own_w.wait()
        arrived(wpiece(y, 0), w_recv.at[2, 0], w_send.at[2])
        for k in range(1, NX):
            arrived(xall.at[:, at_x(-k)], xx_recv.at[k], xx_send.at[k])
        for k in range(2):
            arrived(wpiece(at_y(2), k), wr_recv.at[k], wr_send.at[k])
        part = jnp.dot(
            xbuf[...].reshape(NZ * 2 * SEL, 8 * HD),
            wbuf[...].reshape(8 * HD, KV),
            preferred_element_type=jnp.float32,
        )
        zsum[...] = part.reshape(NZ, 2, SEL, KV)
        for k in (4, 3, 5, 2, 6, 1, 7):
            send(
                pending, zsum.at[at_z(k)], zrecv.at[k], rz_send.at[k], rz_recv.at[k], dev(at_z(k), y, 1, t)
            )
        total = zsum[z]
        for k in range(1, NZ):
            arrived(zrecv.at[k], rz_recv.at[k], rz_send.at[k])
            total = total + zrecv[k]
        fresh = total.astype(jnp.bfloat16).astype(jnp.float32)
        for cc in range(2):
            keys = fresh[cc, :, :HD]
            keys = keys * trig_c[cc] + pltpu.roll(keys, HD // 2, 1) * trig_s[cc]
            own_fresh[cc, :, :HD] = keys.astype(jnp.bfloat16)
            own_fresh[cc, :, HD:] = fresh[cc, :, HD:].astype(jnp.bfloat16)
        for k in (1, 7, 2, 6, 3, 5, 4):
            send(pending, own_fresh, piece(z, y), fz_send.at[k], fz_recv.at[k], dev(at_z(k), y, 1, t))
        keep_fresh = pltpu.make_async_copy(own_fresh, piece(z, y), local_sem.at[len(loads) + 3])
        keep_fresh.start()
        keep_fresh.wait()
        def share(d):
            send(pending, column(at_y(d)), column(at_y(d)), fs_send.at[d], fs_recv.at[d], mate)

        near_first = (0, 1, 7, 2, 6, 3, 5, 4)
        for rel in near_first:
            here = piece(at_z(-rel), y)
            if rel:
                arrived(here, fz_recv.at[rel], fz_send.at[rel])
            for k in range(2):
                send(
                    pending, here, here, fy_send.at[rel, k], fy_recv.at[rel, k],
                    dev(z, at_y(sides[k][1]), 1, t),
                )
        share(0)
        for rel in near_first:
            zz = at_z(-rel)
            for k in range(2):
                yy = at_y(-sides[k][1])
                arrived(piece(zz, yy), fy_recv.at[rel, k], fy_send.at[rel, k])
                send(
                    pending, half_piece(zz, yy, k), half_piece(zz, yy, k), fr_send.at[rel, k], fr_recv.at[rel, k],
                    dev(z, at_y(sides[k][1]), 1, t),
                )
        share(3)
        share(1)
        for rel in near_first:
            for k in range(2):
                arrived(half_piece(at_z(-rel), at_y(2), k), fr_recv.at[rel, k], fr_send.at[rel, k])
        share(2)
        own_copy.wait()
        arrived(kept(z, y, 0), ss_recv.at[0, 0], ss_send.at[0, 0])
        for rel in range(NZ):
            for d in range(NY):
                if rel or d:
                    arrived(chunk(at_z(rel), at_y(d)), ss_recv.at[rel, d], ss_send.at[rel, d])
        for copy in pending:
            copy.wait_send()

    for copy in started:
        copy.wait_send()

    kbufs, vbufs, sbufs, pbufs = (kbuf0, kbuf1), (vbuf0, vbuf1), (sbuf0, sbuf1), (pbuf0, pbuf1)
    steps = q_ref.shape[0] // PAIR

    def result_copy(step):
        rows = pl.ds(step * PAIR, PAIR)
        return pltpu.make_async_copy(out_ref.at[rows], out_hbm.at[rows], out_sem.at[step])

    col = lax.broadcasted_iota(jnp.int32, (CHUNK, 128), 1)
    token = lax.rem(lax.broadcasted_iota(jnp.int32, (CHUNK, 128), 0), QLEN)
    tail = jnp.where(col <= token, jnp.float32(0.0), jnp.float32(NEG))
    for i in range(PAIR):
        kbufs[i][LAST + QLEN :, :] = jnp.zeros((128 - QLEN, HD), jnp.bfloat16)
        vbufs[i][LAST + QLEN :, :] = jnp.zeros((128 - QLEN, HD), jnp.bfloat16)
    for copy in later:
        copy.wait()

    def turn(block, j):
        wide = block.astype(jnp.float32)
        wide = wide * cos_ref[PLEN + j : PLEN + j + 1, :] + pltpu.roll(wide, HD // 2, 1) * sin_ref[PLEN + j : PLEN + j + 1, :]
        return wide.astype(jnp.bfloat16)

    def pair(step, carry):
        for i in range(PAIR):
            kbuf, vbuf = kbufs[i], vbufs[i]
            request = step * PAIR + i
            for j in range(SLOTS):
                o = owner_ref[chosen_ref[j, request]]
                block = pas[o // 8, lax.rem(o, 8) // 2, lax.rem(o, 2)]
                keys = block[:, :HD]
                kbuf[j * PLEN : (j + 1) * PLEN, :] = turn(keys, j) if j else keys
                vbuf[j * PLEN : (j + 1) * PLEN, :] = block[:, HD:]
            own = own_ref[request]
            kbuf[LAST : LAST + QLEN, :] = own[:, :HD]
            vbuf[LAST : LAST + QLEN, :] = own[:, HD:]
        for i in range(PAIR):
            query = q_ref[step * PAIR + i]
            query = jnp.concatenate([query[:, h * HD : (h + 1) * HD] for h in range(GROUP)], 0)
            sbufs[i][...] = lax.dot_general(
                query, kbufs[i][...], (((1,), (1,)), ((), ())), preferred_element_type=jnp.float32
            )
        for i in range(PAIR):
            sbuf, pbuf = sbufs[i], pbufs[i]
            for first in range(0, GROUP * QLEN, CHUNK):
                rows = slice(first, first + CHUNK)
                raw = jnp.concatenate([sbuf[rows, :LAST], sbuf[rows, LAST:] + tail], 1)
                expo = jnp.exp2((raw - jnp.max(raw, 1, keepdims=True)) * SCALE)
                pbuf[rows, :] = (expo * (1.0 / jnp.sum(expo, 1, keepdims=True))).astype(jnp.bfloat16)
            result = jnp.dot(pbuf[...], vbufs[i][...], preferred_element_type=jnp.float32).astype(jnp.bfloat16)
            for h in range(GROUP):
                out_ref[step * PAIR + i, :, h * HD : (h + 1) * HD] = result[h * QLEN : (h + 1) * QLEN]
        result_copy(step).start()
        return carry

    lax.fori_loop(0, steps, pair, 0)
    for step in range(steps):
        result_copy(step).wait()


def local(stale, fresh_input, kv_weight, sel_index, owner, retrieval, queries, question_kv):
    cosine, sine = trig_tables()
    any_spec = pl.BlockSpec(memory_space=pl.ANY)
    dma = pltpu.SemaphoreType.DMA
    rows = GROUP * QLEN
    return pl.pallas_call(
        kernel,
        out_shape=jax.ShapeDtypeStruct(queries.shape, jnp.bfloat16),
        in_specs=[any_spec] * 10,
        out_specs=any_spec,
        scratch_shapes=[
            pltpu.VMEM((NZ, NY, 2, PLEN, KV), jnp.bfloat16),
            pltpu.VMEM((KEYS, HD), jnp.bfloat16),
            pltpu.VMEM((KEYS, HD), jnp.bfloat16),
            pltpu.VMEM((KEYS, HD), jnp.bfloat16),
            pltpu.VMEM((KEYS, HD), jnp.bfloat16),
            pltpu.VMEM((rows, KEYS), jnp.float32),
            pltpu.VMEM((rows, KEYS), jnp.bfloat16),
            pltpu.VMEM((rows, KEYS), jnp.float32),
            pltpu.VMEM((rows, KEYS), jnp.bfloat16),
            pltpu.VMEM(queries.shape, jnp.bfloat16),
            pltpu.VMEM(question_kv.shape, jnp.bfloat16),
            pltpu.VMEM(queries.shape, jnp.bfloat16),
            pltpu.SMEM((64,), jnp.int32),
            pltpu.SMEM((SLOTS, 8), jnp.int32),
            pltpu.VMEM((PLEN, KV), jnp.bfloat16),
            pltpu.VMEM((KEPT, KV), jnp.bfloat16),
            pltpu.VMEM((2, SEL, KV), jnp.bfloat16),
            pltpu.VMEM((8, 2, SEL, 8 * HD), jnp.bfloat16),
            pltpu.VMEM((NY, 2, HD, KV), jnp.bfloat16),
            pltpu.VMEM((NZ, 2, SEL, KV), jnp.float32),
            pltpu.VMEM((NZ, 2, SEL, KV), jnp.float32),
            pltpu.VMEM((2, SEL, HD), jnp.float32),
            pltpu.VMEM((2, SEL, HD), jnp.float32),
            pltpu.VMEM((NY, 2, SEL, HD), jnp.bfloat16),
            pltpu.VMEM((HD, KV), jnp.bfloat16),
            pltpu.VMEM(cosine.shape, jnp.float32),
            pltpu.VMEM(sine.shape, jnp.float32),
            pltpu.SMEM((SEL, 64), jnp.int32),
            dma((12,)),
            dma((8,)), dma((8, 2)),
            dma((NX,)), dma((NX,)),
            dma((3,)), dma((3, 2)),
            dma((2,)), dma((2,)),
            dma((4,)), dma((4, 2)),
            dma((2,)), dma((2,)),
            dma((NZ, 2)), dma((NZ, 2)),
            dma((2, 5, NY, 2)), dma((2, 5, NY, 2)),
            dma((NZ, NY)), dma((NZ, NY)),
            dma((NZ,)), dma((NZ,)),
            dma((NZ,)), dma((NZ,)),
            dma((NZ, 2)), dma((NZ, 2)),
            dma((NZ, 2)), dma((NZ, 2)),
            dma((NY,)), dma((NY,)),
            dma((2,)), dma((4,)),
        ],
        compiler_params=pltpu.CompilerParams(
            collective_id=0, has_side_effects=True, vmem_limit_bytes=62 * 1024 * 1024
        ),
    )(
        stale,
        fresh_input.reshape(NY, 2, SEL, HD),
        kv_weight,
        sel_index.T,
        jnp.asarray(cosine),
        jnp.asarray(sine),
        owner,
        retrieval.T,
        queries,
        question_kv,
    )


def solution(mesh):
    return jax.shard_map(
        local,
        mesh=mesh,
        in_specs=(
            P("req", None, "tp"),
            P("tp", None, "req"),
            P("req", None),
            P(),
            P(),
            P("req", None),
            P("req", None, "tp"),
            P("req", None, "tp"),
        ),
        out_specs=P("req", None, "tp"),
        check_vma=False,
    )
```

```python
import functools
import math

import jax
import jax.numpy as jnp
import numpy as np
from jax import lax
from jax.experimental import pallas as pl
from jax.experimental.pallas import tpu as pltpu
from jax.sharding import PartitionSpec as P

MESH = pl.DeviceIdType.MESH
HD = 128
NZ, NY, NX = 8, 4, 4
PLEN, QLEN, SEL, SLOTS = 128, 32, 16, 4
GROUP = 8
KV = 2 * HD
LAST = SLOTS * PLEN
KEYS = LAST + 128
KEPT = PLEN - SEL
CHUNK = 64
SCALE = math.log2(math.e) / math.sqrt(HD)
NEG = -1e30
THETA = 500000.0
PAIR = 2


def trig_tables():
    positions = np.concatenate([np.arange(PLEN), np.arange(8) * PLEN]).astype(np.float32)
    freqs = (THETA ** (-(np.arange(HD // 2, dtype=np.float64) * 2.0 / HD))).astype(np.float32)
    angle = (positions[:, None] * freqs).astype(np.float32).astype(np.float64)
    cosine, sine = np.cos(angle), np.sin(angle)
    return (
        np.concatenate([cosine, cosine], -1).astype(np.float32),
        np.concatenate([-sine, sine], -1).astype(np.float32),
    )


def kernel(
    stale_hbm, x_hbm, w_hbm, sel_hbm, cos_hbm, sin_hbm, owner_hbm, chosen_hbm, q_hbm, own_hbm,
    out_hbm,
    pas, kbuf0, vbuf0, kbuf1, vbuf1, sbuf0, pbuf0, sbuf1, pbuf1, q_ref, own_ref, out_ref, owner_ref, chosen_ref,
    stale_ref, own_rows, own_fresh, xbuf, wbuf, zsum, zrecv, trig_c, trig_s, x_ref, w_ref, cos_ref, sin_ref, sel_ref,
    local_sem, xy_send, xy_recv, xx_send, xx_recv, w_send, w_recv, wr_send, wr_recv,
    seed_send, seed_recv, yr_send, yr_recv, yf_send, yf_recv, sz_send, sz_recv, ss_send, ss_recv,
    rz_send, rz_recv, fz_send, fz_recv, fy_send, fy_recv, fr_send, fr_recv, fs_send, fs_recv, q_sem, out_sem,
):
    r, t = lax.axis_index("req"), lax.axis_index("tp")
    z, y, c = r // 8, lax.rem(r, 8) // 2, lax.rem(r, 2)
    ylo, x = t // 4, lax.rem(t, 4)

    def dev(zz, yy, cc, tt):
        return (zz * 8 + yy * 2 + cc, tt)

    def at_z(k):
        return lax.rem(z + k + 2 * NZ, NZ)

    def at_y(k):
        return lax.rem(y + k + 2 * NY, NY)

    def at_x(k):
        return lax.rem(x + k + 2 * NX, NX)

    def other(dl):
        return lax.rem(ylo + dl, 2)

    def remote(src, dst, send_sem, recv_sem, device):
        return pltpu.make_async_remote_copy(
            src_ref=src, dst_ref=dst, send_sem=send_sem, recv_sem=recv_sem,
            device_id=device, device_id_type=MESH,
        )

    def arrived(dst, recv_sem, send_sem):
        remote(dst, dst, send_sem, recv_sem, dev(z, y, 1 - c, t)).wait_recv()

    def send(pending, *args):
        copy = remote(*args)
        copy.start()
        pending.append(copy)

    line = [(dy, dl) for dy in range(NY) for dl in range(2)]
    sides = [(0, 1), (0, -1), (1, 0), (-1, 0)]

    barrier = pltpu.get_barrier_semaphore()

    def greet(device):
        pl.semaphore_signal(barrier, inc=1, device_id=device, device_id_type=MESH)

    @pl.when(c == 0)
    def _():
        for dz, dy in sides:
            for cc in range(2):
                greet(dev(at_z(dz), at_y(dy), cc, t))
        greet(dev(z, y, 1, t))

    @pl.when(c == 1)
    def _():
        for dy, dl in line[1:]:
            for cc in range(2):
                greet(dev(z, at_y(dy), cc, other(dl) * 4 + x))
        greet(dev(z, y, 0, t))
        for k in range(1, NX):
            greet((r, ylo * 4 + at_x(k)))
        for k in range(1, NZ):
            greet(dev(at_z(k), y, 1, t))

    columns = pl.ds(pl.multiple_of(t * KV, KV), KV)

    def chunk(zz, yy):
        return pas.at[zz, yy, :, pl.ds(0, KEPT)]

    def kept(zz, yy, cc):
        return pas.at[zz, yy, cc, pl.ds(0, KEPT)]

    def column(yy):
        return pas.at[:, yy, :, pl.ds(KEPT, SEL)]

    def piece(zz, yy):
        return pas.at[zz, yy, :, pl.ds(KEPT, SEL)]

    def half_piece(zz, yy, cc):
        return pas.at[zz, yy, cc, pl.ds(KEPT, SEL)]

    def xpiece(ts, ys, cs):
        return xbuf.at[ts, :, :, pl.ds(pl.multiple_of((ys * 2 + cs) * HD, HD), HD)]

    def wpiece(ys, cs):
        return wbuf.at[ys, cs]

    loads = []

    def load(source, target):
        copy = pltpu.make_async_copy(source, target, local_sem.at[len(loads)])
        copy.start()
        loads.append(copy)
        return copy

    load_sel = load(sel_hbm, sel_ref)
    load_stale = load(stale_hbm.at[0], stale_ref)
    load_x = load(x_hbm, x_ref)
    load_w = load(w_hbm.at[:, columns], w_ref)
    load_cos = load(cos_hbm, cos_ref)
    load_sin = load(sin_hbm, sin_ref)
    load_owner = load(owner_hbm, owner_ref)
    load_chosen = load(chosen_hbm, chosen_ref)
    later = []
    for k, (source, target) in enumerate(((q_hbm, q_ref), (own_hbm, own_ref))):
        later.append(pltpu.make_async_copy(source, target, q_sem.at[k]))
        later[-1].start()

    load_x.wait()

    @pl.when(c == 0)
    def _():
        pl.semaphore_wait(barrier, 12)

    @pl.when(c == 1)
    def _():
        pl.semaphore_wait(barrier, 22)

    started = []
    for k, (dy, dl) in enumerate(line[1:]):
        send(
            started, x_ref.at[at_y(dy)], xpiece(t, y, c), xy_send.at[k + 1], xy_recv.at[k + 1, c],
            dev(z, at_y(dy), 1, other(dl) * 4 + x),
        )
    load_w.wait()
    for k in range(2):
        send(
            started, w_ref, wpiece(y, c), w_send.at[k], w_recv.at[k, c], dev(z, at_y(sides[k][1]), 1, t)
        )

    load_sel.wait()
    lane = lax.broadcasted_iota(jnp.int32, (8, PLEN), 1)
    hit = lane == sel_ref[0, r]
    for k in range(1, SEL):
        hit = hit | (lane == sel_ref[k, r])
    keep = jnp.where(hit, jnp.float32(0.0), jnp.float32(1.0))
    before = lax.broadcasted_iota(jnp.int32, (PLEN, PLEN), 0) < lax.broadcasted_iota(jnp.int32, (PLEN, PLEN), 1)
    rank = jnp.dot(
        keep.astype(jnp.bfloat16),
        jnp.where(before, jnp.float32(1.0), jnp.float32(0.0)).astype(jnp.bfloat16),
        preferred_element_type=jnp.float32,
    )
    order = lax.broadcasted_iota(jnp.int32, (KEPT, PLEN), 0).astype(jnp.float32)
    picked = jnp.where(order == rank[0:1], keep[0:1], jnp.float32(0.0)).astype(jnp.bfloat16)
    load_stale.wait()
    own_rows[...] = jnp.dot(picked, stale_ref[...], preferred_element_type=jnp.float32).astype(jnp.bfloat16)
    for k in (2, 3, 0, 1):
        dz, dy = sides[k]
        send(
            started, own_rows, kept(z, y, c), seed_send.at[k], seed_recv.at[k, c], dev(at_z(dz), at_y(dy), 0, t)
        )
    for copy in (load_cos, load_sin, load_owner, load_chosen):
        copy.wait()

    @pl.when(c == 0)
    def _():
        pending = []
        mate = dev(z, y, 1, t)
        send(pending, x_ref.at[y], xpiece(t, y, 0), xy_send.at[0], xy_recv.at[0, 0], mate)
        send(pending, w_ref, wpiece(y, 0), w_send.at[2], w_recv.at[2, 0], mate)
        own_copy = pltpu.make_async_copy(own_rows, kept(z, y, 0), local_sem.at[len(loads)])
        own_copy.start()

        def ring(zz, yy, s, d, way):
            step = 1 if way == 0 else -1
            send(
                pending, chunk(zz, yy), chunk(zz, yy), sz_send.at[way, s, d], sz_recv.at[way, s, d],
                dev(at_z(step), y, 0, t),
            )

        def share(zz, yy, rel, d):
            send(pending, chunk(zz, yy), chunk(zz, yy), ss_send.at[rel, d], ss_recv.at[rel, d], mate)

        def inject(d):
            for way in range(2):
                ring(z, at_y(d), 1, d, way)
            share(z, at_y(d), 0, d)

        def last_way(d):
            return 0 if d == 1 else 1

        def hop(s, d):
            for way in range(2):
                if s == 4 and way != last_way(d):
                    continue
                rel = (-s if way == 0 else s) % NZ
                zz, yy = at_z(rel), at_y(d)
                if s == 1 and d == 0:
                    for cc in range(2):
                        arrived(kept(zz, yy, cc), seed_recv.at[2 + way, cc], seed_send.at[2 + way])
                else:
                    arrived(chunk(zz, yy), sz_recv.at[way, s, d], sz_send.at[way, s, d])
                if s < (2 if d == 2 else 3) or (s == 3 and way == last_way(d)):
                    ring(zz, yy, s + 1, d, way)
                if s >= 3 and d:
                    k = 0 if d == 3 else 1
                    send(
                        pending, kept(zz, yy, k), kept(zz, yy, k), yf_send.at[rel, k], yf_recv.at[rel, k],
                        dev(z, at_y(sides[k][1]), 0, t),
                    )
                share(zz, yy, rel, d)

        hop(1, 0)
        for k in range(2):
            yy = at_y(-sides[k][1])
            for cc in range(2):
                arrived(kept(z, yy, cc), seed_recv.at[k, cc], seed_send.at[k])
            send(
                pending, kept(z, yy, k), kept(z, yy, k), yr_send.at[k], yr_recv.at[k],
                dev(z, at_y(sides[k][1]), 0, t),
            )
            inject(3 if k == 0 else 1)
        hop(2, 0)
        hop(1, 3)
        hop(1, 1)
        for k in range(2):
            arrived(kept(z, at_y(2), k), yr_recv.at[k], yr_send.at[k])
        inject(2)
        own_copy.wait()
        arrived(kept(z, y, 1), ss_recv.at[0, 0], ss_send.at[0, 0])
        send(pending, kept(z, y, 0), kept(z, y, 0), ss_send.at[0, 0], ss_recv.at[0, 0], mate)
        for s, d in (
            (3, 0), (2, 3), (2, 1), (1, 2), (4, 0), (3, 3), (3, 1), (2, 2), (4, 3), (4, 1),
        ):
            hop(s, d)
        for rel in (5, 3, 4):
            for k in range(2):
                arrived(kept(at_z(rel), at_y(2), k), yf_recv.at[rel, k], yf_send.at[rel, k])
            share(at_z(rel), at_y(2), rel, 2)
        for d in range(NY):
            arrived(column(at_y(d)), fs_recv.at[d], fs_send.at[d])
        for copy in pending:
            copy.wait_send()

    @pl.when(c == 1)
    def _():
        pending = []
        mate = dev(z, y, 0, t)
        own_x = pltpu.make_async_copy(x_ref.at[y], xpiece(t, y, 1), local_sem.at[len(loads)])
        own_w = pltpu.make_async_copy(w_ref, wpiece(y, 1), local_sem.at[len(loads) + 1])
        own_copy = pltpu.make_async_copy(own_rows, kept(z, y, 1), local_sem.at[len(loads) + 2])
        own_x.start()
        own_w.start()
        own_copy.start()
        send(pending, own_rows, kept(z, y, 1), ss_send.at[0, 0], ss_recv.at[0, 0], mate)
        own_x.wait()
        arrived(xpiece(t, y, 0), xy_recv.at[0, 0], xy_send.at[0])
        for k, (dy, dl) in enumerate(line[1:]):
            for cc in range(2):
                arrived(xpiece(other(dl) * 4 + x, at_y(-dy), cc), xy_recv.at[k + 1, cc], xy_send.at[k + 1])
        xall = xbuf.reshape(2, 4, 2, SEL, 8 * HD)
        for k in range(1, NX):
            send(
                pending, xall.at[:, x], xall.at[:, x], xx_send.at[k], xx_recv.at[k], (r, ylo * 4 + at_x(k))
            )
        for k in range(2):
            yy = at_y(-sides[k][1])
            for cc in range(2):
                arrived(wpiece(yy, cc), w_recv.at[k, cc], w_send.at[k])
            send(
                pending, wpiece(yy, k), wpiece(yy, k), wr_send.at[k], wr_recv.at[k],
                dev(z, at_y(sides[k][1]), 1, t),
            )
        for cc in range(2):
            for k in range(SEL):
                position = sel_ref[k, r - 1 + cc]
                trig_c[cc, pl.ds(k, 1), :] = cos_ref[pl.ds(position, 1), :]
                trig_s[cc, pl.ds(k, 1), :] = sin_ref[pl.ds(position, 1), :]
        own_w.wait()
        arrived(wpiece(y, 0), w_recv.at[2, 0], w_send.at[2])
        for k in range(1, NX):
            arrived(xall.at[:, at_x(-k)], xx_recv.at[k], xx_send.at[k])
        for k in range(2):
            arrived(wpiece(at_y(2), k), wr_recv.at[k], wr_send.at[k])
        part = jnp.dot(
            xbuf[...].reshape(NZ * 2 * SEL, 8 * HD),
            wbuf[...].reshape(8 * HD, KV),
            preferred_element_type=jnp.float32,
        )
        zsum[...] = part.reshape(NZ, 2, SEL, KV)
        for k in (4, 3, 5, 2, 6, 1, 7):
            send(
                pending, zsum.at[at_z(k)], zrecv.at[k], rz_send.at[k], rz_recv.at[k], dev(at_z(k), y, 1, t)
            )
        total = zsum[z]
        for k in range(1, NZ):
            arrived(zrecv.at[k], rz_recv.at[k], rz_send.at[k])
            total = total + zrecv[k]
        fresh = total.astype(jnp.bfloat16).astype(jnp.float32)
        for cc in range(2):
            keys = fresh[cc, :, :HD]
            keys = keys * trig_c[cc] + pltpu.roll(keys, HD // 2, 1) * trig_s[cc]
            own_fresh[cc, :, :HD] = keys.astype(jnp.bfloat16)
            own_fresh[cc, :, HD:] = fresh[cc, :, HD:].astype(jnp.bfloat16)
        for k in (1, 7, 2, 6, 3, 5, 4):
            send(pending, own_fresh, piece(z, y), fz_send.at[k], fz_recv.at[k], dev(at_z(k), y, 1, t))
        keep_fresh = pltpu.make_async_copy(own_fresh, piece(z, y), local_sem.at[len(loads) + 3])
        keep_fresh.start()
        def share(d):
            send(pending, column(at_y(d)), column(at_y(d)), fs_send.at[d], fs_recv.at[d], mate)

        near_first = (0, 1, 7, 2, 6, 3, 5, 4)
        for rel in near_first:
            here = piece(at_z(-rel), y)
            if rel:
                arrived(here, fz_recv.at[rel], fz_send.at[rel])
            for k in range(2):
                send(
                    pending, here if rel else own_fresh, here, fy_send.at[rel, k], fy_recv.at[rel, k],
                    dev(z, at_y(sides[k][1]), 1, t),
                )
        keep_fresh.wait()
        share(0)
        for rel in near_first:
            zz = at_z(-rel)
            for k in range(2):
                yy = at_y(-sides[k][1])
                arrived(piece(zz, yy), fy_recv.at[rel, k], fy_send.at[rel, k])
                send(
                    pending, half_piece(zz, yy, k), half_piece(zz, yy, k), fr_send.at[rel, k], fr_recv.at[rel, k],
                    dev(z, at_y(sides[k][1]), 1, t),
                )
        share(3)
        share(1)
        for rel in near_first:
            for k in range(2):
                arrived(half_piece(at_z(-rel), at_y(2), k), fr_recv.at[rel, k], fr_send.at[rel, k])
        share(2)
        own_copy.wait()
        arrived(kept(z, y, 0), ss_recv.at[0, 0], ss_send.at[0, 0])
        for rel in range(NZ):
            for d in range(NY):
                if rel or d:
                    arrived(chunk(at_z(rel), at_y(d)), ss_recv.at[rel, d], ss_send.at[rel, d])
        for copy in pending:
            copy.wait_send()

    for copy in started:
        copy.wait_send()

    kbufs, vbufs, sbufs, pbufs = (kbuf0, kbuf1), (vbuf0, vbuf1), (sbuf0, sbuf1), (pbuf0, pbuf1)
    steps = q_ref.shape[0] // PAIR

    def result_copy(step):
        rows = pl.ds(step * PAIR, PAIR)
        return pltpu.make_async_copy(out_ref.at[rows], out_hbm.at[rows], out_sem.at[step])

    col = lax.broadcasted_iota(jnp.int32, (CHUNK, 128), 1)
    token = lax.rem(lax.broadcasted_iota(jnp.int32, (CHUNK, 128), 0), QLEN)
    tail = jnp.where(col <= token, jnp.float32(0.0), jnp.float32(NEG))
    for i in range(PAIR):
        kbufs[i][LAST + QLEN :, :] = jnp.zeros((128 - QLEN, HD), jnp.bfloat16)
        vbufs[i][LAST + QLEN :, :] = jnp.zeros((128 - QLEN, HD), jnp.bfloat16)
    for copy in later:
        copy.wait()

    def turn(block, j):
        wide = block.astype(jnp.float32)
        wide = wide * cos_ref[PLEN + j : PLEN + j + 1, :] + pltpu.roll(wide, HD // 2, 1) * sin_ref[PLEN + j : PLEN + j + 1, :]
        return wide.astype(jnp.bfloat16)

    def pair(step, carry):
        for i in range(PAIR):
            kbuf, vbuf = kbufs[i], vbufs[i]
            request = step * PAIR + i
            for j in range(SLOTS):
                o = owner_ref[chosen_ref[j, request]]
                block = pas[o // 8, lax.rem(o, 8) // 2, lax.rem(o, 2)]
                keys = block[:, :HD]
                kbuf[j * PLEN : (j + 1) * PLEN, :] = turn(keys, j) if j else keys
                vbuf[j * PLEN : (j + 1) * PLEN, :] = block[:, HD:]
            own = own_ref[request]
            kbuf[LAST : LAST + QLEN, :] = own[:, :HD]
            vbuf[LAST : LAST + QLEN, :] = own[:, HD:]
        for i in range(PAIR):
            query = q_ref[step * PAIR + i]
            query = jnp.concatenate([query[:, h * HD : (h + 1) * HD] for h in range(GROUP)], 0)
            sbufs[i][...] = lax.dot_general(
                query, kbufs[i][...], (((1,), (1,)), ((), ())), preferred_element_type=jnp.float32
            )
        for i in range(PAIR):
            sbuf, pbuf = sbufs[i], pbufs[i]
            for first in range(0, GROUP * QLEN, CHUNK):
                rows = slice(first, first + CHUNK)
                raw = jnp.concatenate([sbuf[rows, :LAST], sbuf[rows, LAST:] + tail], 1)
                expo = jnp.exp2((raw - jnp.max(raw, 1, keepdims=True)) * SCALE)
                pbuf[rows, :] = (expo * (1.0 / jnp.sum(expo, 1, keepdims=True))).astype(jnp.bfloat16)
            result = jnp.dot(pbuf[...], vbufs[i][...], preferred_element_type=jnp.float32).astype(jnp.bfloat16)
            for h in range(GROUP):
                out_ref[step * PAIR + i, :, h * HD : (h + 1) * HD] = result[h * QLEN : (h + 1) * QLEN]
        result_copy(step).start()
        return carry

    lax.fori_loop(0, steps, pair, 0)
    for step in range(steps):
        result_copy(step).wait()


def local(stale, fresh_input, kv_weight, sel_index, owner, retrieval, queries, question_kv):
    cosine, sine = trig_tables()
    any_spec = pl.BlockSpec(memory_space=pl.ANY)
    dma = pltpu.SemaphoreType.DMA
    rows = GROUP * QLEN
    return pl.pallas_call(
        kernel,
        out_shape=jax.ShapeDtypeStruct(queries.shape, jnp.bfloat16),
        in_specs=[any_spec] * 10,
        out_specs=any_spec,
        scratch_shapes=[
            pltpu.VMEM((NZ, NY, 2, PLEN, KV), jnp.bfloat16),
            pltpu.VMEM((KEYS, HD), jnp.bfloat16),
            pltpu.VMEM((KEYS, HD), jnp.bfloat16),
            pltpu.VMEM((KEYS, HD), jnp.bfloat16),
            pltpu.VMEM((KEYS, HD), jnp.bfloat16),
            pltpu.VMEM((rows, KEYS), jnp.float32),
            pltpu.VMEM((rows, KEYS), jnp.bfloat16),
            pltpu.VMEM((rows, KEYS), jnp.float32),
            pltpu.VMEM((rows, KEYS), jnp.bfloat16),
            pltpu.VMEM(queries.shape, jnp.bfloat16),
            pltpu.VMEM(question_kv.shape, jnp.bfloat16),
            pltpu.VMEM(queries.shape, jnp.bfloat16),
            pltpu.SMEM((64,), jnp.int32),
            pltpu.SMEM((SLOTS, 8), jnp.int32),
            pltpu.VMEM((PLEN, KV), jnp.bfloat16),
            pltpu.VMEM((KEPT, KV), jnp.bfloat16),
            pltpu.VMEM((2, SEL, KV), jnp.bfloat16),
            pltpu.VMEM((8, 2, SEL, 8 * HD), jnp.bfloat16),
            pltpu.VMEM((NY, 2, HD, KV), jnp.bfloat16),
            pltpu.VMEM((NZ, 2, SEL, KV), jnp.float32),
            pltpu.VMEM((NZ, 2, SEL, KV), jnp.float32),
            pltpu.VMEM((2, SEL, HD), jnp.float32),
            pltpu.VMEM((2, SEL, HD), jnp.float32),
            pltpu.VMEM((NY, 2, SEL, HD), jnp.bfloat16),
            pltpu.VMEM((HD, KV), jnp.bfloat16),
            pltpu.VMEM(cosine.shape, jnp.float32),
            pltpu.VMEM(sine.shape, jnp.float32),
            pltpu.SMEM((SEL, 64), jnp.int32),
            dma((12,)),
            dma((8,)), dma((8, 2)),
            dma((NX,)), dma((NX,)),
            dma((3,)), dma((3, 2)),
            dma((2,)), dma((2,)),
            dma((4,)), dma((4, 2)),
            dma((2,)), dma((2,)),
            dma((NZ, 2)), dma((NZ, 2)),
            dma((2, 5, NY)), dma((2, 5, NY)),
            dma((NZ, NY)), dma((NZ, NY)),
            dma((NZ,)), dma((NZ,)),
            dma((NZ,)), dma((NZ,)),
            dma((NZ, 2)), dma((NZ, 2)),
            dma((NZ, 2)), dma((NZ, 2)),
            dma((NY,)), dma((NY,)),
            dma((2,)), dma((4,)),
        ],
        compiler_params=pltpu.CompilerParams(
            collective_id=0, has_side_effects=True, vmem_limit_bytes=62 * 1024 * 1024
        ),
    )(
        stale,
        fresh_input.reshape(NY, 2, SEL, HD),
        kv_weight,
        sel_index.T,
        jnp.asarray(cosine),
        jnp.asarray(sine),
        owner,
        retrieval.T,
        queries,
        question_kv,
    )


def solution(mesh):
    return jax.shard_map(
        local,
        mesh=mesh,
        in_specs=(
            P("req", None, "tp"),
            P("tp", None, "req"),
            P("req", None),
            P(),
            P(),
            P("req", None),
            P("req", None, "tp"),
            P("req", None, "tp"),
        ),
        out_specs=P("req", None, "tp"),
        check_vma=False,
    )
```

```python
import functools
import math

import jax
import jax.numpy as jnp
import numpy as np
from jax import lax
from jax.experimental import pallas as pl
from jax.experimental.pallas import tpu as pltpu
from jax.sharding import PartitionSpec as P

MESH = pl.DeviceIdType.MESH
HD = 128
NZ, NY, NX = 8, 4, 4
PLEN, QLEN, SEL, SLOTS = 128, 32, 16, 4
GROUP = 8
KV = 2 * HD
LAST = SLOTS * PLEN
KEYS = LAST + 128
KEPT = PLEN - SEL
CHUNK = 64
SCALE = math.log2(math.e) / math.sqrt(HD)
NEG = -1e30
THETA = 500000.0
PAIR = 2


def trig_tables():
    positions = np.concatenate([np.arange(PLEN), np.arange(8) * PLEN]).astype(np.float32)
    freqs = (THETA ** (-(np.arange(HD // 2, dtype=np.float64) * 2.0 / HD))).astype(np.float32)
    angle = (positions[:, None] * freqs).astype(np.float32).astype(np.float64)
    cosine, sine = np.cos(angle), np.sin(angle)
    return (
        np.concatenate([cosine, cosine], -1).astype(np.float32),
        np.concatenate([-sine, sine], -1).astype(np.float32),
    )


def kernel(
    stale_hbm, x_hbm, w_hbm, sel_hbm, cos_hbm, sin_hbm, owner_hbm, chosen_hbm, q_hbm, own_hbm,
    out_hbm,
    pas, kbuf0, vbuf0, kbuf1, vbuf1, sbuf0, pbuf0, sbuf1, pbuf1, q_ref, own_ref, out_ref, owner_ref, chosen_ref,
    stale_ref, own_rows, own_fresh, xbuf, wbuf, zsum, zrecv, trig_c, trig_s, x_ref, w_ref, cos_ref, sin_ref, sel_ref,
    local_sem, xy_send, xy_recv, xx_send, xx_recv, w_send, w_recv, wr_send, wr_recv,
    seed_send, seed_recv, yr_send, yr_recv, yf_send, yf_recv, sz_send, sz_recv, ss_send, ss_recv,
    rz_send, rz_recv, fz_send, fz_recv, fy_send, fy_recv, fr_send, fr_recv, fs_send, fs_recv, q_sem, out_sem,
):
    r, t = lax.axis_index("req"), lax.axis_index("tp")
    z, y, c = r // 8, lax.rem(r, 8) // 2, lax.rem(r, 2)
    ylo, x = t // 4, lax.rem(t, 4)

    def dev(zz, yy, cc, tt):
        return (zz * 8 + yy * 2 + cc, tt)

    def at_z(k):
        return lax.rem(z + k + 2 * NZ, NZ)

    def at_y(k):
        return lax.rem(y + k + 2 * NY, NY)

    def at_x(k):
        return lax.rem(x + k + 2 * NX, NX)

    def other(dl):
        return lax.rem(ylo + dl, 2)

    def remote(src, dst, send_sem, recv_sem, device):
        return pltpu.make_async_remote_copy(
            src_ref=src, dst_ref=dst, send_sem=send_sem[0].at[send_sem[1]], recv_sem=recv_sem[0].at[recv_sem[1]],
            device_id=device, device_id_type=MESH,
        )

    def arrived(dst, recv_sem, send_sem):
        remote(dst, dst, send_sem, recv_sem, dev(z, y, 1 - c, t)).wait_recv()

    def send(pending, src, dst, send_sem, recv_sem, device):
        remote(src, dst, send_sem, recv_sem, device).start()
        pending.append((tuple(src.shape), jnp.dtype(src.dtype), send_sem, recv_sem))

    def drain(pending):
        shapes = [
            pas.at[0, 0, :, pl.ds(0, KEPT)], pas.at[0, 0, 0, pl.ds(0, KEPT)], pas.at[:, 0, :, pl.ds(KEPT, SEL)],
            pas.at[0, 0, :, pl.ds(KEPT, SEL)], pas.at[0, 0, 0, pl.ds(KEPT, SEL)], x_ref.at[0], w_ref,
            xbuf.reshape(2, 4, 2, SEL, 8 * HD).at[:, 0], zsum.at[0],
        ]
        kinds = {(tuple(ref.shape), jnp.dtype(ref.dtype)): ref for ref in shapes}
        for shape, kind, send_sem, recv_sem in pending:
            ref = kinds[shape, kind]
            remote(ref, ref, send_sem, recv_sem, dev(z, y, 1 - c, t)).wait_send()

    sent = [[], []]

    line = [(dy, dl) for dy in range(NY) for dl in range(2)]
    sides = [(0, 1), (0, -1), (1, 0), (-1, 0)]

    barrier = pltpu.get_barrier_semaphore()

    def greet(device):
        pl.semaphore_signal(barrier, inc=1, device_id=device, device_id_type=MESH)

    @pl.when(c == 0)
    def _():
        for dz, dy in sides:
            for cc in range(2):
                greet(dev(at_z(dz), at_y(dy), cc, t))
        greet(dev(z, y, 1, t))

    @pl.when(c == 1)
    def _():
        for dy, dl in line[1:]:
            for cc in range(2):
                greet(dev(z, at_y(dy), cc, other(dl) * 4 + x))
        greet(dev(z, y, 0, t))
        for k in range(1, NX):
            greet((r, ylo * 4 + at_x(k)))
        for k in range(1, NZ):
            greet(dev(at_z(k), y, 1, t))

    columns = pl.ds(pl.multiple_of(t * KV, KV), KV)

    def chunk(zz, yy):
        return pas.at[zz, yy, :, pl.ds(0, KEPT)]

    def kept(zz, yy, cc):
        return pas.at[zz, yy, cc, pl.ds(0, KEPT)]

    def column(yy):
        return pas.at[:, yy, :, pl.ds(KEPT, SEL)]

    def piece(zz, yy):
        return pas.at[zz, yy, :, pl.ds(KEPT, SEL)]

    def half_piece(zz, yy, cc):
        return pas.at[zz, yy, cc, pl.ds(KEPT, SEL)]

    def xpiece(ts, ys, cs):
        return xbuf.at[ts, :, :, pl.ds(pl.multiple_of((ys * 2 + cs) * HD, HD), HD)]

    def wpiece(ys, cs):
        return wbuf.at[ys, cs]

    loads = []

    def load(source, target):
        copy = pltpu.make_async_copy(source, target, local_sem.at[len(loads)])
        copy.start()
        loads.append(copy)
        return copy

    load_sel = load(sel_hbm, sel_ref)
    load_stale = load(stale_hbm.at[0], stale_ref)
    load_x = load(x_hbm, x_ref)
    load_w = load(w_hbm.at[:, columns], w_ref)
    load_cos = load(cos_hbm, cos_ref)
    load_sin = load(sin_hbm, sin_ref)
    load_owner = load(owner_hbm, owner_ref)
    load_chosen = load(chosen_hbm, chosen_ref)
    later = []
    for k, (source, target) in enumerate(((q_hbm, q_ref), (own_hbm, own_ref))):
        later.append(pltpu.make_async_copy(source, target, q_sem.at[k]))
        later[-1].start()

    load_sel.wait()
    lane = lax.broadcasted_iota(jnp.int32, (8, PLEN), 1)
    hit = lane == sel_ref[0, r]
    for k in range(1, SEL):
        hit = hit | (lane == sel_ref[k, r])
    keep = jnp.where(hit, jnp.float32(0.0), jnp.float32(1.0))
    before = lax.broadcasted_iota(jnp.int32, (PLEN, PLEN), 0) < lax.broadcasted_iota(jnp.int32, (PLEN, PLEN), 1)
    rank = jnp.dot(
        keep.astype(jnp.bfloat16),
        jnp.where(before, jnp.float32(1.0), jnp.float32(0.0)).astype(jnp.bfloat16),
        preferred_element_type=jnp.float32,
    )
    order = lax.broadcasted_iota(jnp.int32, (KEPT, PLEN), 0).astype(jnp.float32)
    picked = jnp.where(order == rank[0:1], keep[0:1], jnp.float32(0.0)).astype(jnp.bfloat16)
    load_stale.wait()
    own_rows[...] = jnp.dot(picked, stale_ref[...], preferred_element_type=jnp.float32).astype(jnp.bfloat16)
    load_x.wait()
    load_w.wait()
    load_cos.wait()
    load_sin.wait()
    load_owner.wait()
    load_chosen.wait()

    @pl.when(c == 0)
    def _():
        pl.semaphore_wait(barrier, 12)

    @pl.when(c == 1)
    def _():
        pl.semaphore_wait(barrier, 22)

    started = []
    for k, (dy, dl) in enumerate(line[1:]):
        send(
            started, x_ref.at[at_y(dy)], xpiece(t, y, c), (xy_send, (k + 1,)), (xy_recv, (k + 1, c,)),
            dev(z, at_y(dy), 1, other(dl) * 4 + x),
        )
    for k in (2, 3, 0, 1):
        dz, dy = sides[k]
        send(
            started, own_rows, kept(z, y, c), (seed_send, (k,)), (seed_recv, (k, c,)), dev(at_z(dz), at_y(dy), 0, t)
        )
    for k in range(2):
        send(
            started, w_ref, wpiece(y, c), (w_send, (k,)), (w_recv, (k, c,)), dev(z, at_y(sides[k][1]), 1, t)
        )

    @pl.when(c == 0)
    def _():
        pending = sent[0]
        mate = dev(z, y, 1, t)
        send(pending, x_ref.at[y], xpiece(t, y, 0), (xy_send, (0,)), (xy_recv, (0, 0,)), mate)
        send(pending, w_ref, wpiece(y, 0), (w_send, (2,)), (w_recv, (2, 0,)), mate)
        own_copy = pltpu.make_async_copy(own_rows, kept(z, y, 0), local_sem.at[len(loads)])
        own_copy.start()

        def ring(zz, yy, s, d, way):
            step = 1 if way == 0 else -1
            send(
                pending, chunk(zz, yy), chunk(zz, yy), (sz_send, (way, s, d,)), (sz_recv, (way, s, d,)),
                dev(at_z(step), y, 0, t),
            )

        def share(zz, yy, rel, d):
            send(pending, chunk(zz, yy), chunk(zz, yy), (ss_send, (rel, d,)), (ss_recv, (rel, d,)), mate)

        def inject(d):
            for way in range(2):
                ring(z, at_y(d), 1, d, way)
            share(z, at_y(d), 0, d)

        def last_way(d):
            return 0 if d == 1 else 1

        def hop(s, d):
            for way in range(2):
                if s == 4 and way != last_way(d):
                    continue
                rel = (-s if way == 0 else s) % NZ
                zz, yy = at_z(rel), at_y(d)
                if s == 1 and d == 0:
                    for cc in range(2):
                        arrived(kept(zz, yy, cc), (seed_recv, (2 + way, cc,)), (seed_send, (2 + way,)))
                else:
                    arrived(chunk(zz, yy), (sz_recv, (way, s, d,)), (sz_send, (way, s, d,)))
                if (s < 3 and d != 2) or (s == 3 and way == last_way(d)):
                    ring(zz, yy, s + 1, d, way)
                if s >= 2 and d:
                    k = 0 if d == 3 else 1
                    send(
                        pending, kept(zz, yy, k), kept(zz, yy, k), (yf_send, (rel, k,)), (yf_recv, (rel, k,)),
                        dev(z, at_y(sides[k][1]), 0, t),
                    )
                share(zz, yy, rel, d)

        hop(1, 0)
        for k in range(2):
            yy = at_y(-sides[k][1])
            for cc in range(2):
                arrived(kept(z, yy, cc), (seed_recv, (k, cc,)), (seed_send, (k,)))
            send(
                pending, kept(z, yy, k), kept(z, yy, k), (yr_send, (k,)), (yr_recv, (k,)),
                dev(z, at_y(sides[k][1]), 0, t),
            )
            inject(3 if k == 0 else 1)
        hop(2, 0)
        hop(1, 3)
        hop(1, 1)
        for k in range(2):
            arrived(kept(z, at_y(2), k), (yr_recv, (k,)), (yr_send, (k,)))
        inject(2)
        own_copy.wait()
        arrived(kept(z, y, 1), (ss_recv, (0, 0,)), (ss_send, (0, 0,)))
        send(pending, kept(z, y, 0), kept(z, y, 0), (ss_send, (0, 0,)), (ss_recv, (0, 0,)), mate)
        for s, d in (
            (3, 0), (2, 3), (2, 1), (1, 2), (4, 0), (3, 3), (3, 1), (4, 3), (4, 1),
        ):
            hop(s, d)
        for rel in (6, 2, 5, 3, 4):
            for k in range(2):
                arrived(kept(at_z(rel), at_y(2), k), (yf_recv, (rel, k,)), (yf_send, (rel, k,)))
            share(at_z(rel), at_y(2), rel, 2)
        for d in range(NY):
            arrived(column(at_y(d)), (fs_recv, (d,)), (fs_send, (d,)))

    @pl.when(c == 1)
    def _():
        pending = sent[1]
        mate = dev(z, y, 0, t)
        own_x = pltpu.make_async_copy(x_ref.at[y], xpiece(t, y, 1), local_sem.at[len(loads)])
        own_w = pltpu.make_async_copy(w_ref, wpiece(y, 1), local_sem.at[len(loads) + 1])
        own_copy = pltpu.make_async_copy(own_rows, kept(z, y, 1), local_sem.at[len(loads) + 2])
        own_x.start()
        own_w.start()
        own_copy.start()
        send(pending, own_rows, kept(z, y, 1), (ss_send, (0, 0,)), (ss_recv, (0, 0,)), mate)
        own_x.wait()
        arrived(xpiece(t, y, 0), (xy_recv, (0, 0,)), (xy_send, (0,)))
        for k, (dy, dl) in enumerate(line[1:]):
            for cc in range(2):
                arrived(xpiece(other(dl) * 4 + x, at_y(-dy), cc), (xy_recv, (k + 1, cc,)), (xy_send, (k + 1,)))
        xall = xbuf.reshape(2, 4, 2, SEL, 8 * HD)
        for k in range(1, NX):
            send(
                pending, xall.at[:, x], xall.at[:, x], (xx_send, (k,)), (xx_recv, (k,)), (r, ylo * 4 + at_x(k))
            )
        for k in range(2):
            yy = at_y(-sides[k][1])
            for cc in range(2):
                arrived(wpiece(yy, cc), (w_recv, (k, cc,)), (w_send, (k,)))
            send(
                pending, wpiece(yy, k), wpiece(yy, k), (wr_send, (k,)), (wr_recv, (k,)),
                dev(z, at_y(sides[k][1]), 1, t),
            )
        for cc in range(2):
            for k in range(SEL):
                position = sel_ref[k, r - 1 + cc]
                trig_c[cc, pl.ds(k, 1), :] = cos_ref[pl.ds(position, 1), :]
                trig_s[cc, pl.ds(k, 1), :] = sin_ref[pl.ds(position, 1), :]
        own_w.wait()
        arrived(wpiece(y, 0), (w_recv, (2, 0,)), (w_send, (2,)))
        for k in range(1, NX):
            arrived(xall.at[:, at_x(-k)], (xx_recv, (k,)), (xx_send, (k,)))
        for k in range(2):
            arrived(wpiece(at_y(2), k), (wr_recv, (k,)), (wr_send, (k,)))
        part = jnp.dot(
            xbuf[...].reshape(NZ * 2 * SEL, 8 * HD),
            wbuf[...].reshape(8 * HD, KV),
            preferred_element_type=jnp.float32,
        )
        zsum[...] = part.reshape(NZ, 2, SEL, KV)
        for k in range(1, NZ):
            send(
                pending, zsum.at[at_z(k)], zrecv.at[k], (rz_send, (k,)), (rz_recv, (k,)), dev(at_z(k), y, 1, t)
            )
        total = zsum[z]
        for k in range(1, NZ):
            arrived(zrecv.at[k], (rz_recv, (k,)), (rz_send, (k,)))
            total = total + zrecv[k]
        fresh = total.astype(jnp.bfloat16).astype(jnp.float32)
        for cc in range(2):
            keys = fresh[cc, :, :HD]
            keys = keys * trig_c[cc] + pltpu.roll(keys, HD // 2, 1) * trig_s[cc]
            own_fresh[cc, :, :HD] = keys.astype(jnp.bfloat16)
            own_fresh[cc, :, HD:] = fresh[cc, :, HD:].astype(jnp.bfloat16)
        for k in range(1, NZ):
            send(pending, own_fresh, piece(z, y), (fz_send, (k,)), (fz_recv, (k,)), dev(at_z(k), y, 1, t))
        keep_fresh = pltpu.make_async_copy(own_fresh, piece(z, y), local_sem.at[len(loads) + 3])
        keep_fresh.start()
        keep_fresh.wait()
        def share(d):
            send(pending, column(at_y(d)), column(at_y(d)), (fs_send, (d,)), (fs_recv, (d,)), mate)

        near_first = (0, 1, 7, 2, 6, 3, 5, 4)
        for rel in near_first:
            here = piece(at_z(-rel), y)
            if rel:
                arrived(here, (fz_recv, (rel,)), (fz_send, (rel,)))
            for k in range(2):
                send(
                    pending, here, here, (fy_send, (rel, k,)), (fy_recv, (rel, k,)),
                    dev(z, at_y(sides[k][1]), 1, t),
                )
        share(0)
        for rel in near_first:
            zz = at_z(-rel)
            for k in range(2):
                yy = at_y(-sides[k][1])
                arrived(piece(zz, yy), (fy_recv, (rel, k,)), (fy_send, (rel, k,)))
                send(
                    pending, half_piece(zz, yy, k), half_piece(zz, yy, k), (fr_send, (rel, k,)), (fr_recv, (rel, k,)),
                    dev(z, at_y(sides[k][1]), 1, t),
                )
        share(3)
        share(1)
        for rel in near_first:
            for k in range(2):
                arrived(half_piece(at_z(-rel), at_y(2), k), (fr_recv, (rel, k,)), (fr_send, (rel, k,)))
        share(2)
        own_copy.wait()
        arrived(kept(z, y, 0), (ss_recv, (0, 0,)), (ss_send, (0, 0,)))
        for rel in range(NZ):
            for d in range(NY):
                if rel or d:
                    arrived(chunk(at_z(rel), at_y(d)), (ss_recv, (rel, d,)), (ss_send, (rel, d,)))

    kbufs, vbufs, sbufs, pbufs = (kbuf0, kbuf1), (vbuf0, vbuf1), (sbuf0, sbuf1), (pbuf0, pbuf1)
    steps = q_ref.shape[0] // PAIR

    def result_copy(step):
        rows = pl.ds(step * PAIR, PAIR)
        return pltpu.make_async_copy(out_ref.at[rows], out_hbm.at[rows], out_sem.at[step])

    col = lax.broadcasted_iota(jnp.int32, (CHUNK, 128), 1)
    token = lax.rem(lax.broadcasted_iota(jnp.int32, (CHUNK, 128), 0), QLEN)
    tail = jnp.where(col <= token, jnp.float32(0.0), jnp.float32(NEG))
    for i in range(PAIR):
        kbufs[i][LAST + QLEN :, :] = jnp.zeros((128 - QLEN, HD), jnp.bfloat16)
        vbufs[i][LAST + QLEN :, :] = jnp.zeros((128 - QLEN, HD), jnp.bfloat16)
    for copy in later:
        copy.wait()

    def turn(block, j):
        wide = block.astype(jnp.float32)
        wide = wide * cos_ref[PLEN + j : PLEN + j + 1, :] + pltpu.roll(wide, HD // 2, 1) * sin_ref[PLEN + j : PLEN + j + 1, :]
        return wide.astype(jnp.bfloat16)

    def pair(step, carry):
        for i in range(PAIR):
            kbuf, vbuf = kbufs[i], vbufs[i]
            request = step * PAIR + i
            for j in range(SLOTS):
                o = owner_ref[chosen_ref[j, request]]
                block = pas[o // 8, lax.rem(o, 8) // 2, lax.rem(o, 2)]
                keys = block[:, :HD]
                kbuf[j * PLEN : (j + 1) * PLEN, :] = turn(keys, j) if j else keys
                vbuf[j * PLEN : (j + 1) * PLEN, :] = block[:, HD:]
            own = own_ref[request]
            kbuf[LAST : LAST + QLEN, :] = own[:, :HD]
            vbuf[LAST : LAST + QLEN, :] = own[:, HD:]
        for i in range(PAIR):
            query = q_ref[step * PAIR + i]
            query = jnp.concatenate([query[:, h * HD : (h + 1) * HD] for h in range(GROUP)], 0)
            sbufs[i][...] = lax.dot_general(
                query, kbufs[i][...], (((1,), (1,)), ((), ())), preferred_element_type=jnp.float32
            )
        for i in range(PAIR):
            sbuf, pbuf = sbufs[i], pbufs[i]
            for first in range(0, GROUP * QLEN, CHUNK):
                rows = slice(first, first + CHUNK)
                raw = jnp.concatenate([sbuf[rows, :LAST], sbuf[rows, LAST:] + tail], 1)
                expo = jnp.exp2((raw - jnp.max(raw, 1, keepdims=True)) * SCALE)
                pbuf[rows, :] = (expo * (1.0 / jnp.sum(expo, 1, keepdims=True))).astype(jnp.bfloat16)
            result = jnp.dot(pbuf[...], vbufs[i][...], preferred_element_type=jnp.float32).astype(jnp.bfloat16)
            for h in range(GROUP):
                out_ref[step * PAIR + i, :, h * HD : (h + 1) * HD] = result[h * QLEN : (h + 1) * QLEN]
        result_copy(step).start()
        return carry

    lax.fori_loop(0, steps, pair, 0)
    for step in range(steps):
        result_copy(step).wait()
    drain(started)
    for core in range(2):

        @pl.when(c == core)
        def _(core=core):
            drain(sent[core])


def local(stale, fresh_input, kv_weight, sel_index, owner, retrieval, queries, question_kv):
    cosine, sine = trig_tables()
    any_spec = pl.BlockSpec(memory_space=pl.ANY)
    dma = pltpu.SemaphoreType.DMA
    rows = GROUP * QLEN
    return pl.pallas_call(
        kernel,
        out_shape=jax.ShapeDtypeStruct(queries.shape, jnp.bfloat16),
        in_specs=[any_spec] * 10,
        out_specs=any_spec,
        scratch_shapes=[
            pltpu.VMEM((NZ, NY, 2, PLEN, KV), jnp.bfloat16),
            pltpu.VMEM((KEYS, HD), jnp.bfloat16),
            pltpu.VMEM((KEYS, HD), jnp.bfloat16),
            pltpu.VMEM((KEYS, HD), jnp.bfloat16),
            pltpu.VMEM((KEYS, HD), jnp.bfloat16),
            pltpu.VMEM((rows, KEYS), jnp.float32),
            pltpu.VMEM((rows, KEYS), jnp.bfloat16),
            pltpu.VMEM((rows, KEYS), jnp.float32),
            pltpu.VMEM((rows, KEYS), jnp.bfloat16),
            pltpu.VMEM(queries.shape, jnp.bfloat16),
            pltpu.VMEM(question_kv.shape, jnp.bfloat16),
            pltpu.VMEM(queries.shape, jnp.bfloat16),
            pltpu.SMEM((64,), jnp.int32),
            pltpu.SMEM((SLOTS, 8), jnp.int32),
            pltpu.VMEM((PLEN, KV), jnp.bfloat16),
            pltpu.VMEM((KEPT, KV), jnp.bfloat16),
            pltpu.VMEM((2, SEL, KV), jnp.bfloat16),
            pltpu.VMEM((8, 2, SEL, 8 * HD), jnp.bfloat16),
            pltpu.VMEM((NY, 2, HD, KV), jnp.bfloat16),
            pltpu.VMEM((NZ, 2, SEL, KV), jnp.float32),
            pltpu.VMEM((NZ, 2, SEL, KV), jnp.float32),
            pltpu.VMEM((2, SEL, HD), jnp.float32),
            pltpu.VMEM((2, SEL, HD), jnp.float32),
            pltpu.VMEM((NY, 2, SEL, HD), jnp.bfloat16),
            pltpu.VMEM((HD, KV), jnp.bfloat16),
            pltpu.VMEM(cosine.shape, jnp.float32),
            pltpu.VMEM(sine.shape, jnp.float32),
            pltpu.SMEM((SEL, 64), jnp.int32),
            dma((12,)),
            dma((8,)), dma((8, 2)),
            dma((NX,)), dma((NX,)),
            dma((3,)), dma((3, 2)),
            dma((2,)), dma((2,)),
            dma((4,)), dma((4, 2)),
            dma((2,)), dma((2,)),
            dma((NZ, 2)), dma((NZ, 2)),
            dma((2, 5, NY)), dma((2, 5, NY)),
            dma((NZ, NY)), dma((NZ, NY)),
            dma((NZ,)), dma((NZ,)),
            dma((NZ,)), dma((NZ,)),
            dma((NZ, 2)), dma((NZ, 2)),
            dma((NZ, 2)), dma((NZ, 2)),
            dma((NY,)), dma((NY,)),
            dma((2,)), dma((4,)),
        ],
        compiler_params=pltpu.CompilerParams(
            collective_id=0, has_side_effects=True, vmem_limit_bytes=62 * 1024 * 1024
        ),
    )(
        stale,
        fresh_input.reshape(NY, 2, SEL, HD),
        kv_weight,
        sel_index.T,
        jnp.asarray(cosine),
        jnp.asarray(sine),
        owner,
        retrieval.T,
        queries,
        question_kv,
    )


def solution(mesh):
    return jax.shard_map(
        local,
        mesh=mesh,
        in_specs=(
            P("req", None, "tp"),
            P("tp", None, "req"),
            P("req", None),
            P(),
            P(),
            P("req", None),
            P("req", None, "tp"),
            P("req", None, "tp"),
        ),
        out_specs=P("req", None, "tp"),
        check_vma=False,
    )
```

```python
import functools
import math

import jax
import jax.numpy as jnp
import numpy as np
from jax import lax
from jax.experimental import pallas as pl
from jax.experimental.pallas import tpu as pltpu
from jax.sharding import PartitionSpec as P

MESH = pl.DeviceIdType.MESH
HD = 128
NZ, NY, NX = 8, 4, 4
PLEN, QLEN, SEL, SLOTS = 128, 32, 16, 4
GROUP = 8
KV = 2 * HD
LAST = SLOTS * PLEN
KEYS = LAST + 128
KEPT = PLEN - SEL
CHUNK = 64
SCALE = math.log2(math.e) / math.sqrt(HD)
NEG = -1e30
THETA = 500000.0
PAIR = 2


def trig_tables():
    positions = np.concatenate([np.arange(PLEN), np.arange(8) * PLEN]).astype(np.float32)
    freqs = (THETA ** (-(np.arange(HD // 2, dtype=np.float64) * 2.0 / HD))).astype(np.float32)
    angle = (positions[:, None] * freqs).astype(np.float32).astype(np.float64)
    cosine, sine = np.cos(angle), np.sin(angle)
    return (
        np.concatenate([cosine, cosine], -1).astype(np.float32),
        np.concatenate([-sine, sine], -1).astype(np.float32),
    )


def kernel(
    stale_hbm, x_hbm, w_hbm, sel_hbm, cos_hbm, sin_hbm, owner_hbm, chosen_hbm, q_hbm, own_hbm,
    out_hbm,
    pas, kbuf0, vbuf0, kbuf1, vbuf1, sbuf0, pbuf0, sbuf1, pbuf1, q_ref, own_ref, out_ref, owner_ref, chosen_ref,
    stale_ref, own_rows, own_fresh, xbuf, wbuf, zsum, zrecv, trig_c, trig_s, x_ref, w_ref, cos_ref, sin_ref, sel_ref,
    local_sem, xy_send, xy_recv, xx_send, xx_recv, w_send, w_recv, wr_send, wr_recv,
    seed_send, seed_recv, yr_send, yr_recv, yf_send, yf_recv, sz_send, sz_recv, ss_send, ss_recv,
    rz_send, rz_recv, fz_send, fz_recv, fy_send, fy_recv, fr_send, fr_recv, fs_send, fs_recv, q_sem, out_sem,
):
    r, t = lax.axis_index("req"), lax.axis_index("tp")
    z, y, c = r // 8, lax.rem(r, 8) // 2, lax.rem(r, 2)
    ylo, x = t // 4, lax.rem(t, 4)

    def dev(zz, yy, cc, tt):
        return (zz * 8 + yy * 2 + cc, tt)

    def at_z(k):
        return lax.rem(z + k + 2 * NZ, NZ)

    def at_y(k):
        return lax.rem(y + k + 2 * NY, NY)

    def at_x(k):
        return lax.rem(x + k + 2 * NX, NX)

    def other(dl):
        return lax.rem(ylo + dl, 2)

    def remote(src, dst, send_sem, recv_sem, device):
        return pltpu.make_async_remote_copy(
            src_ref=src, dst_ref=dst, send_sem=send_sem[0].at[send_sem[1]], recv_sem=recv_sem[0].at[recv_sem[1]],
            device_id=device, device_id_type=MESH,
        )

    def arrived(dst, recv_sem, send_sem):
        remote(dst, dst, send_sem, recv_sem, dev(z, y, 1 - c, t)).wait_recv()

    def send(pending, src, dst, send_sem, recv_sem, device):
        remote(src, dst, send_sem, recv_sem, device).start()
        pending.append((tuple(src.shape), jnp.dtype(src.dtype), send_sem, recv_sem))

    def drain(pending):
        shapes = [
            pas.at[0, 0, :, pl.ds(0, KEPT)], pas.at[0, 0, 0, pl.ds(0, KEPT)], pas.at[:, 0, :, pl.ds(KEPT, SEL)],
            pas.at[0, 0, :, pl.ds(KEPT, SEL)], pas.at[0, 0, 0, pl.ds(KEPT, SEL)], x_ref.at[0], w_ref,
            xbuf.reshape(2, 4, 2, SEL, 8 * HD).at[:, 0], zsum.at[0],
        ]
        kinds = {(tuple(ref.shape), jnp.dtype(ref.dtype)): ref for ref in shapes}
        for shape, kind, send_sem, recv_sem in pending:
            ref = kinds[shape, kind]
            remote(ref, ref, send_sem, recv_sem, dev(z, y, 1 - c, t)).wait_send()

    sent = [[], []]

    line = [(dy, dl) for dy in range(NY) for dl in range(2)]
    sides = [(0, 1), (0, -1), (1, 0), (-1, 0)]

    barrier = pltpu.get_barrier_semaphore()

    def greet(device):
        pl.semaphore_signal(barrier, inc=1, device_id=device, device_id_type=MESH)

    @pl.when(c == 0)
    def _():
        for dz, dy in sides:
            for cc in range(2):
                greet(dev(at_z(dz), at_y(dy), cc, t))
        greet(dev(z, y, 1, t))

    @pl.when(c == 1)
    def _():
        for dy, dl in line[1:]:
            for cc in range(2):
                greet(dev(z, at_y(dy), cc, other(dl) * 4 + x))
        greet(dev(z, y, 0, t))
        for k in range(1, NX):
            greet((r, ylo * 4 + at_x(k)))
        for k in range(1, NZ):
            greet(dev(at_z(k), y, 1, t))

    columns = pl.ds(pl.multiple_of(t * KV, KV), KV)

    def chunk(zz, yy):
        return pas.at[zz, yy, :, pl.ds(0, KEPT)]

    def kept(zz, yy, cc):
        return pas.at[zz, yy, cc, pl.ds(0, KEPT)]

    def column(yy):
        return pas.at[:, yy, :, pl.ds(KEPT, SEL)]

    def piece(zz, yy):
        return pas.at[zz, yy, :, pl.ds(KEPT, SEL)]

    def half_piece(zz, yy, cc):
        return pas.at[zz, yy, cc, pl.ds(KEPT, SEL)]

    def xpiece(ts, ys, cs):
        return xbuf.at[ts, :, :, pl.ds(pl.multiple_of((ys * 2 + cs) * HD, HD), HD)]

    def wpiece(ys, cs):
        return wbuf.at[ys, cs]

    loads = []

    def load(source, target):
        copy = pltpu.make_async_copy(source, target, local_sem.at[len(loads)])
        copy.start()
        loads.append(copy)
        return copy

    load_sel = load(sel_hbm, sel_ref)
    load_stale = load(stale_hbm.at[0], stale_ref)
    load_x = load(x_hbm, x_ref)
    load_w = load(w_hbm.at[:, columns], w_ref)
    load_cos = load(cos_hbm, cos_ref)
    load_sin = load(sin_hbm, sin_ref)
    load_owner = load(owner_hbm, owner_ref)
    load_chosen = load(chosen_hbm, chosen_ref)
    later = []
    for k, (source, target) in enumerate(((q_hbm, q_ref), (own_hbm, own_ref))):
        later.append(pltpu.make_async_copy(source, target, q_sem.at[k]))
        later[-1].start()

    load_x.wait()

    @pl.when(c == 0)
    def _():
        pl.semaphore_wait(barrier, 12)

    @pl.when(c == 1)
    def _():
        pl.semaphore_wait(barrier, 22)

    started = []
    for k, (dy, dl) in enumerate(line[1:]):
        send(
            started, x_ref.at[at_y(dy)], xpiece(t, y, c), (xy_send, (k + 1,)), (xy_recv, (k + 1, c,)),
            dev(z, at_y(dy), 1, other(dl) * 4 + x),
        )
    load_sel.wait()
    lane = lax.broadcasted_iota(jnp.int32, (8, PLEN), 1)
    hit = lane == sel_ref[0, r]
    for k in range(1, SEL):
        hit = hit | (lane == sel_ref[k, r])
    keep = jnp.where(hit, jnp.float32(0.0), jnp.float32(1.0))
    before = lax.broadcasted_iota(jnp.int32, (PLEN, PLEN), 0) < lax.broadcasted_iota(jnp.int32, (PLEN, PLEN), 1)
    rank = jnp.dot(
        keep.astype(jnp.bfloat16),
        jnp.where(before, jnp.float32(1.0), jnp.float32(0.0)).astype(jnp.bfloat16),
        preferred_element_type=jnp.float32,
    )
    order = lax.broadcasted_iota(jnp.int32, (KEPT, PLEN), 0).astype(jnp.float32)
    picked = jnp.where(order == rank[0:1], keep[0:1], jnp.float32(0.0)).astype(jnp.bfloat16)
    load_stale.wait()
    own_rows[...] = jnp.dot(picked, stale_ref[...], preferred_element_type=jnp.float32).astype(jnp.bfloat16)
    for k in (2, 3, 0, 1):
        dz, dy = sides[k]
        send(
            started, own_rows, kept(z, y, c), (seed_send, (k,)), (seed_recv, (k, c,)), dev(at_z(dz), at_y(dy), 0, t)
        )
    load_w.wait()
    for k in range(2):
        send(
            started, w_ref, wpiece(y, c), (w_send, (k,)), (w_recv, (k, c,)), dev(z, at_y(sides[k][1]), 1, t)
        )

    for copy in (load_cos, load_sin, load_owner, load_chosen):
        copy.wait()

    @pl.when(c == 0)
    def _():
        pending = sent[0]
        mate = dev(z, y, 1, t)
        send(pending, x_ref.at[y], xpiece(t, y, 0), (xy_send, (0,)), (xy_recv, (0, 0,)), mate)
        send(pending, w_ref, wpiece(y, 0), (w_send, (2,)), (w_recv, (2, 0,)), mate)
        own_copy = pltpu.make_async_copy(own_rows, kept(z, y, 0), local_sem.at[len(loads)])
        own_copy.start()

        def ring(zz, yy, s, d, way):
            step = 1 if way == 0 else -1
            send(
                pending, chunk(zz, yy), chunk(zz, yy), (sz_send, (way, s, d,)), (sz_recv, (way, s, d,)),
                dev(at_z(step), y, 0, t),
            )

        def share(zz, yy, rel, d):
            send(pending, chunk(zz, yy), chunk(zz, yy), (ss_send, (rel, d,)), (ss_recv, (rel, d,)), mate)

        def inject(d):
            for way in range(2):
                ring(z, at_y(d), 1, d, way)
            share(z, at_y(d), 0, d)

        def last_way(d):
            return 0 if d == 1 else 1

        def hop(s, d):
            for way in range(2):
                if s == 4 and way != last_way(d):
                    continue
                rel = (-s if way == 0 else s) % NZ
                zz, yy = at_z(rel), at_y(d)
                if s == 1 and d == 0:
                    for cc in range(2):
                        arrived(kept(zz, yy, cc), (seed_recv, (2 + way, cc,)), (seed_send, (2 + way,)))
                else:
                    arrived(chunk(zz, yy), (sz_recv, (way, s, d,)), (sz_send, (way, s, d,)))
                if (s < 3 and d != 2) or (s == 3 and way == last_way(d)):
                    ring(zz, yy, s + 1, d, way)
                if s >= 2 and d:
                    k = 0 if d == 3 else 1
                    send(
                        pending, kept(zz, yy, k), kept(zz, yy, k), (yf_send, (rel, k,)), (yf_recv, (rel, k,)),
                        dev(z, at_y(sides[k][1]), 0, t),
                    )
                share(zz, yy, rel, d)

        hop(1, 0)
        for k in range(2):
            yy = at_y(-sides[k][1])
            for cc in range(2):
                arrived(kept(z, yy, cc), (seed_recv, (k, cc,)), (seed_send, (k,)))
            send(
                pending, kept(z, yy, k), kept(z, yy, k), (yr_send, (k,)), (yr_recv, (k,)),
                dev(z, at_y(sides[k][1]), 0, t),
            )
            inject(3 if k == 0 else 1)
        hop(2, 0)
        hop(1, 3)
        hop(1, 1)
        for k in range(2):
            arrived(kept(z, at_y(2), k), (yr_recv, (k,)), (yr_send, (k,)))
        inject(2)
        own_copy.wait()
        arrived(kept(z, y, 1), (ss_recv, (0, 0,)), (ss_send, (0, 0,)))
        send(pending, kept(z, y, 0), kept(z, y, 0), (ss_send, (0, 0,)), (ss_recv, (0, 0,)), mate)
        for s, d in (
            (3, 0), (2, 3), (2, 1), (1, 2), (4, 0), (3, 3), (3, 1), (4, 3), (4, 1),
        ):
            hop(s, d)
        for rel in (6, 2, 5, 3, 4):
            for k in range(2):
                arrived(kept(at_z(rel), at_y(2), k), (yf_recv, (rel, k,)), (yf_send, (rel, k,)))
            share(at_z(rel), at_y(2), rel, 2)
        for d in range(NY):
            arrived(column(at_y(d)), (fs_recv, (d,)), (fs_send, (d,)))

    @pl.when(c == 1)
    def _():
        pending = sent[1]
        mate = dev(z, y, 0, t)
        own_x = pltpu.make_async_copy(x_ref.at[y], xpiece(t, y, 1), local_sem.at[len(loads)])
        own_w = pltpu.make_async_copy(w_ref, wpiece(y, 1), local_sem.at[len(loads) + 1])
        own_copy = pltpu.make_async_copy(own_rows, kept(z, y, 1), local_sem.at[len(loads) + 2])
        own_x.start()
        own_w.start()
        own_copy.start()
        send(pending, own_rows, kept(z, y, 1), (ss_send, (0, 0,)), (ss_recv, (0, 0,)), mate)
        own_x.wait()
        arrived(xpiece(t, y, 0), (xy_recv, (0, 0,)), (xy_send, (0,)))
        for k, (dy, dl) in enumerate(line[1:]):
            for cc in range(2):
                arrived(xpiece(other(dl) * 4 + x, at_y(-dy), cc), (xy_recv, (k + 1, cc,)), (xy_send, (k + 1,)))
        xall = xbuf.reshape(2, 4, 2, SEL, 8 * HD)
        for k in range(1, NX):
            send(
                pending, xall.at[:, x], xall.at[:, x], (xx_send, (k,)), (xx_recv, (k,)), (r, ylo * 4 + at_x(k))
            )
        for k in range(2):
            yy = at_y(-sides[k][1])
            for cc in range(2):
                arrived(wpiece(yy, cc), (w_recv, (k, cc,)), (w_send, (k,)))
            send(
                pending, wpiece(yy, k), wpiece(yy, k), (wr_send, (k,)), (wr_recv, (k,)),
                dev(z, at_y(sides[k][1]), 1, t),
            )
        for cc in range(2):
            for k in range(SEL):
                position = sel_ref[k, r - 1 + cc]
                trig_c[cc, pl.ds(k, 1), :] = cos_ref[pl.ds(position, 1), :]
                trig_s[cc, pl.ds(k, 1), :] = sin_ref[pl.ds(position, 1), :]
        own_w.wait()
        arrived(wpiece(y, 0), (w_recv, (2, 0,)), (w_send, (2,)))
        for k in range(1, NX):
            arrived(xall.at[:, at_x(-k)], (xx_recv, (k,)), (xx_send, (k,)))
        for k in range(2):
            arrived(wpiece(at_y(2), k), (wr_recv, (k,)), (wr_send, (k,)))
        part = jnp.dot(
            xbuf[...].reshape(NZ * 2 * SEL, 8 * HD),
            wbuf[...].reshape(8 * HD, KV),
            preferred_element_type=jnp.float32,
        )
        zsum[...] = part.reshape(NZ, 2, SEL, KV)
        for k in (4, 3, 5, 2, 6, 1, 7):
            send(
                pending, zsum.at[at_z(k)], zrecv.at[k], (rz_send, (k,)), (rz_recv, (k,)), dev(at_z(k), y, 1, t)
            )
        total = zsum[z]
        for k in range(1, NZ):
            arrived(zrecv.at[k], (rz_recv, (k,)), (rz_send, (k,)))
            total = total + zrecv[k]
        fresh = total.astype(jnp.bfloat16).astype(jnp.float32)
        for cc in range(2):
            keys = fresh[cc, :, :HD]
            keys = keys * trig_c[cc] + pltpu.roll(keys, HD // 2, 1) * trig_s[cc]
            own_fresh[cc, :, :HD] = keys.astype(jnp.bfloat16)
            own_fresh[cc, :, HD:] = fresh[cc, :, HD:].astype(jnp.bfloat16)
        for k in (1, 7, 2, 6, 3, 5, 4):
            send(pending, own_fresh, piece(z, y), (fz_send, (k,)), (fz_recv, (k,)), dev(at_z(k), y, 1, t))
        keep_fresh = pltpu.make_async_copy(own_fresh, piece(z, y), local_sem.at[len(loads) + 3])
        keep_fresh.start()
        def share(d):
            send(pending, column(at_y(d)), column(at_y(d)), (fs_send, (d,)), (fs_recv, (d,)), mate)

        near_first = (0, 1, 7, 2, 6, 3, 5, 4)
        for rel in near_first:
            here = piece(at_z(-rel), y)
            if rel:
                arrived(here, (fz_recv, (rel,)), (fz_send, (rel,)))
            for k in range(2):
                send(
                    pending, here if rel else own_fresh, here, (fy_send, (rel, k,)), (fy_recv, (rel, k,)),
                    dev(z, at_y(sides[k][1]), 1, t),
                )
        keep_fresh.wait()
        share(0)
        for rel in near_first:
            zz = at_z(-rel)
            for k in range(2):
                yy = at_y(-sides[k][1])
                arrived(piece(zz, yy), (fy_recv, (rel, k,)), (fy_send, (rel, k,)))
                send(
                    pending, half_piece(zz, yy, k), half_piece(zz, yy, k), (fr_send, (rel, k,)), (fr_recv, (rel, k,)),
                    dev(z, at_y(sides[k][1]), 1, t),
                )
        share(3)
        share(1)
        for rel in near_first:
            for k in range(2):
                arrived(half_piece(at_z(-rel), at_y(2), k), (fr_recv, (rel, k,)), (fr_send, (rel, k,)))
        share(2)
        own_copy.wait()
        arrived(kept(z, y, 0), (ss_recv, (0, 0,)), (ss_send, (0, 0,)))
        for rel in range(NZ):
            for d in range(NY):
                if rel or d:
                    arrived(chunk(at_z(rel), at_y(d)), (ss_recv, (rel, d,)), (ss_send, (rel, d,)))

    kbufs, vbufs, sbufs, pbufs = (kbuf0, kbuf1), (vbuf0, vbuf1), (sbuf0, sbuf1), (pbuf0, pbuf1)
    steps = q_ref.shape[0] // PAIR

    def result_copy(step):
        rows = pl.ds(step * PAIR, PAIR)
        return pltpu.make_async_copy(out_ref.at[rows], out_hbm.at[rows], out_sem.at[step])

    col = lax.broadcasted_iota(jnp.int32, (CHUNK, 128), 1)
    token = lax.rem(lax.broadcasted_iota(jnp.int32, (CHUNK, 128), 0), QLEN)
    tail = jnp.where(col <= token, jnp.float32(0.0), jnp.float32(NEG))
    for i in range(PAIR):
        kbufs[i][LAST + QLEN :, :] = jnp.zeros((128 - QLEN, HD), jnp.bfloat16)
        vbufs[i][LAST + QLEN :, :] = jnp.zeros((128 - QLEN, HD), jnp.bfloat16)
    for copy in later:
        copy.wait()

    def turn(block, j):
        wide = block.astype(jnp.float32)
        wide = wide * cos_ref[PLEN + j : PLEN + j + 1, :] + pltpu.roll(wide, HD // 2, 1) * sin_ref[PLEN + j : PLEN + j + 1, :]
        return wide.astype(jnp.bfloat16)

    def pair(step, carry):
        for i in range(PAIR):
            kbuf, vbuf = kbufs[i], vbufs[i]
            request = step * PAIR + i
            for j in range(SLOTS):
                o = owner_ref[chosen_ref[j, request]]
                block = pas[o // 8, lax.rem(o, 8) // 2, lax.rem(o, 2)]
                keys = block[:, :HD]
                kbuf[j * PLEN : (j + 1) * PLEN, :] = turn(keys, j) if j else keys
                vbuf[j * PLEN : (j + 1) * PLEN, :] = block[:, HD:]
            own = own_ref[request]
            kbuf[LAST : LAST + QLEN, :] = own[:, :HD]
            vbuf[LAST : LAST + QLEN, :] = own[:, HD:]
        for i in range(PAIR):
            query = q_ref[step * PAIR + i]
            query = jnp.concatenate([query[:, h * HD : (h + 1) * HD] for h in range(GROUP)], 0)
            sbufs[i][...] = lax.dot_general(
                query, kbufs[i][...], (((1,), (1,)), ((), ())), preferred_element_type=jnp.float32
            )
        for i in range(PAIR):
            sbuf, pbuf = sbufs[i], pbufs[i]
            for first in range(0, GROUP * QLEN, CHUNK):
                rows = slice(first, first + CHUNK)
                raw = jnp.concatenate([sbuf[rows, :LAST], sbuf[rows, LAST:] + tail], 1)
                expo = jnp.exp2((raw - jnp.max(raw, 1, keepdims=True)) * SCALE)
                pbuf[rows, :] = (expo * (1.0 / jnp.sum(expo, 1, keepdims=True))).astype(jnp.bfloat16)
            result = jnp.dot(pbuf[...], vbufs[i][...], preferred_element_type=jnp.float32).astype(jnp.bfloat16)
            for h in range(GROUP):
                out_ref[step * PAIR + i, :, h * HD : (h + 1) * HD] = result[h * QLEN : (h + 1) * QLEN]
        result_copy(step).start()
        return carry

    lax.fori_loop(0, steps, pair, 0)
    for step in range(steps):
        result_copy(step).wait()
    drain(started)
    for core in range(2):

        @pl.when(c == core)
        def _(core=core):
            drain(sent[core])


def local(stale, fresh_input, kv_weight, sel_index, owner, retrieval, queries, question_kv):
    cosine, sine = trig_tables()
    any_spec = pl.BlockSpec(memory_space=pl.ANY)
    dma = pltpu.SemaphoreType.DMA
    rows = GROUP * QLEN
    return pl.pallas_call(
        kernel,
        out_shape=jax.ShapeDtypeStruct(queries.shape, jnp.bfloat16),
        in_specs=[any_spec] * 10,
        out_specs=any_spec,
        scratch_shapes=[
            pltpu.VMEM((NZ, NY, 2, PLEN, KV), jnp.bfloat16),
            pltpu.VMEM((KEYS, HD), jnp.bfloat16),
            pltpu.VMEM((KEYS, HD), jnp.bfloat16),
            pltpu.VMEM((KEYS, HD), jnp.bfloat16),
            pltpu.VMEM((KEYS, HD), jnp.bfloat16),
            pltpu.VMEM((rows, KEYS), jnp.float32),
            pltpu.VMEM((rows, KEYS), jnp.bfloat16),
            pltpu.VMEM((rows, KEYS), jnp.float32),
            pltpu.VMEM((rows, KEYS), jnp.bfloat16),
            pltpu.VMEM(queries.shape, jnp.bfloat16),
            pltpu.VMEM(question_kv.shape, jnp.bfloat16),
            pltpu.VMEM(queries.shape, jnp.bfloat16),
            pltpu.SMEM((64,), jnp.int32),
            pltpu.SMEM((SLOTS, 8), jnp.int32),
            pltpu.VMEM((PLEN, KV), jnp.bfloat16),
            pltpu.VMEM((KEPT, KV), jnp.bfloat16),
            pltpu.VMEM((2, SEL, KV), jnp.bfloat16),
            pltpu.VMEM((8, 2, SEL, 8 * HD), jnp.bfloat16),
            pltpu.VMEM((NY, 2, HD, KV), jnp.bfloat16),
            pltpu.VMEM((NZ, 2, SEL, KV), jnp.float32),
            pltpu.VMEM((NZ, 2, SEL, KV), jnp.float32),
            pltpu.VMEM((2, SEL, HD), jnp.float32),
            pltpu.VMEM((2, SEL, HD), jnp.float32),
            pltpu.VMEM((NY, 2, SEL, HD), jnp.bfloat16),
            pltpu.VMEM((HD, KV), jnp.bfloat16),
            pltpu.VMEM(cosine.shape, jnp.float32),
            pltpu.VMEM(sine.shape, jnp.float32),
            pltpu.SMEM((SEL, 64), jnp.int32),
            dma((12,)),
            dma((8,)), dma((8, 2)),
            dma((NX,)), dma((NX,)),
            dma((3,)), dma((3, 2)),
            dma((2,)), dma((2,)),
            dma((4,)), dma((4, 2)),
            dma((2,)), dma((2,)),
            dma((NZ, 2)), dma((NZ, 2)),
            dma((2, 5, NY)), dma((2, 5, NY)),
            dma((NZ, NY)), dma((NZ, NY)),
            dma((NZ,)), dma((NZ,)),
            dma((NZ,)), dma((NZ,)),
            dma((NZ, 2)), dma((NZ, 2)),
            dma((NZ, 2)), dma((NZ, 2)),
            dma((NY,)), dma((NY,)),
            dma((2,)), dma((4,)),
        ],
        compiler_params=pltpu.CompilerParams(
            collective_id=0, has_side_effects=True, vmem_limit_bytes=62 * 1024 * 1024
        ),
    )(
        stale,
        fresh_input.reshape(NY, 2, SEL, HD),
        kv_weight,
        sel_index.T,
        jnp.asarray(cosine),
        jnp.asarray(sine),
        owner,
        retrieval.T,
        queries,
        question_kv,
    )


def solution(mesh):
    return jax.shard_map(
        local,
        mesh=mesh,
        in_specs=(
            P("req", None, "tp"),
            P("tp", None, "req"),
            P("req", None),
            P(),
            P(),
            P("req", None),
            P("req", None, "tp"),
            P("req", None, "tp"),
        ),
        out_specs=P("req", None, "tp"),
        check_vma=False,
    )
```

```python
import functools
import math

import jax
import jax.numpy as jnp
import numpy as np
from jax import lax
from jax.experimental import pallas as pl
from jax.experimental.pallas import tpu as pltpu
from jax.sharding import PartitionSpec as P

MESH = pl.DeviceIdType.MESH
HD = 128
NZ, NY, NX = 8, 4, 4
PLEN, QLEN, SEL, SLOTS = 128, 32, 16, 4
GROUP = 8
KV = 2 * HD
LAST = SLOTS * PLEN
KEYS = LAST + 128
KEPT = PLEN - SEL
CHUNK = 64
SCALE = math.log2(math.e) / math.sqrt(HD)
NEG = -1e30
THETA = 500000.0
PAIR = 2


def trig_tables():
    positions = np.concatenate([np.arange(PLEN), np.arange(8) * PLEN]).astype(np.float32)
    freqs = (THETA ** (-(np.arange(HD // 2, dtype=np.float64) * 2.0 / HD))).astype(np.float32)
    angle = (positions[:, None] * freqs).astype(np.float32).astype(np.float64)
    cosine, sine = np.cos(angle), np.sin(angle)
    return (
        np.concatenate([cosine, cosine], -1).astype(np.float32),
        np.concatenate([-sine, sine], -1).astype(np.float32),
    )


def kernel(
    stale_hbm, x_hbm, w_hbm, sel_hbm, cos_hbm, sin_hbm, owner_hbm, chosen_hbm, q_hbm, own_hbm,
    out_hbm,
    pas, kbuf0, vbuf0, kbuf1, vbuf1, sbuf0, pbuf0, sbuf1, pbuf1, q_ref, own_ref, out_ref, owner_ref, chosen_ref,
    stale_ref, own_rows, own_fresh, xbuf, wbuf, zsum, zrecv, trig_c, trig_s, x_ref, w_ref, cos_ref, sin_ref, sel_ref,
    local_sem, xy_send, xy_recv, xx_send, xx_recv, w_send, w_recv, wr_send, wr_recv,
    seed_send, seed_recv, yr_send, yr_recv, yf_send, yf_recv, sz_send, sz_recv, ss_send, ss_recv,
    rz_send, rz_recv, fz_send, fz_recv, fy_send, fy_recv, fr_send, fr_recv, fs_send, fs_recv, q_sem, out_sem,
):
    r, t = lax.axis_index("req"), lax.axis_index("tp")
    z, y, c = r // 8, lax.rem(r, 8) // 2, lax.rem(r, 2)
    ylo, x = t // 4, lax.rem(t, 4)

    def dev(zz, yy, cc, tt):
        return (zz * 8 + yy * 2 + cc, tt)

    def at_z(k):
        return lax.rem(z + k + 2 * NZ, NZ)

    def at_y(k):
        return lax.rem(y + k + 2 * NY, NY)

    def at_x(k):
        return lax.rem(x + k + 2 * NX, NX)

    def other(dl):
        return lax.rem(ylo + dl, 2)

    def remote(src, dst, send_sem, recv_sem, device):
        return pltpu.make_async_remote_copy(
            src_ref=src, dst_ref=dst, send_sem=send_sem[0].at[send_sem[1]], recv_sem=recv_sem[0].at[recv_sem[1]],
            device_id=device, device_id_type=MESH,
        )

    def arrived(dst, recv_sem, send_sem):
        remote(dst, dst, send_sem, recv_sem, dev(z, y, 1 - c, t)).wait_recv()

    def send(pending, src, dst, send_sem, recv_sem, device):
        remote(src, dst, send_sem, recv_sem, device).start()
        pending.append((tuple(src.shape), jnp.dtype(src.dtype), send_sem, recv_sem))

    def drain(pending):
        shapes = [
            pas.at[0, 0, :, pl.ds(0, KEPT)], pas.at[0, 0, 0, pl.ds(0, KEPT)], pas.at[:, 0, :, pl.ds(KEPT, SEL)],
            pas.at[0, 0, :, pl.ds(KEPT, SEL)], pas.at[0, 0, 0, pl.ds(KEPT, SEL)], x_ref.at[0], w_ref,
            xbuf.reshape(2, 4, 2, SEL, 8 * HD).at[:, 0], zsum.at[0],
        ]
        kinds = {(tuple(ref.shape), jnp.dtype(ref.dtype)): ref for ref in shapes}
        for shape, kind, send_sem, recv_sem in pending:
            ref = kinds[shape, kind]
            remote(ref, ref, send_sem, recv_sem, dev(z, y, 1 - c, t)).wait_send()

    sent = [[], []]

    line = [(dy, dl) for dy in range(NY) for dl in range(2)]
    sides = [(0, 1), (0, -1), (1, 0), (-1, 0)]

    barrier = pltpu.get_barrier_semaphore()

    def greet(device):
        pl.semaphore_signal(barrier, inc=1, device_id=device, device_id_type=MESH)

    @pl.when(c == 0)
    def _():
        for dz, dy in sides:
            for cc in range(2):
                greet(dev(at_z(dz), at_y(dy), cc, t))
        greet(dev(z, y, 1, t))

    @pl.when(c == 1)
    def _():
        for dy, dl in line[1:]:
            for cc in range(2):
                greet(dev(z, at_y(dy), cc, other(dl) * 4 + x))
        greet(dev(z, y, 0, t))
        for k in range(1, NX):
            greet((r, ylo * 4 + at_x(k)))
        for k in range(1, NZ):
            greet(dev(at_z(k), y, 1, t))

    columns = pl.ds(pl.multiple_of(t * KV, KV), KV)

    def chunk(zz, yy):
        return pas.at[zz, yy, :, pl.ds(0, KEPT)]

    def kept(zz, yy, cc):
        return pas.at[zz, yy, cc, pl.ds(0, KEPT)]

    def column(yy):
        return pas.at[:, yy, :, pl.ds(KEPT, SEL)]

    def piece(zz, yy):
        return pas.at[zz, yy, :, pl.ds(KEPT, SEL)]

    def half_piece(zz, yy, cc):
        return pas.at[zz, yy, cc, pl.ds(KEPT, SEL)]

    def xpiece(ts, ys, cs):
        return xbuf.at[ts, :, :, pl.ds(pl.multiple_of((ys * 2 + cs) * HD, HD), HD)]

    def wpiece(ys, cs):
        return wbuf.at[ys, cs]

    loads = []

    def load(source, target):
        copy = pltpu.make_async_copy(source, target, local_sem.at[len(loads)])
        copy.start()
        loads.append(copy)
        return copy

    load_sel = load(sel_hbm, sel_ref)
    load_stale = load(stale_hbm.at[0], stale_ref)
    load_x = load(x_hbm, x_ref)
    load_w = load(w_hbm.at[:, columns], w_ref)
    load_cos = load(cos_hbm, cos_ref)
    load_sin = load(sin_hbm, sin_ref)
    load_owner = load(owner_hbm, owner_ref)
    load_chosen = load(chosen_hbm, chosen_ref)
    later = []
    for k, (source, target) in enumerate(((q_hbm, q_ref), (own_hbm, own_ref))):
        later.append(pltpu.make_async_copy(source, target, q_sem.at[k]))
        later[-1].start()

    load_x.wait()

    @pl.when(c == 0)
    def _():
        pl.semaphore_wait(barrier, 12)

    @pl.when(c == 1)
    def _():
        pl.semaphore_wait(barrier, 22)

    started = []
    for k, (dy, dl) in enumerate(line[1:]):
        send(
            started, x_ref.at[at_y(dy)], xpiece(t, y, c), (xy_send, (k + 1,)), (xy_recv, (k + 1, c,)),
            dev(z, at_y(dy), 1, other(dl) * 4 + x),
        )
    load_sel.wait()
    lane = lax.broadcasted_iota(jnp.int32, (8, PLEN), 1)
    hit = lane == sel_ref[0, r]
    for k in range(1, SEL):
        hit = hit | (lane == sel_ref[k, r])
    keep = jnp.where(hit, jnp.float32(0.0), jnp.float32(1.0))
    before = lax.broadcasted_iota(jnp.int32, (PLEN, PLEN), 0) < lax.broadcasted_iota(jnp.int32, (PLEN, PLEN), 1)
    rank = jnp.dot(
        keep.astype(jnp.bfloat16),
        jnp.where(before, jnp.float32(1.0), jnp.float32(0.0)).astype(jnp.bfloat16),
        preferred_element_type=jnp.float32,
    )
    order = lax.broadcasted_iota(jnp.int32, (KEPT, PLEN), 0).astype(jnp.float32)
    picked = jnp.where(order == rank[0:1], keep[0:1], jnp.float32(0.0)).astype(jnp.bfloat16)
    load_stale.wait()
    own_rows[...] = jnp.dot(picked, stale_ref[...], preferred_element_type=jnp.float32).astype(jnp.bfloat16)
    for k in (2, 3, 0, 1):
        dz, dy = sides[k]
        send(
            started, own_rows, kept(z, y, c), (seed_send, (k,)), (seed_recv, (k, c,)), dev(at_z(dz), at_y(dy), 0, t)
        )
    load_w.wait()
    for k in range(2):
        send(
            started, w_ref, wpiece(y, c), (w_send, (k,)), (w_recv, (k, c,)), dev(z, at_y(sides[k][1]), 1, t)
        )

    for copy in (load_cos, load_sin, load_owner, load_chosen):
        copy.wait()

    @pl.when(c == 0)
    def _():
        pending = sent[0]
        mate = dev(z, y, 1, t)
        send(pending, x_ref.at[y], xpiece(t, y, 0), (xy_send, (0,)), (xy_recv, (0, 0,)), mate)
        send(pending, w_ref, wpiece(y, 0), (w_send, (2,)), (w_recv, (2, 0,)), mate)
        own_copy = pltpu.make_async_copy(own_rows, kept(z, y, 0), local_sem.at[len(loads)])
        own_copy.start()

        def ring(zz, yy, s, d, way):
            step = 1 if way == 0 else -1
            send(
                pending, chunk(zz, yy), chunk(zz, yy), (sz_send, (way, s, d,)), (sz_recv, (way, s, d,)),
                dev(at_z(step), y, 0, t),
            )

        def share(zz, yy, rel, d):
            send(pending, chunk(zz, yy), chunk(zz, yy), (ss_send, (rel, d,)), (ss_recv, (rel, d,)), mate)

        def inject(d):
            for way in range(2):
                ring(z, at_y(d), 1, d, way)
            share(z, at_y(d), 0, d)

        def last_way(d):
            return 0 if d == 1 else 1

        def hop(s, d):
            for way in range(2):
                if s == 4 and way != last_way(d):
                    continue
                rel = (-s if way == 0 else s) % NZ
                zz, yy = at_z(rel), at_y(d)
                if s == 1 and d == 0:
                    for cc in range(2):
                        arrived(kept(zz, yy, cc), (seed_recv, (2 + way, cc,)), (seed_send, (2 + way,)))
                else:
                    arrived(chunk(zz, yy), (sz_recv, (way, s, d,)), (sz_send, (way, s, d,)))
                if (s < 3 and d != 2) or (s == 3 and way == last_way(d)):
                    ring(zz, yy, s + 1, d, way)
                if s >= 2 and d:
                    k = 0 if d == 3 else 1
                    send(
                        pending, kept(zz, yy, k), kept(zz, yy, k), (yf_send, (rel, k,)), (yf_recv, (rel, k,)),
                        dev(z, at_y(sides[k][1]), 0, t),
                    )
                share(zz, yy, rel, d)

        hop(1, 0)
        for k in range(2):
            yy = at_y(-sides[k][1])
            for cc in range(2):
                arrived(kept(z, yy, cc), (seed_recv, (k, cc,)), (seed_send, (k,)))
            send(
                pending, kept(z, yy, k), kept(z, yy, k), (yr_send, (k,)), (yr_recv, (k,)),
                dev(z, at_y(sides[k][1]), 0, t),
            )
            inject(3 if k == 0 else 1)
        hop(2, 0)
        hop(1, 3)
        hop(1, 1)
        for k in range(2):
            arrived(kept(z, at_y(2), k), (yr_recv, (k,)), (yr_send, (k,)))
        inject(2)
        own_copy.wait()
        arrived(kept(z, y, 1), (ss_recv, (0, 0,)), (ss_send, (0, 0,)))
        send(pending, kept(z, y, 0), kept(z, y, 0), (ss_send, (0, 0,)), (ss_recv, (0, 0,)), mate)
        for s, d in (
            (3, 0), (2, 3), (2, 1), (1, 2), (4, 0), (3, 3), (3, 1), (4, 3), (4, 1),
        ):
            hop(s, d)
        for rel in (6, 2, 5, 3, 4):
            for k in range(2):
                arrived(kept(at_z(rel), at_y(2), k), (yf_recv, (rel, k,)), (yf_send, (rel, k,)))
            share(at_z(rel), at_y(2), rel, 2)
        for d in range(NY):
            arrived(column(at_y(d)), (fs_recv, (d,)), (fs_send, (d,)))

    @pl.when(c == 1)
    def _():
        pending = sent[1]
        mate = dev(z, y, 0, t)
        own_x = pltpu.make_async_copy(x_ref.at[y], xpiece(t, y, 1), local_sem.at[len(loads)])
        own_w = pltpu.make_async_copy(w_ref, wpiece(y, 1), local_sem.at[len(loads) + 1])
        own_copy = pltpu.make_async_copy(own_rows, kept(z, y, 1), local_sem.at[len(loads) + 2])
        own_x.start()
        own_w.start()
        own_copy.start()
        send(pending, own_rows, kept(z, y, 1), (ss_send, (0, 0,)), (ss_recv, (0, 0,)), mate)
        own_x.wait()
        arrived(xpiece(t, y, 0), (xy_recv, (0, 0,)), (xy_send, (0,)))
        for k, (dy, dl) in enumerate(line[1:]):
            for cc in range(2):
                arrived(xpiece(other(dl) * 4 + x, at_y(-dy), cc), (xy_recv, (k + 1, cc,)), (xy_send, (k + 1,)))
        xall = xbuf.reshape(2, 4, 2, SEL, 8 * HD)
        for k in range(1, NX):
            send(
                pending, xall.at[:, x], xall.at[:, x], (xx_send, (k,)), (xx_recv, (k,)), (r, ylo * 4 + at_x(k))
            )
        for k in range(2):
            yy = at_y(-sides[k][1])
            for cc in range(2):
                arrived(wpiece(yy, cc), (w_recv, (k, cc,)), (w_send, (k,)))
            send(
                pending, wpiece(yy, k), wpiece(yy, k), (wr_send, (k,)), (wr_recv, (k,)),
                dev(z, at_y(sides[k][1]), 1, t),
            )
        for cc in range(2):
            for k in range(SEL):
                position = sel_ref[k, r - 1 + cc]
                trig_c[cc, pl.ds(k, 1), :] = cos_ref[pl.ds(position, 1), :]
                trig_s[cc, pl.ds(k, 1), :] = sin_ref[pl.ds(position, 1), :]
        own_w.wait()
        arrived(wpiece(y, 0), (w_recv, (2, 0,)), (w_send, (2,)))
        for k in range(1, NX):
            arrived(xall.at[:, at_x(-k)], (xx_recv, (k,)), (xx_send, (k,)))
        for k in range(2):
            arrived(wpiece(at_y(2), k), (wr_recv, (k,)), (wr_send, (k,)))
        part = jnp.dot(
            xbuf[...].reshape(NZ * 2 * SEL, 8 * HD),
            wbuf[...].reshape(8 * HD, KV),
            preferred_element_type=jnp.float32,
        )
        zsum[...] = part.reshape(NZ, 2, SEL, KV)
        for k in (4, 3, 5, 2, 6, 1, 7):
            send(
                pending, zsum.at[at_z(k)], zrecv.at[k], (rz_send, (k,)), (rz_recv, (k,)), dev(at_z(k), y, 1, t)
            )
        total = zsum[z]
        for k in range(1, NZ):
            arrived(zrecv.at[k], (rz_recv, (k,)), (rz_send, (k,)))
            total = total + zrecv[k]
        fresh = total.astype(jnp.bfloat16).astype(jnp.float32)
        for cc in range(2):
            keys = fresh[cc, :, :HD]
            keys = keys * trig_c[cc] + pltpu.roll(keys, HD // 2, 1) * trig_s[cc]
            own_fresh[cc, :, :HD] = keys.astype(jnp.bfloat16)
            own_fresh[cc, :, HD:] = fresh[cc, :, HD:].astype(jnp.bfloat16)
        for k in (1, 7, 2, 6, 3, 5, 4):
            send(pending, own_fresh, piece(z, y), (fz_send, (k,)), (fz_recv, (k,)), dev(at_z(k), y, 1, t))
        keep_fresh = pltpu.make_async_copy(own_fresh, piece(z, y), local_sem.at[len(loads) + 3])
        keep_fresh.start()
        def share(d):
            send(pending, column(at_y(d)), column(at_y(d)), (fs_send, (d,)), (fs_recv, (d,)), mate)

        near_first = (0, 1, 7, 2, 6, 3, 5, 4)
        for rel in near_first:
            here = piece(at_z(-rel), y)
            if rel:
                arrived(here, (fz_recv, (rel,)), (fz_send, (rel,)))
            for k in range(2):
                send(
                    pending, here if rel else own_fresh, here, (fy_send, (rel, k,)), (fy_recv, (rel, k,)),
                    dev(z, at_y(sides[k][1]), 1, t),
                )
        keep_fresh.wait()
        share(0)
        for rel in near_first:
            zz = at_z(-rel)
            for k in range(2):
                yy = at_y(-sides[k][1])
                arrived(piece(zz, yy), (fy_recv, (rel, k,)), (fy_send, (rel, k,)))
                send(
                    pending, half_piece(zz, yy, k), half_piece(zz, yy, k), (fr_send, (rel, k,)), (fr_recv, (rel, k,)),
                    dev(z, at_y(sides[k][1]), 1, t),
                )
        share(3)
        share(1)
        for rel in near_first:
            for k in range(2):
                arrived(half_piece(at_z(-rel), at_y(2), k), (fr_recv, (rel, k,)), (fr_send, (rel, k,)))
        share(2)
        own_copy.wait()
        arrived(kept(z, y, 0), (ss_recv, (0, 0,)), (ss_send, (0, 0,)))
        for rel in range(NZ):
            for d in range(NY):
                if rel or d:
                    arrived(chunk(at_z(rel), at_y(d)), (ss_recv, (rel, d,)), (ss_send, (rel, d,)))

    kbufs, vbufs, sbufs, pbufs = (kbuf0, kbuf1), (vbuf0, vbuf1), (sbuf0, sbuf1), (pbuf0, pbuf1)
    steps = q_ref.shape[0] // PAIR

    def result_copy(step):
        rows = pl.ds(step * PAIR, PAIR)
        return pltpu.make_async_copy(out_ref.at[rows], out_hbm.at[rows], out_sem.at[step])

    col = lax.broadcasted_iota(jnp.int32, (CHUNK, 128), 1)
    token = lax.rem(lax.broadcasted_iota(jnp.int32, (CHUNK, 128), 0), QLEN)
    tail = jnp.where(col <= token, jnp.float32(0.0), jnp.float32(NEG))
    for i in range(PAIR):
        kbufs[i][LAST + QLEN :, :] = jnp.zeros((128 - QLEN, HD), jnp.bfloat16)
        vbufs[i][LAST + QLEN :, :] = jnp.zeros((128 - QLEN, HD), jnp.bfloat16)
    for copy in later:
        copy.wait()

    def turn(block, j):
        wide = block.astype(jnp.float32)
        wide = wide * cos_ref[PLEN + j : PLEN + j + 1, :] + pltpu.roll(wide, HD // 2, 1) * sin_ref[PLEN + j : PLEN + j + 1, :]
        return wide.astype(jnp.bfloat16)

    def pair(step, carry):
        for i in range(PAIR):
            kbuf, vbuf = kbufs[i], vbufs[i]
            request = step * PAIR + i
            for j in range(SLOTS):
                o = owner_ref[chosen_ref[j, request]]
                block = pas[o // 8, lax.rem(o, 8) // 2, lax.rem(o, 2)]
                keys = block[:, :HD]
                kbuf[j * PLEN : (j + 1) * PLEN, :] = turn(keys, j) if j else keys
                vbuf[j * PLEN : (j + 1) * PLEN, :] = block[:, HD:]
            own = own_ref[request]
            kbuf[LAST : LAST + QLEN, :] = own[:, :HD]
            vbuf[LAST : LAST + QLEN, :] = own[:, HD:]
        for i in range(PAIR):
            query = q_ref[step * PAIR + i]
            query = jnp.concatenate([query[:, h * HD : (h + 1) * HD] for h in range(GROUP)], 0)
            sbufs[i][...] = lax.dot_general(
                query, kbufs[i][...], (((1,), (1,)), ((), ())), preferred_element_type=jnp.float32
            )
        for i in range(PAIR):
            sbuf, pbuf = sbufs[i], pbufs[i]
            for first in range(0, GROUP * QLEN, CHUNK):
                rows = slice(first, first + CHUNK)
                raw = jnp.concatenate([sbuf[rows, :LAST], sbuf[rows, LAST:] + tail], 1)
                expo = jnp.exp2((raw - jnp.max(raw, 1, keepdims=True)) * SCALE)
                pbuf[rows, :] = (expo * (1.0 / jnp.sum(expo, 1, keepdims=True))).astype(jnp.bfloat16)
            result = jnp.dot(pbuf[...], vbufs[i][...], preferred_element_type=jnp.float32)
            for h in range(GROUP):
                out_ref[step * PAIR + i, :, h * HD : (h + 1) * HD] = result[h * QLEN : (h + 1) * QLEN]
        result_copy(step).start()
        return carry

    lax.fori_loop(0, steps, pair, 0)
    for step in range(steps):
        result_copy(step).wait()
    drain(started)
    for core in range(2):

        @pl.when(c == core)
        def _(core=core):
            drain(sent[core])


def local(stale, fresh_input, kv_weight, sel_index, owner, retrieval, queries, question_kv):
    cosine, sine = trig_tables()
    any_spec = pl.BlockSpec(memory_space=pl.ANY)
    dma = pltpu.SemaphoreType.DMA
    rows = GROUP * QLEN
    return pl.pallas_call(
        kernel,
        out_shape=jax.ShapeDtypeStruct(queries.shape, jnp.float32),
        in_specs=[any_spec] * 10,
        out_specs=any_spec,
        scratch_shapes=[
            pltpu.VMEM((NZ, NY, 2, PLEN, KV), jnp.bfloat16),
            pltpu.VMEM((KEYS, HD), jnp.bfloat16),
            pltpu.VMEM((KEYS, HD), jnp.bfloat16),
            pltpu.VMEM((KEYS, HD), jnp.bfloat16),
            pltpu.VMEM((KEYS, HD), jnp.bfloat16),
            pltpu.VMEM((rows, KEYS), jnp.float32),
            pltpu.VMEM((rows, KEYS), jnp.bfloat16),
            pltpu.VMEM((rows, KEYS), jnp.float32),
            pltpu.VMEM((rows, KEYS), jnp.bfloat16),
            pltpu.VMEM(queries.shape, jnp.bfloat16),
            pltpu.VMEM(question_kv.shape, jnp.bfloat16),
            pltpu.VMEM(queries.shape, jnp.float32),
            pltpu.SMEM((64,), jnp.int32),
            pltpu.SMEM((SLOTS, 8), jnp.int32),
            pltpu.VMEM((PLEN, KV), jnp.bfloat16),
            pltpu.VMEM((KEPT, KV), jnp.bfloat16),
            pltpu.VMEM((2, SEL, KV), jnp.bfloat16),
            pltpu.VMEM((8, 2, SEL, 8 * HD), jnp.bfloat16),
            pltpu.VMEM((NY, 2, HD, KV), jnp.bfloat16),
            pltpu.VMEM((NZ, 2, SEL, KV), jnp.float32),
            pltpu.VMEM((NZ, 2, SEL, KV), jnp.float32),
            pltpu.VMEM((2, SEL, HD), jnp.float32),
            pltpu.VMEM((2, SEL, HD), jnp.float32),
            pltpu.VMEM((NY, 2, SEL, HD), jnp.bfloat16),
            pltpu.VMEM((HD, KV), jnp.bfloat16),
            pltpu.VMEM(cosine.shape, jnp.float32),
            pltpu.VMEM(sine.shape, jnp.float32),
            pltpu.SMEM((SEL, 64), jnp.int32),
            dma((12,)),
            dma((8,)), dma((8, 2)),
            dma((NX,)), dma((NX,)),
            dma((3,)), dma((3, 2)),
            dma((2,)), dma((2,)),
            dma((4,)), dma((4, 2)),
            dma((2,)), dma((2,)),
            dma((NZ, 2)), dma((NZ, 2)),
            dma((2, 5, NY)), dma((2, 5, NY)),
            dma((NZ, NY)), dma((NZ, NY)),
            dma((NZ,)), dma((NZ,)),
            dma((NZ,)), dma((NZ,)),
            dma((NZ, 2)), dma((NZ, 2)),
            dma((NZ, 2)), dma((NZ, 2)),
            dma((NY,)), dma((NY,)),
            dma((2,)), dma((4,)),
        ],
        compiler_params=pltpu.CompilerParams(
            collective_id=0, has_side_effects=True, vmem_limit_bytes=62 * 1024 * 1024
        ),
    )(
        stale,
        fresh_input.reshape(NY, 2, SEL, HD),
        kv_weight,
        sel_index.T,
        jnp.asarray(cosine),
        jnp.asarray(sine),
        owner,
        retrieval.T,
        queries,
        question_kv,
    ).astype(jnp.bfloat16)


def solution(mesh):
    return jax.shard_map(
        local,
        mesh=mesh,
        in_specs=(
            P("req", None, "tp"),
            P("tp", None, "req"),
            P("req", None),
            P(),
            P(),
            P("req", None),
            P("req", None, "tp"),
            P("req", None, "tp"),
        ),
        out_specs=P("req", None, "tp"),
        check_vma=False,
    )
```

```python
import functools
import math

import jax
import jax.numpy as jnp
import numpy as np
from jax import lax
from jax.experimental import pallas as pl
from jax.experimental.pallas import tpu as pltpu
from jax.sharding import PartitionSpec as P

MESH = pl.DeviceIdType.MESH
HD = 128
NZ, NY, NX = 8, 4, 4
PLEN, QLEN, SEL, SLOTS = 128, 32, 16, 4
GROUP = 8
KV = 2 * HD
LAST = SLOTS * PLEN
KEYS = LAST + 128
KEPT = PLEN - SEL
CHUNK = 64
SCALE = math.log2(math.e) / math.sqrt(HD)
NEG = -1e30
THETA = 500000.0
PAIR = 2


def trig_tables():
    positions = np.concatenate([np.arange(PLEN), np.arange(8) * PLEN]).astype(np.float32)
    freqs = (THETA ** (-(np.arange(HD // 2, dtype=np.float64) * 2.0 / HD))).astype(np.float32)
    angle = (positions[:, None] * freqs).astype(np.float32).astype(np.float64)
    cosine, sine = np.cos(angle), np.sin(angle)
    return (
        np.concatenate([cosine, cosine], -1).astype(np.float32),
        np.concatenate([-sine, sine], -1).astype(np.float32),
    )


def kernel(
    stale_hbm, x_hbm, w_hbm, sel_hbm, cos_hbm, sin_hbm, owner_hbm, chosen_hbm, q_hbm, own_hbm,
    out_hbm,
    pas, kbuf0, vbuf0, kbuf1, vbuf1, sbuf0, pbuf0, sbuf1, pbuf1, q_ref, own_ref, out_ref, owner_ref, chosen_ref,
    stale_ref, own_rows, own_fresh, xbuf, wbuf, zsum, zrecv, trig_c, trig_s, x_ref, w_ref, cos_ref, sin_ref, sel_ref,
    local_sem, xy_send, xy_recv, xx_send, xx_recv, w_send, w_recv, wr_send, wr_recv,
    seed_send, seed_recv, yr_send, yr_recv, yf_send, yf_recv, sz_send, sz_recv, ss_send, ss_recv,
    rz_send, rz_recv, fz_send, fz_recv, fy_send, fy_recv, fr_send, fr_recv, fs_send, fs_recv, q_sem, out_sem,
):
    r, t = lax.axis_index("req"), lax.axis_index("tp")
    z, y, c = r // 8, lax.rem(r, 8) // 2, lax.rem(r, 2)
    ylo, x = t // 4, lax.rem(t, 4)

    def dev(zz, yy, cc, tt):
        return (zz * 8 + yy * 2 + cc, tt)

    def at_z(k):
        return lax.rem(z + k + 2 * NZ, NZ)

    def at_y(k):
        return lax.rem(y + k + 2 * NY, NY)

    def at_x(k):
        return lax.rem(x + k + 2 * NX, NX)

    def other(dl):
        return lax.rem(ylo + dl, 2)

    def remote(src, dst, send_sem, recv_sem, device):
        return pltpu.make_async_remote_copy(
            src_ref=src, dst_ref=dst, send_sem=send_sem[0].at[send_sem[1]], recv_sem=recv_sem[0].at[recv_sem[1]],
            device_id=device, device_id_type=MESH,
        )

    def arrived(dst, recv_sem, send_sem):
        remote(dst, dst, send_sem, recv_sem, dev(z, y, 1 - c, t)).wait_recv()

    def send(pending, src, dst, send_sem, recv_sem, device):
        remote(src, dst, send_sem, recv_sem, device).start()
        pending.append((tuple(src.shape), jnp.dtype(src.dtype), send_sem, recv_sem))

    def drain(pending):
        shapes = [
            pas.at[0, 0, :, pl.ds(0, KEPT)], pas.at[0, 0, 0, pl.ds(0, KEPT)], pas.at[:, 0, :, pl.ds(KEPT, SEL)],
            pas.at[0, 0, :, pl.ds(KEPT, SEL)], pas.at[0, 0, 0, pl.ds(KEPT, SEL)], x_ref.at[0], w_ref,
            xbuf.reshape(2, 4, 2, SEL, 8 * HD).at[:, 0], zsum.at[0],
        ]
        kinds = {(tuple(ref.shape), jnp.dtype(ref.dtype)): ref for ref in shapes}
        for shape, kind, send_sem, recv_sem in pending:
            ref = kinds[shape, kind]
            remote(ref, ref, send_sem, recv_sem, dev(z, y, 1 - c, t)).wait_send()

    sent = [[], []]

    line = [(dy, dl) for dy in range(NY) for dl in range(2)]
    sides = [(0, 1), (0, -1), (1, 0), (-1, 0)]

    barrier = pltpu.get_barrier_semaphore()

    def greet(device):
        pl.semaphore_signal(barrier, inc=1, device_id=device, device_id_type=MESH)

    @pl.when(c == 0)
    def _():
        for dz, dy in sides:
            for cc in range(2):
                greet(dev(at_z(dz), at_y(dy), cc, t))
        greet(dev(z, y, 1, t))

    @pl.when(c == 1)
    def _():
        for dy, dl in line[1:]:
            for cc in range(2):
                greet(dev(z, at_y(dy), cc, other(dl) * 4 + x))
        greet(dev(z, y, 0, t))
        for k in range(1, NX):
            greet((r, ylo * 4 + at_x(k)))
        for k in range(1, NZ):
            greet(dev(at_z(k), y, 1, t))

    columns = pl.ds(pl.multiple_of(t * KV, KV), KV)

    def chunk(zz, yy):
        return pas.at[zz, yy, :, pl.ds(0, KEPT)]

    def kept(zz, yy, cc):
        return pas.at[zz, yy, cc, pl.ds(0, KEPT)]

    def column(yy):
        return pas.at[:, yy, :, pl.ds(KEPT, SEL)]

    def piece(zz, yy):
        return pas.at[zz, yy, :, pl.ds(KEPT, SEL)]

    def half_piece(zz, yy, cc):
        return pas.at[zz, yy, cc, pl.ds(KEPT, SEL)]

    def xpiece(ts, ys, cs):
        return xbuf.at[ts, :, :, pl.ds(pl.multiple_of((ys * 2 + cs) * HD, HD), HD)]

    def wpiece(ys, cs):
        return wbuf.at[ys, cs]

    loads = []

    def load(source, target):
        copy = pltpu.make_async_copy(source, target, local_sem.at[len(loads)])
        copy.start()
        loads.append(copy)
        return copy

    load_sel = load(sel_hbm, sel_ref)
    load_stale = load(stale_hbm.at[0], stale_ref)
    load_x = load(x_hbm, x_ref)
    load_w = load(w_hbm.at[:, columns], w_ref)
    load_cos = load(cos_hbm, cos_ref)
    load_sin = load(sin_hbm, sin_ref)
    load_owner = load(owner_hbm, owner_ref)
    load_chosen = load(chosen_hbm, chosen_ref)
    later = []
    for k, (source, target) in enumerate(((q_hbm, q_ref), (own_hbm, own_ref))):
        later.append(pltpu.make_async_copy(source, target, q_sem.at[k]))
        later[-1].start()

    load_x.wait()

    @pl.when(c == 0)
    def _():
        pl.semaphore_wait(barrier, 12)

    @pl.when(c == 1)
    def _():
        pl.semaphore_wait(barrier, 22)

    started = []
    for k, (dy, dl) in enumerate(line[1:]):
        send(
            started, x_ref.at[at_y(dy)], xpiece(t, y, c), (xy_send, (k + 1,)), (xy_recv, (k + 1, c,)),
            dev(z, at_y(dy), 1, other(dl) * 4 + x),
        )
    load_sel.wait()
    lane = lax.broadcasted_iota(jnp.int32, (8, PLEN), 1)
    hit = lane == sel_ref[0, r]
    for k in range(1, SEL):
        hit = hit | (lane == sel_ref[k, r])
    keep = jnp.where(hit, jnp.float32(0.0), jnp.float32(1.0))
    before = lax.broadcasted_iota(jnp.int32, (PLEN, PLEN), 0) < lax.broadcasted_iota(jnp.int32, (PLEN, PLEN), 1)
    rank = jnp.dot(
        keep.astype(jnp.bfloat16),
        jnp.where(before, jnp.float32(1.0), jnp.float32(0.0)).astype(jnp.bfloat16),
        preferred_element_type=jnp.float32,
    )
    order = lax.broadcasted_iota(jnp.int32, (KEPT, PLEN), 0).astype(jnp.float32)
    picked = jnp.where(order == rank[0:1], keep[0:1], jnp.float32(0.0)).astype(jnp.bfloat16)
    load_stale.wait()
    own_rows[...] = jnp.dot(picked, stale_ref[...], preferred_element_type=jnp.float32).astype(jnp.bfloat16)
    for k in (2, 3, 0, 1):
        dz, dy = sides[k]
        send(
            started, own_rows, kept(z, y, c), (seed_send, (k,)), (seed_recv, (k, c,)), dev(at_z(dz), at_y(dy), 0, t)
        )
    load_w.wait()
    for k in range(2):
        send(
            started, w_ref, wpiece(y, c), (w_send, (k,)), (w_recv, (k, c,)), dev(z, at_y(sides[k][1]), 1, t)
        )

    for copy in (load_cos, load_sin, load_owner, load_chosen):
        copy.wait()

    @pl.when(c == 0)
    def _():
        pending = sent[0]
        mate = dev(z, y, 1, t)
        send(pending, x_ref.at[y], xpiece(t, y, 0), (xy_send, (0,)), (xy_recv, (0, 0,)), mate)
        send(pending, w_ref, wpiece(y, 0), (w_send, (2,)), (w_recv, (2, 0,)), mate)
        own_copy = pltpu.make_async_copy(own_rows, kept(z, y, 0), local_sem.at[len(loads)])
        own_copy.start()

        def ring(zz, yy, s, d, way):
            step = 1 if way == 0 else -1
            send(
                pending, chunk(zz, yy), chunk(zz, yy), (sz_send, (way, s, d,)), (sz_recv, (way, s, d,)),
                dev(at_z(step), y, 0, t),
            )

        def share(zz, yy, rel, d):
            send(pending, chunk(zz, yy), chunk(zz, yy), (ss_send, (rel, d,)), (ss_recv, (rel, d,)), mate)

        def inject(d):
            for way in range(2):
                ring(z, at_y(d), 1, d, way)
            share(z, at_y(d), 0, d)

        def last_way(d):
            return 0 if d == 1 else 1

        def hop(s, d):
            for way in range(2):
                if s == 4 and way != last_way(d):
                    continue
                rel = (-s if way == 0 else s) % NZ
                zz, yy = at_z(rel), at_y(d)
                if s == 1 and d == 0:
                    for cc in range(2):
                        arrived(kept(zz, yy, cc), (seed_recv, (2 + way, cc,)), (seed_send, (2 + way,)))
                else:
                    arrived(chunk(zz, yy), (sz_recv, (way, s, d,)), (sz_send, (way, s, d,)))
                if s < (2 if d == 2 else 3) or (s == 3 and way == last_way(d)):
                    ring(zz, yy, s + 1, d, way)
                if s >= 3 and d:
                    k = 0 if d == 3 else 1
                    send(
                        pending, kept(zz, yy, k), kept(zz, yy, k), (yf_send, (rel, k,)), (yf_recv, (rel, k,)),
                        dev(z, at_y(sides[k][1]), 0, t),
                    )
                share(zz, yy, rel, d)

        hop(1, 0)
        for k in range(2):
            yy = at_y(-sides[k][1])
            for cc in range(2):
                arrived(kept(z, yy, cc), (seed_recv, (k, cc,)), (seed_send, (k,)))
            send(
                pending, kept(z, yy, k), kept(z, yy, k), (yr_send, (k,)), (yr_recv, (k,)),
                dev(z, at_y(sides[k][1]), 0, t),
            )
            inject(3 if k == 0 else 1)
        hop(2, 0)
        hop(1, 3)
        hop(1, 1)
        for k in range(2):
            arrived(kept(z, at_y(2), k), (yr_recv, (k,)), (yr_send, (k,)))
        inject(2)
        own_copy.wait()
        arrived(kept(z, y, 1), (ss_recv, (0, 0,)), (ss_send, (0, 0,)))
        send(pending, kept(z, y, 0), kept(z, y, 0), (ss_send, (0, 0,)), (ss_recv, (0, 0,)), mate)
        for s, d in (
            (3, 0), (2, 3), (2, 1), (1, 2), (4, 0), (3, 3), (3, 1), (2, 2), (4, 3), (4, 1),
        ):
            hop(s, d)
        for rel in (5, 3, 4):
            for k in range(2):
                arrived(kept(at_z(rel), at_y(2), k), (yf_recv, (rel, k,)), (yf_send, (rel, k,)))
            share(at_z(rel), at_y(2), rel, 2)
        for d in range(NY):
            arrived(column(at_y(d)), (fs_recv, (d,)), (fs_send, (d,)))

    @pl.when(c == 1)
    def _():
        pending = sent[1]
        mate = dev(z, y, 0, t)
        own_x = pltpu.make_async_copy(x_ref.at[y], xpiece(t, y, 1), local_sem.at[len(loads)])
        own_w = pltpu.make_async_copy(w_ref, wpiece(y, 1), local_sem.at[len(loads) + 1])
        own_copy = pltpu.make_async_copy(own_rows, kept(z, y, 1), local_sem.at[len(loads) + 2])
        own_x.start()
        own_w.start()
        own_copy.start()
        send(pending, own_rows, kept(z, y, 1), (ss_send, (0, 0,)), (ss_recv, (0, 0,)), mate)
        own_x.wait()
        arrived(xpiece(t, y, 0), (xy_recv, (0, 0,)), (xy_send, (0,)))
        for k, (dy, dl) in enumerate(line[1:]):
            for cc in range(2):
                arrived(xpiece(other(dl) * 4 + x, at_y(-dy), cc), (xy_recv, (k + 1, cc,)), (xy_send, (k + 1,)))
        xall = xbuf.reshape(2, 4, 2, SEL, 8 * HD)
        for k in range(1, NX):
            send(
                pending, xall.at[:, x], xall.at[:, x], (xx_send, (k,)), (xx_recv, (k,)), (r, ylo * 4 + at_x(k))
            )
        for k in range(2):
            yy = at_y(-sides[k][1])
            for cc in range(2):
                arrived(wpiece(yy, cc), (w_recv, (k, cc,)), (w_send, (k,)))
            send(
                pending, wpiece(yy, k), wpiece(yy, k), (wr_send, (k,)), (wr_recv, (k,)),
                dev(z, at_y(sides[k][1]), 1, t),
            )
        for cc in range(2):
            for k in range(SEL):
                position = sel_ref[k, r - 1 + cc]
                trig_c[cc, pl.ds(k, 1), :] = cos_ref[pl.ds(position, 1), :]
                trig_s[cc, pl.ds(k, 1), :] = sin_ref[pl.ds(position, 1), :]
        own_w.wait()
        arrived(wpiece(y, 0), (w_recv, (2, 0,)), (w_send, (2,)))
        for k in range(1, NX):
            arrived(xall.at[:, at_x(-k)], (xx_recv, (k,)), (xx_send, (k,)))
        for k in range(2):
            arrived(wpiece(at_y(2), k), (wr_recv, (k,)), (wr_send, (k,)))
        part = jnp.dot(
            xbuf[...].reshape(NZ * 2 * SEL, 8 * HD),
            wbuf[...].reshape(8 * HD, KV),
            preferred_element_type=jnp.float32,
        )
        zsum[...] = part.reshape(NZ, 2, SEL, KV)
        for k in (4, 3, 5, 2, 6, 1, 7):
            send(
                pending, zsum.at[at_z(k)], zrecv.at[k], (rz_send, (k,)), (rz_recv, (k,)), dev(at_z(k), y, 1, t)
            )
        total = zsum[z]
        for k in range(1, NZ):
            arrived(zrecv.at[k], (rz_recv, (k,)), (rz_send, (k,)))
            total = total + zrecv[k]
        fresh = total.astype(jnp.bfloat16).astype(jnp.float32)
        for cc in range(2):
            keys = fresh[cc, :, :HD]
            keys = keys * trig_c[cc] + pltpu.roll(keys, HD // 2, 1) * trig_s[cc]
            own_fresh[cc, :, :HD] = keys.astype(jnp.bfloat16)
            own_fresh[cc, :, HD:] = fresh[cc, :, HD:].astype(jnp.bfloat16)
        for k in (1, 7, 2, 6, 3, 5, 4):
            send(pending, own_fresh, piece(z, y), (fz_send, (k,)), (fz_recv, (k,)), dev(at_z(k), y, 1, t))
        keep_fresh = pltpu.make_async_copy(own_fresh, piece(z, y), local_sem.at[len(loads) + 3])
        keep_fresh.start()
        def share(d):
            send(pending, column(at_y(d)), column(at_y(d)), (fs_send, (d,)), (fs_recv, (d,)), mate)

        near_first = (0, 1, 7, 2, 6, 3, 5, 4)
        for rel in near_first:
            here = piece(at_z(-rel), y)
            if rel:
                arrived(here, (fz_recv, (rel,)), (fz_send, (rel,)))
            for k in range(2):
                send(
                    pending, here if rel else own_fresh, here, (fy_send, (rel, k,)), (fy_recv, (rel, k,)),
                    dev(z, at_y(sides[k][1]), 1, t),
                )
        keep_fresh.wait()
        share(0)
        for rel in near_first:
            zz = at_z(-rel)
            for k in range(2):
                yy = at_y(-sides[k][1])
                arrived(piece(zz, yy), (fy_recv, (rel, k,)), (fy_send, (rel, k,)))
                send(
                    pending, half_piece(zz, yy, k), half_piece(zz, yy, k), (fr_send, (rel, k,)), (fr_recv, (rel, k,)),
                    dev(z, at_y(sides[k][1]), 1, t),
                )
        share(3)
        share(1)
        for rel in near_first:
            for k in range(2):
                arrived(half_piece(at_z(-rel), at_y(2), k), (fr_recv, (rel, k,)), (fr_send, (rel, k,)))
        share(2)
        own_copy.wait()
        arrived(kept(z, y, 0), (ss_recv, (0, 0,)), (ss_send, (0, 0,)))
        for rel in range(NZ):
            for d in range(NY):
                if rel or d:
                    arrived(chunk(at_z(rel), at_y(d)), (ss_recv, (rel, d,)), (ss_send, (rel, d,)))

    kbufs, vbufs, sbufs, pbufs = (kbuf0, kbuf1), (vbuf0, vbuf1), (sbuf0, sbuf1), (pbuf0, pbuf1)
    steps = q_ref.shape[0] // PAIR

    def result_copy(step):
        rows = pl.ds(step * PAIR, PAIR)
        return pltpu.make_async_copy(out_ref.at[rows], out_hbm.at[rows], out_sem.at[step])

    col = lax.broadcasted_iota(jnp.int32, (CHUNK, 128), 1)
    token = lax.rem(lax.broadcasted_iota(jnp.int32, (CHUNK, 128), 0), QLEN)
    tail = jnp.where(col <= token, jnp.float32(0.0), jnp.float32(NEG))
    for i in range(PAIR):
        kbufs[i][LAST + QLEN :, :] = jnp.zeros((128 - QLEN, HD), jnp.bfloat16)
        vbufs[i][LAST + QLEN :, :] = jnp.zeros((128 - QLEN, HD), jnp.bfloat16)
    for copy in later:
        copy.wait()

    def turn(block, j):
        wide = block.astype(jnp.float32)
        wide = wide * cos_ref[PLEN + j : PLEN + j + 1, :] + pltpu.roll(wide, HD // 2, 1) * sin_ref[PLEN + j : PLEN + j + 1, :]
        return wide.astype(jnp.bfloat16)

    def pair(step, carry):
        for i in range(PAIR):
            kbuf, vbuf = kbufs[i], vbufs[i]
            request = step * PAIR + i
            for j in range(SLOTS):
                o = owner_ref[chosen_ref[j, request]]
                block = pas[o // 8, lax.rem(o, 8) // 2, lax.rem(o, 2)]
                keys = block[:, :HD]
                kbuf[j * PLEN : (j + 1) * PLEN, :] = turn(keys, j) if j else keys
                vbuf[j * PLEN : (j + 1) * PLEN, :] = block[:, HD:]
            own = own_ref[request]
            kbuf[LAST : LAST + QLEN, :] = own[:, :HD]
            vbuf[LAST : LAST + QLEN, :] = own[:, HD:]
        for i in range(PAIR):
            query = q_ref[step * PAIR + i]
            query = jnp.concatenate([query[:, h * HD : (h + 1) * HD] for h in range(GROUP)], 0)
            sbufs[i][...] = lax.dot_general(
                query, kbufs[i][...], (((1,), (1,)), ((), ())), preferred_element_type=jnp.float32
            )
        for i in range(PAIR):
            sbuf, pbuf = sbufs[i], pbufs[i]
            for first in range(0, GROUP * QLEN, CHUNK):
                rows = slice(first, first + CHUNK)
                raw = jnp.concatenate([sbuf[rows, :LAST], sbuf[rows, LAST:] + tail], 1)
                expo = jnp.exp2((raw - jnp.max(raw, 1, keepdims=True)) * SCALE)
                pbuf[rows, :] = (expo * (1.0 / jnp.sum(expo, 1, keepdims=True))).astype(jnp.bfloat16)
            result = jnp.dot(pbuf[...], vbufs[i][...], preferred_element_type=jnp.float32).astype(jnp.bfloat16)
            for h in range(GROUP):
                out_ref[step * PAIR + i, :, h * HD : (h + 1) * HD] = result[h * QLEN : (h + 1) * QLEN]
        result_copy(step).start()
        return carry

    lax.fori_loop(0, steps, pair, 0)
    for step in range(steps):
        result_copy(step).wait()
    drain(started)
    for core in range(2):

        @pl.when(c == core)
        def _(core=core):
            drain(sent[core])


def local(stale, fresh_input, kv_weight, sel_index, owner, retrieval, queries, question_kv):
    cosine, sine = trig_tables()
    any_spec = pl.BlockSpec(memory_space=pl.ANY)
    dma = pltpu.SemaphoreType.DMA
    rows = GROUP * QLEN
    return pl.pallas_call(
        kernel,
        out_shape=jax.ShapeDtypeStruct(queries.shape, jnp.bfloat16),
        in_specs=[any_spec] * 10,
        out_specs=any_spec,
        scratch_shapes=[
            pltpu.VMEM((NZ, NY, 2, PLEN, KV), jnp.bfloat16),
            pltpu.VMEM((KEYS, HD), jnp.bfloat16),
            pltpu.VMEM((KEYS, HD), jnp.bfloat16),
            pltpu.VMEM((KEYS, HD), jnp.bfloat16),
            pltpu.VMEM((KEYS, HD), jnp.bfloat16),
            pltpu.VMEM((rows, KEYS), jnp.float32),
            pltpu.VMEM((rows, KEYS), jnp.bfloat16),
            pltpu.VMEM((rows, KEYS), jnp.float32),
            pltpu.VMEM((rows, KEYS), jnp.bfloat16),
            pltpu.VMEM(queries.shape, jnp.bfloat16),
            pltpu.VMEM(question_kv.shape, jnp.bfloat16),
            pltpu.VMEM(queries.shape, jnp.bfloat16),
            pltpu.SMEM((64,), jnp.int32),
            pltpu.SMEM((SLOTS, 8), jnp.int32),
            pltpu.VMEM((PLEN, KV), jnp.bfloat16),
            pltpu.VMEM((KEPT, KV), jnp.bfloat16),
            pltpu.VMEM((2, SEL, KV), jnp.bfloat16),
            pltpu.VMEM((8, 2, SEL, 8 * HD), jnp.bfloat16),
            pltpu.VMEM((NY, 2, HD, KV), jnp.bfloat16),
            pltpu.VMEM((NZ, 2, SEL, KV), jnp.float32),
            pltpu.VMEM((NZ, 2, SEL, KV), jnp.float32),
            pltpu.VMEM((2, SEL, HD), jnp.float32),
            pltpu.VMEM((2, SEL, HD), jnp.float32),
            pltpu.VMEM((NY, 2, SEL, HD), jnp.bfloat16),
            pltpu.VMEM((HD, KV), jnp.bfloat16),
            pltpu.VMEM(cosine.shape, jnp.float32),
            pltpu.VMEM(sine.shape, jnp.float32),
            pltpu.SMEM((SEL, 64), jnp.int32),
            dma((12,)),
            dma((8,)), dma((8, 2)),
            dma((NX,)), dma((NX,)),
            dma((3,)), dma((3, 2)),
            dma((2,)), dma((2,)),
            dma((4,)), dma((4, 2)),
            dma((2,)), dma((2,)),
            dma((NZ, 2)), dma((NZ, 2)),
            dma((2, 5, NY)), dma((2, 5, NY)),
            dma((NZ, NY)), dma((NZ, NY)),
            dma((NZ,)), dma((NZ,)),
            dma((NZ,)), dma((NZ,)),
            dma((NZ, 2)), dma((NZ, 2)),
            dma((NZ, 2)), dma((NZ, 2)),
            dma((NY,)), dma((NY,)),
            dma((2,)), dma((4,)),
        ],
        compiler_params=pltpu.CompilerParams(
            collective_id=0, has_side_effects=True, vmem_limit_bytes=62 * 1024 * 1024
        ),
    )(
        stale,
        fresh_input.reshape(NY, 2, SEL, HD),
        kv_weight,
        sel_index.T,
        jnp.asarray(cosine),
        jnp.asarray(sine),
        owner,
        retrieval.T,
        queries,
        question_kv,
    )


def solution(mesh):
    return jax.shard_map(
        local,
        mesh=mesh,
        in_specs=(
            P("req", None, "tp"),
            P("tp", None, "req"),
            P("req", None),
            P(),
            P(),
            P("req", None),
            P("req", None, "tp"),
            P("req", None, "tp"),
        ),
        out_specs=P("req", None, "tp"),
        check_vma=False,
    )
```
